256 devices in a mesh: blk: 8 (over y, x_lo), dom: 32 (over x_hi, z, core).
Axes of the slice: x: 4 (x_hi: 2, x_lo: 2; x = x_hi * 2 + x_lo), y: 4, z: 8, core: 2. Of those that a mesh axis runs over, the one named last changes fastest.
Arguments:
- refs: bfloat16 [128, 32768], P('blk'), may hold values from -6 to 6
- particles: bfloat16 [8192, 32768], P(('blk', 'dom')), may hold values from -24 to 24
- shift_ids: int32 [8192, 8], P(('blk', 'dom')), may hold values from 0 to 124
- wedge: int32 [8192, 32], P(('blk', 'dom')), may hold values 0 or 1
- defocus: float32 [8192, 32], P(('blk', 'dom')), may hold values from 1 to 6
- inv_sigma: float32 [8192], P(('blk', 'dom')), may hold values from 0.005 to 0.05
Outputs:
- accum: float32 [128, 32768], P('blk', 'dom')
The draws below stay inside these ranges and needn't reach their ends.
All inputs are finite; a program needn't handle non-finite values. No bound on the sum of `wedge` on one device may be relied on, other than what follows from the above.
Results may differ from the reference program's by a relative error of at most 0.0087.
Values may be sent and summed in bfloat16 or wider, within the bound.
No kernel may reach another device: no remote copies, remote signals or barrier semaphores. Data moves between devices by JAX's collectives and lax.ppermute only.
A program may use at most 128 MiB of HBM per device.

```python
import math
import jax
import jax.numpy as jnp
from jax import lax

F = 16384
NT = 32
BOX = 32
SHIFTS = 8
P_DEV = 32
ORIENTS = 128
PARTS_SIZE = 8192
N_BLK = 8
N_DOM = 32


def refs_table(base_key):
    table_key = jax.random.fold_in(base_key, 102)
    values = jax.random.normal(table_key, (ORIENTS, 2 * F), jnp.float32)
    return jnp.clip(values, -6.0, 6.0)


def defocus_table(base_key):
    table_key = jax.random.fold_in(base_key, 101)
    return jax.random.uniform(table_key, (PARTS_SIZE, NT), jnp.float32, 1.0, 6.0)


def draw_refs(base_key, part):
    return refs_table(base_key).astype(jnp.bfloat16)


def draw_defocus(base_key, part):
    return defocus_table(base_key)


def draw_particles(base_key, part):
    own_key = jax.random.fold_in(base_key, 7)
    background = jnp.clip(jax.random.normal(own_key, (PARTS_SIZE, 2 * F), jnp.float32), -6.0, 6.0)
    return background.astype(jnp.bfloat16)


def plant(entries, key, least, largest):
    dims = entries.shape
    spot = [jax.random.randint(jax.random.fold_in(key, axis), (), 0, dims[axis]) for axis in range(len(dims))]
    entries = entries.at[tuple(spot)].set(least)
    longest = dims.index(max(dims))
    spot[longest] = (spot[longest] + 1) % dims[longest]
    return entries.at[tuple(spot)].set(largest)


def steps_of(key, shape, cuts, low, high):
    gain, own = 1.0, jax.random.fold_in(key, 6)
    for dim, parts in cuts:
        steps = jnp.exp(jax.random.uniform(jax.random.fold_in(own, dim), (parts,), jnp.float32, low / len(cuts), high / len(cuts)))
        gain = gain * jnp.repeat(steps, shape[dim] // parts).reshape([-1 if axis == dim else 1 for axis in range(len(shape))])
    return gain


def setup_inputs(seed: int = 0) -> dict:
    arg_keys = jax.random.split(jax.random.key(seed), 7)
    refs = draw_refs(jax.random.fold_in(arg_keys[6], 71), 0)
    particles = draw_particles(jax.random.fold_in(arg_keys[6], 71), 0)
    shift_ids = plant(jax.random.randint(arg_keys[2], (PARTS_SIZE, SHIFTS), 0, 125), jax.random.fold_in(arg_keys[2], 1), 0, 124).astype(jnp.int32)
    wedge = plant((jax.random.randint(arg_keys[3], (PARTS_SIZE, NT), 0, 4) < 3).astype(jnp.int32), jax.random.fold_in(arg_keys[3], 1), 0, 1)
    defocus = draw_defocus(jax.random.fold_in(arg_keys[6], 71), 0)
    inv_sigma = jnp.clip(jnp.exp(math.log(0.05) - 2.3025851 * jax.random.uniform(arg_keys[5], (PARTS_SIZE,), jnp.float32) ** steps_of(arg_keys[5], (PARTS_SIZE,), ((0, 256),), -0.2, 0.2)), 0.005, 0.05)
    return {"refs": refs, "particles": particles, "shift_ids": shift_ids, "wedge": wedge, "defocus": defocus, "inv_sigma": inv_sigma}


def spread_tilts(table, slice_len):
    count_rows, tilt_count = table.shape
    widened = jnp.broadcast_to(table[:, :, None], (count_rows, tilt_count, slice_len))
    return widened.reshape(count_rows, tilt_count * slice_len)


def prepare(particles, shift_ids, wedge, defocus, inv_sigma):
    half = particles.shape[1] // 2
    tilt_count = wedge.shape[1]
    slice_len = half // tilt_count
    position = jnp.arange(half, dtype=jnp.int32)
    tilt_index = (position // slice_len).astype(jnp.float32)
    within = position % slice_len
    radial = (within // BOX).astype(jnp.float32)
    lateral = (within % BOX - BOX // 2).astype(jnp.float32)
    tilt_angle = (tilt_index - 0.5 * (tilt_count - 1)) * (2.0 / tilt_count)
    freq_x = radial * jnp.cos(tilt_angle)
    freq_y = lateral
    freq_z = radial * jnp.sin(tilt_angle)
    shell = (radial * radial + lateral * lateral) / (0.25 * BOX * BOX)
    defocus_map = spread_tilts(defocus, slice_len)
    wedge_weight = spread_tilts(wedge.astype(jnp.float32), slice_len)
    transfer = -jnp.sin(4.0 * defocus_map * shell + 0.1)
    precision_col = inv_sigma[:, None]
    weighting = wedge_weight * transfer * precision_col
    penalty = (0.5 * wedge_weight * transfer * transfer * precision_col).astype(jnp.bfloat16)
    shift_x = ((shift_ids // 25) - 2).astype(jnp.float32) * 0.5
    shift_y = ((shift_ids // 5) % 5 - 2).astype(jnp.float32) * 0.5
    shift_z = (shift_ids % 5 - 2).astype(jnp.float32) * 0.5
    phase_angle = (2.0 * math.pi / BOX) * (shift_x[:, :, None] * freq_x + shift_y[:, :, None] * freq_y + shift_z[:, :, None] * freq_z)
    cosine = jnp.cos(phase_angle)
    sine_part = jnp.sin(phase_angle)
    real_part = particles[:, None, :half].astype(jnp.float32)
    imag_part = particles[:, None, half:].astype(jnp.float32)
    weighted_real = weighting[:, None, :] * (real_part * cosine + imag_part * sine_part)
    weighted_imag = weighting[:, None, :] * (imag_part * cosine - real_part * sine_part)
    shifted = jnp.concatenate([weighted_real, weighted_imag], axis=2)
    return shifted.reshape(-1, 2 * half).astype(jnp.bfloat16), penalty


def power_of(ref_block):
    half = ref_block.shape[1] // 2
    real_part = ref_block[:, :half].astype(jnp.float32)
    imag_part = ref_block[:, half:].astype(jnp.float32)
    return (real_part * real_part + imag_part * imag_part).astype(jnp.bfloat16)


def block_scores(ref_block, ref_power, weighted_rows, penalty):
    contract = (((1,), (1,)), ((), ()))
    correlation = lax.dot_general(ref_block, weighted_rows, contract, preferred_element_type=jnp.float32)
    energy = lax.dot_general(ref_power, penalty, contract, preferred_element_type=jnp.float32)
    shift_count = weighted_rows.shape[0] // penalty.shape[0]
    block_rows = ref_block.shape[0]
    energy = jnp.broadcast_to(energy[:, :, None], (block_rows, penalty.shape[0], shift_count)).reshape(block_rows, -1)
    return correlation - energy


def posterior_of(scores, part_count):
    orient_count = scores.shape[0]
    grouped = scores.reshape(orient_count, part_count, -1)
    peak = jnp.max(grouped, axis=(0, 2))
    expo = jnp.exp(grouped - peak[None, :, None])
    total = jnp.sum(expo, axis=(0, 2))
    posterior = (expo / total[None, :, None]).astype(jnp.bfloat16)
    return posterior.reshape(orient_count, -1)


def reference(refs, particles, shift_ids, wedge, defocus, inv_sigma):
    groups = N_BLK * N_DOM
    ref_power = power_of(refs)
    group_inputs = (
        particles.reshape(groups, P_DEV, -1),
        shift_ids.reshape(groups, P_DEV, -1),
        wedge.reshape(groups, P_DEV, -1),
        defocus.reshape(groups, P_DEV, -1),
        inv_sigma.reshape(groups, P_DEV),
    )

    def group_step(accumulated, inputs_now):
        particle_rows, ids_now, wedge_now, defocus_now, sigma_now = inputs_now
        weighted_rows, penalty = prepare(particle_rows, ids_now, wedge_now, defocus_now, sigma_now)
        scores = block_scores(refs, ref_power, weighted_rows, penalty)
        posterior = posterior_of(scores, P_DEV)
        accumulated = accumulated + jnp.dot(posterior, weighted_rows, preferred_element_type=jnp.float32)
        return accumulated, jnp.zeros((), jnp.float32)

    initial = jnp.zeros((refs.shape[0], refs.shape[1]), jnp.float32)
    accum, unused = lax.scan(group_step, initial, group_inputs)
    return accum
```

```python
import math

import jax
import jax.numpy as jnp
import numpy as np
from jax import lax
from jax.experimental import pallas as pl
from jax.experimental.pallas import tpu as pltpu
from jax.sharding import PartitionSpec as P

BOX = 32
TILTS = 32
SHIFTS = 8
P_DEV = 32
Y, X, Z = 4, 4, 8
COLS = 1024
HALF = 512
G = 4
NB = 16 // G
ROWS = P_DEV * SHIFTS
AXES = ("blk", "dom")
F32, BF16 = jnp.float32, jnp.bfloat16
NT = (((1,), (1,)), ((), ()))
MIB = 1 << 20


def linear(y, x, z, core):
    y, x, z = y % Y, x % X, z % Z
    return (y * 2 + x % 2) * 32 + (x // 2) * 16 + z * 2 + core


def moves(dy=0, dx=0, dz=0):
    return [
        (linear(y, x, z, c), linear(y + dy, x + dx, z + dz, c))
        for y in range(Y) for x in range(X) for z in range(Z) for c in range(2)
    ]


def partners(k):
    return [
        (linear(y, x, z, c), linear(y, x, z ^ (k >> 1), c ^ (k & 1)))
        for y in range(Y) for x in range(X) for z in range(Z) for c in range(2)
    ]


def send(value, pairs):
    return lax.ppermute(value, AXES, pairs)


def geometry():
    position = np.arange(TILTS * HALF)
    tilt, within = position // HALF, position % HALF
    radial = (within // BOX).astype(np.float64)
    lateral = (within % BOX - BOX // 2).astype(np.float64)
    angle = (tilt - 0.5 * (TILTS - 1)) * (2.0 / TILTS)
    shell = (radial * radial + lateral * lateral) / (0.25 * BOX * BOX)
    zero = np.zeros_like(shell)
    table = np.stack([radial * np.cos(angle), lateral, radial * np.sin(angle), shell] + [zero] * 4)
    return table.reshape(8, 16, COLS).transpose(1, 0, 2).astype(np.float32)


def translations():
    ids = np.arange(128)
    out = np.zeros((128, 8), np.float32)
    for column, digit in enumerate((ids // 25, ids // 5 % 5, ids % 5)):
        out[:, column] = (digit - 2) * 0.5 / BOX
    out[125:] = 0
    return out


def fold(turns):
    turns = turns - jnp.floor(turns + 0.5)
    far = jnp.abs(turns) > 0.25
    near = jnp.where(far, jnp.where(turns > 0, 0.5, -0.5) - turns, turns)
    return near * (2.0 * math.pi), far


def series(square, terms):
    total = jnp.full_like(square, terms[-1])
    for term in terms[-2::-1]:
        total = total * square + term
    return total


SIN_TERMS = [(-1) ** n / math.factorial(2 * n + 1) for n in range(6)]
COS_TERMS = [(-1) ** n / math.factorial(2 * n) for n in range(7)]


def sine_turns(turns):
    angle, _ = fold(turns)
    return angle * series(angle * angle, SIN_TERMS)


def table_kernel(geo_ref, shift_ref, out_ref):
    geo = geo_ref[0]
    shift = shift_ref[...]
    turns = shift[:, 0:1] * geo[0:1] + shift[:, 1:2] * geo[1:2] + shift[:, 2:3] * geo[2:3]
    angle, far = fold(turns)
    square = angle * angle
    sine = angle * series(square, SIN_TERMS)
    cosine = series(square, COS_TERMS)
    cosine = jnp.where(far, -cosine, cosine)
    for tilt in range(2):
        for part, values in enumerate((cosine, sine)):
            values = values[:, tilt * HALF : (tilt + 1) * HALF]
            high = values.astype(BF16)
            low = (values - high.astype(F32)).astype(BF16)
            lanes = slice(tilt * COLS + part * HALF, tilt * COLS + (part + 1) * HALF)
            out_ref[0:128, lanes] = high
            out_ref[128:256, lanes] = low


def make_table(geo):
    return pl.pallas_call(
        table_kernel,
        grid=(NB,),
        in_specs=[
            pl.BlockSpec((1, 8, COLS), lambda b: (b, 0, 0)),
            pl.BlockSpec((128, 8), lambda b: (0, 0)),
        ],
        out_specs=pl.BlockSpec((256, 2 * COLS), lambda b: (0, b)),
        out_shape=jax.ShapeDtypeStruct((256, NB * 2 * COLS), BF16),
        cost_estimate=pl.CostEstimate(flops=NB * 128 * COLS * 40, bytes_accessed=4 * MIB, transcendentals=0),
        name="phase_table",
    )(geo, jnp.asarray(translations()))


def arrange_kernel(count, member_ref, *refs):
    for n in range(count):
        real, imag, out = refs[2 * n], refs[2 * n + 1], refs[2 * count + n]
        for tilt in range(2):
            lanes = slice(tilt * HALF, (tilt + 1) * HALF)
            out[:, tilt * COLS : tilt * COLS + HALF] = real[:, lanes]
            out[:, tilt * COLS + HALF : (tilt + 1) * COLS] = imag[:, lanes]


def arrange(member, source, count):
    rows = source.shape[0]

    def picked(n, part):
        return pl.BlockSpec((rows, COLS), lambda b, m: (0, part * 16 + b * G + (m[0] ^ n)))

    return pl.pallas_call(
        lambda *refs: arrange_kernel(count, *refs),
        grid_spec=pltpu.PrefetchScalarGridSpec(
            num_scalar_prefetch=1,
            grid=(NB,),
            in_specs=[picked(n, part) for n in range(count) for part in range(2)],
            out_specs=[pl.BlockSpec((rows, 2 * COLS), lambda b, m: (0, b))] * count,
        ),
        out_shape=[jax.ShapeDtypeStruct((rows, NB * 2 * COLS), BF16)] * count,
        cost_estimate=pl.CostEstimate(flops=0, bytes_accessed=count * rows * NB * COLS * 8, transcendentals=0),
        name="arrange",
    )(member, *([source] * (2 * count)))


def rows_kernel(x_ref, meta_ref, ids_ref, geo_ref, table_ref, rows_ref, pen_ref):
    meta = meta_ref[0]
    lane = lax.broadcasted_iota(jnp.int32, (ROWS, 256), 1) & 127
    pick = (ids_ref[...] == lane.astype(F32)).astype(BF16)
    sigma = meta[:, 4:5]
    for tilt in range(2):
        base = tilt * COLS
        shell = geo_ref[0, 3:4, tilt * HALF : (tilt + 1) * HALF]
        focus, kept = meta[:, tilt : tilt + 1], meta[:, 2 + tilt : 3 + tilt]
        transfer = -sine_turns((4.0 * focus * shell + 0.1) * (0.5 / math.pi))
        weighting = kept * transfer * sigma
        pen_ref[:, tilt * HALF : (tilt + 1) * HALF] = (0.5 * weighting * transfer).astype(BF16)
        real = (weighting * x_ref[:, base : base + HALF].astype(F32))[None]
        imag = (weighting * x_ref[:, base + HALF : base + COLS].astype(F32))[None]
        turned = jnp.dot(pick, table_ref[:, base : base + COLS], preferred_element_type=F32)
        turned = turned.reshape(SHIFTS, P_DEV, COLS)
        cosine, sine = turned[:, :, :HALF], turned[:, :, HALF:]
        out_real = (real * cosine + imag * sine).reshape(ROWS, HALF)
        out_imag = (imag * cosine - real * sine).reshape(ROWS, HALF)
        rows_ref[:, base : base + HALF] = out_real.astype(BF16)
        rows_ref[:, base + HALF : base + COLS] = out_imag.astype(BF16)


def make_rows(x, meta, ids, geo, table):
    return pl.pallas_call(
        rows_kernel,
        grid=(NB,),
        in_specs=[
            pl.BlockSpec((P_DEV, 2 * COLS), lambda b: (0, b)),
            pl.BlockSpec((1, P_DEV, 8), lambda b: (b, 0, 0)),
            pl.BlockSpec((ROWS, 1), lambda b: (0, 0)),
            pl.BlockSpec((1, 8, COLS), lambda b: (b, 0, 0)),
            pl.BlockSpec((256, 2 * COLS), lambda b: (0, b)),
        ],
        out_specs=[
            pl.BlockSpec((ROWS, 2 * COLS), lambda b: (0, b)),
            pl.BlockSpec((P_DEV, COLS), lambda b: (0, b)),
        ],
        out_shape=[
            jax.ShapeDtypeStruct((ROWS, NB * 2 * COLS), BF16),
            jax.ShapeDtypeStruct((P_DEV, NB * COLS), BF16),
        ],
        cost_estimate=pl.CostEstimate(
            flops=2 * ROWS * 256 * NB * 2 * COLS, bytes_accessed=9 * MIB, transcendentals=0
        ),
        compiler_params=pltpu.CompilerParams(vmem_limit_bytes=32 * MIB),
        name="shifted_rows",
    )(x, meta, ids, geo, table)


def scores_kernel(count, *refs):
    blocks = refs[2 * count : 2 * count + 8]
    outs = refs[2 * count + 8 :]
    stacked = jnp.concatenate([block[...] for block in blocks], axis=0)
    wide = stacked.astype(F32)
    squares = wide * wide
    power = jnp.concatenate(
        [
            squares[:, t * COLS : t * COLS + HALF] + squares[:, t * COLS + HALF : (t + 1) * COLS]
            for t in range(2)
        ],
        axis=1,
    ).astype(BF16)
    first = pl.program_id(0) == 0
    for n in range(count):
        rows, pen, out = refs[n], refs[count + n], outs[n]
        energy = lax.dot_general(pen[...], power, NT, preferred_element_type=F32)
        fresh = lax.dot_general(rows[...], stacked, NT, preferred_element_type=F32)
        fresh = (fresh.reshape(SHIFTS, P_DEV, 128) - energy[None]).reshape(ROWS, 128)

        @pl.when(first)
        def _(out=out, fresh=fresh):
            out[...] = fresh

        @pl.when(jnp.logical_not(first))
        def _(out=out, fresh=fresh):
            out[...] += fresh


def make_scores(rows, pens, blocks):
    count = len(rows)
    return pl.pallas_call(
        lambda *refs: scores_kernel(count, *refs),
        grid=(NB,),
        in_specs=[pl.BlockSpec((ROWS, 2 * COLS), lambda b: (0, b))] * count
        + [pl.BlockSpec((P_DEV, COLS), lambda b: (0, b))] * count
        + [pl.BlockSpec((16, 2 * COLS), lambda b: (0, b))] * 8,
        out_specs=[pl.BlockSpec((ROWS, 128), lambda b: (0, 0))] * count,
        out_shape=[jax.ShapeDtypeStruct((ROWS, 128), F32)] * count,
        cost_estimate=pl.CostEstimate(
            flops=2 * count * ROWS * 128 * NB * 2 * COLS, bytes_accessed=(4 * count + 2) * MIB, transcendentals=0
        ),
        compiler_params=pltpu.CompilerParams(vmem_limit_bytes=40 * MIB),
        name="partial_scores",
    )(*rows, *pens, *blocks)


def posterior_kernel(*refs):
    out = refs[-1]
    total = refs[0][...]
    for other in refs[1:-1]:
        total = total + other[...]
    total = total.reshape(SHIFTS, P_DEV, 128)
    peak = jnp.max(jnp.max(total, axis=0), axis=1, keepdims=True)
    expo = jnp.exp(total - peak[None])
    norm = jnp.sum(jnp.sum(expo, axis=0), axis=1, keepdims=True)
    share = (expo / norm[None]).reshape(ROWS, 128)
    out[...] = share.T.astype(BF16)


def make_posterior(parts):
    return pl.pallas_call(
        posterior_kernel,
        out_shape=jax.ShapeDtypeStruct((128, ROWS), BF16),
        name="posterior",
    )(*parts)


def accum_kernel(part, flag_ref, *refs):
    rows, posts, outs = refs[:G], refs[G : 2 * G], refs[2 * G :]
    total = jnp.dot(posts[0][...], rows[0][...], preferred_element_type=F32)
    for n in range(1, G):
        total = total + jnp.dot(posts[n][...], rows[n][...], preferred_element_type=F32)
    if part == 0:
        for n in range(Y):
            outs[n][...] = total[n * 32 : (n + 1) * 32].astype(BF16)
    else:
        for n in range(X):
            low = n & 1
            imag = flag_ref[n] == 1
            for k in range(Y):
                mine = total[k * 32 + low * 16 : k * 32 + low * 16 + 16]
                chosen = jnp.where(imag, mine[:, HALF:], mine[:, :HALF])
                outs[n][k * 16 : (k + 1) * 16] = chosen.astype(BF16)


def make_accum(part, flags, rows, posts):
    shape = (32, COLS) if part == 0 else (64, HALF)
    return pl.pallas_call(
        lambda *refs: accum_kernel(part, *refs),
        grid_spec=pltpu.PrefetchScalarGridSpec(
            num_scalar_prefetch=1,
            grid=(NB,),
            in_specs=[pl.BlockSpec((ROWS, COLS), lambda b, f: (0, 2 * b + part))] * G
            + [pl.BlockSpec((128, ROWS), lambda b, f: (0, 0))] * G,
            out_specs=[pl.BlockSpec(shape, lambda b, f: (0, b))] * 4,
        ),
        out_shape=[jax.ShapeDtypeStruct((shape[0], NB * shape[1]), BF16)] * 4,
        cost_estimate=pl.CostEstimate(
            flops=2 * G * ROWS * 128 * NB * COLS, bytes_accessed=(2 * G + 1) * MIB, transcendentals=0
        ),
        compiler_params=pltpu.CompilerParams(vmem_limit_bytes=40 * MIB),
        name="weighted_sums",
    )(flags, *rows, *posts)


def added(values):
    total = values[0].astype(F32)
    for value in values[1:]:
        total = total + value.astype(F32)
    return total


def per_device(refs, particles, shift_ids, wedge, defocus, inv_sigma):
    dom = lax.axis_index("dom")
    x_at = (dom // 16) * 2 + lax.axis_index("blk") % 2
    member = dom % G
    block = (dom % 16) // G
    member_arr = member.astype(jnp.int32).reshape(1)
    flags = (((x_at + jnp.arange(X)) % X) // 2).astype(jnp.int32)

    gathered = {}
    (own,) = arrange(member_arr, refs, 1)
    gathered[0, 0] = own
    gathered[1, 0] = send(own, moves(dy=-1))
    gathered[3, 0] = send(own, moves(dy=1))
    gathered[0, 1] = send(own, moves(dx=-1))
    gathered[2, 0] = send(own, moves(dy=2))
    gathered[1, 1] = send(gathered[1, 0], moves(dx=-1))
    gathered[3, 1] = send(gathered[3, 0], moves(dx=1))
    gathered[2, 1] = send(gathered[2, 0], moves(dx=1))
    blocks = [gathered[ky, kx] for ky in range(Y) for kx in range(2)]

    meta = jnp.concatenate(
        [shift_ids.astype(F32), wedge.astype(F32), defocus, inv_sigma[:, None]], axis=1
    )
    metas = [meta] + [send(meta, partners(n)) for n in range(1, G)]
    chunks = arrange(member_arr, particles, G)
    chunks = [chunks[0]] + [send(chunks[n], partners(n)) for n in range(1, G)]

    geo = lax.dynamic_slice(
        jnp.asarray(geometry()).reshape(NB, G, 8, COLS), (0, member, 0, 0), (NB, 1, 8, COLS)
    ).reshape(NB, 8, COLS)
    table = make_table(geo)

    rows, pens = [], []
    for chunk, info in zip(chunks, metas):
        ids = info[:, :SHIFTS].T.reshape(ROWS, 1)
        tilts = info[:, SHIFTS : SHIFTS + 2 * TILTS].reshape(P_DEV, 2, NB, G, 2)
        tilts = lax.dynamic_slice(tilts, (0, 0, 0, member, 0), (P_DEV, 2, NB, 1, 2))[:, :, :, 0]
        kept, focus = tilts[:, 0].transpose(1, 0, 2), tilts[:, 1].transpose(1, 0, 2)
        sigma = jnp.broadcast_to(info[None, :, -1:], (NB, P_DEV, 1))
        packed = jnp.concatenate([focus, kept, sigma, jnp.zeros((NB, P_DEV, 3), F32)], axis=2)
        made, pen = make_rows(chunk, packed, ids, geo, table)
        rows.append(made)
        pens.append(pen)

    remote = make_scores(rows[1:], pens[1:], blocks)
    arrived = [send(remote[n - 1], partners(n)) for n in range(1, G)]
    (local,) = make_scores(rows[:1], pens[:1], blocks)
    posterior = make_posterior([local] + arrived)
    posts = [posterior] + [send(posterior, partners(n)) for n in range(1, G)]

    first = make_accum(0, flags, rows, posts)
    first = [first[0]] + [send(first[n], moves(dy=n)) for n in range(1, Y)]
    second = make_accum(1, flags, rows, posts)
    second = [second[0]] + [send(second[n], moves(dx=n)) for n in range(1, X)]

    first = added(first).reshape(2, 16, NB, 2, HALF)
    pieces = []
    for n in range(X):
        piece = lax.dynamic_index_in_dim(first[n & 1], flags[n], axis=2, keepdims=False)
        piece = piece.reshape(16, NB * HALF)
        pieces.append(piece if n == 0 else send(piece.astype(BF16), moves(dx=n)))
    first = added(pieces)

    second = added(second)
    pieces = []
    for n in range(Y):
        piece = second[n * 16 : (n + 1) * 16]
        pieces.append(piece if n == 0 else send(piece.astype(BF16), moves(dy=n)))
    second = added(pieces)

    joined = jnp.concatenate([first.reshape(16, NB, HALF), second.reshape(16, NB, HALF)], axis=2)
    pieces = []
    for n in range(NB):
        piece = lax.dynamic_index_in_dim(joined, (block + n) % NB, axis=1, keepdims=False)
        pieces.append(piece if n == 0 else send(piece.astype(BF16), moves(dz=n * (G // 2))))
    return added(pieces)


def solution(mesh):
    return jax.shard_map(
        per_device,
        mesh=mesh,
        in_specs=(
            P("blk", None),
            P(("blk", "dom"), None),
            P(("blk", "dom"), None),
            P(("blk", "dom"), None),
            P(("blk", "dom"), None),
            P(("blk", "dom")),
        ),
        out_specs=P("blk", "dom"),
        check_vma=False,
    )
```

```python
import math

import jax
import jax.numpy as jnp
import numpy as np
from jax import lax
from jax.experimental import pallas as pl
from jax.experimental.pallas import tpu as pltpu
from jax.sharding import PartitionSpec as P

BOX = 32
TILTS = 32
SHIFTS = 8
P_DEV = 32
Y, X, Z = 4, 4, 8
COLS = 1024
HALF = 512
G = 4
NB = 16 // G
ROWS = P_DEV * SHIFTS
WIDTH = NB * 2 * COLS
EXTRA = 384
AXES = ("blk", "dom")
F32, BF16 = jnp.float32, jnp.bfloat16
NT = (((1,), (1,)), ((), ()))
MIB = 1 << 20


def linear(y, x, z, core):
    y, x, z = y % Y, x % X, z % Z
    return (y * 2 + x % 2) * 32 + (x // 2) * 16 + z * 2 + core


def moves(dy=0, dx=0, dz=0):
    return [
        (linear(y, x, z, c), linear(y + dy, x + dx, z + dz, c))
        for y in range(Y) for x in range(X) for z in range(Z) for c in range(2)
    ]


def partners(k):
    return [
        (linear(y, x, z, c), linear(y, x, z ^ (k >> 1), c ^ (k & 1)))
        for y in range(Y) for x in range(X) for z in range(Z) for c in range(2)
    ]


def send(value, pairs):
    return lax.ppermute(value, AXES, pairs)


def geometry():
    position = np.arange(TILTS * HALF)
    tilt, within = position // HALF, position % HALF
    radial = (within // BOX).astype(np.float64)
    lateral = (within % BOX - BOX // 2).astype(np.float64)
    angle = (tilt - 0.5 * (TILTS - 1)) * (2.0 / TILTS)
    shell = (radial * radial + lateral * lateral) / (0.25 * BOX * BOX)
    zero = np.zeros_like(shell)
    table = np.stack([radial * np.cos(angle), lateral, radial * np.sin(angle), shell] + [zero] * 4)
    return table.reshape(8, 16, COLS).transpose(1, 0, 2).astype(np.float32)


def translations():
    ids = np.arange(128)
    out = np.zeros((128, 8), np.float32)
    for column, digit in enumerate((ids // 25, ids // 5 % 5, ids % 5)):
        out[:, column] = (digit - 2) * 0.5 / BOX
    out[125:] = 0
    return out


def fold(turns):
    turns = turns - jnp.floor(turns + 0.5)
    far = jnp.abs(turns) > 0.25
    near = jnp.where(far, jnp.where(turns > 0, 0.5, -0.5) - turns, turns)
    return near * (2.0 * math.pi), far


def series(square, terms):
    total = jnp.full_like(square, terms[-1])
    for term in terms[-2::-1]:
        total = total * square + term
    return total


SIN_TERMS = [(-1) ** n / math.factorial(2 * n + 1) for n in range(6)]
COS_TERMS = [(-1) ** n / math.factorial(2 * n) for n in range(7)]


def sine_turns(turns):
    angle, _ = fold(turns)
    return angle * series(angle * angle, SIN_TERMS)


def table_kernel(member_ref, geo_ref, shift_ref, out_ref):
    geo = geo_ref[0]
    shift = shift_ref[...]
    turns = shift[:, 0:1] * geo[0:1] + shift[:, 1:2] * geo[1:2] + shift[:, 2:3] * geo[2:3]
    angle, far = fold(turns)
    square = angle * angle
    sine = angle * series(square, SIN_TERMS)
    cosine = series(square, COS_TERMS)
    cosine = jnp.where(far, -cosine, cosine)
    for tilt in range(2):
        for part, values in enumerate((cosine, sine)):
            values = values[:, tilt * HALF : (tilt + 1) * HALF]
            high = values.astype(BF16)
            low = (values - high.astype(F32)).astype(BF16)
            lanes = slice(tilt * COLS + part * HALF, tilt * COLS + (part + 1) * HALF)
            out_ref[0:128, lanes] = high
            out_ref[128:256, lanes] = low


def make_table(member, geo):
    return pl.pallas_call(
        table_kernel,
        grid_spec=pltpu.PrefetchScalarGridSpec(
            num_scalar_prefetch=1,
            grid=(NB,),
            in_specs=[
                pl.BlockSpec((1, 8, COLS), lambda b, m: (b * G + m[0], 0, 0)),
                pl.BlockSpec((128, 8), lambda b, m: (0, 0)),
            ],
            out_specs=pl.BlockSpec((256, 2 * COLS), lambda b, m: (0, b)),
        ),
        out_shape=jax.ShapeDtypeStruct((256, WIDTH), BF16),
        cost_estimate=pl.CostEstimate(flops=NB * 128 * COLS * 40, bytes_accessed=4 * MIB, transcendentals=0),
        compiler_params=pltpu.CompilerParams(vmem_limit_bytes=12 * MIB),
        name="phase_table",
    )(member, geo, jnp.asarray(translations()))


def column(part, block, who):
    return pl.ds(pl.multiple_of((part * 16 + block * G + who) * COLS, COLS), COLS)


def own_kernel(member_ref, source, out):
    for block in range(NB):
        for part in range(2):
            spot = (block * 2 + part) * COLS
            out[:, spot : spot + COLS] = source[:, column(part, block, member_ref[0])]


def own_columns(member, refs):
    return pl.pallas_call(
        own_kernel,
        in_specs=[pl.BlockSpec(memory_space=pltpu.SMEM), pl.BlockSpec(memory_space=pltpu.VMEM)],
        out_specs=pl.BlockSpec(memory_space=pltpu.VMEM),
        out_shape=jax.ShapeDtypeStruct((16, WIDTH), BF16),
        cost_estimate=pl.CostEstimate(flops=0, bytes_accessed=2 * MIB, transcendentals=0),
        compiler_params=pltpu.CompilerParams(vmem_limit_bytes=8 * MIB),
        name="own_references",
    )(member, refs)


def split_kernel(member_ref, after, source, ids, wedge, focus, sigma, *outs):
    info = jnp.concatenate(
        [
            ids[...].astype(F32),
            wedge[...].astype(F32),
            focus[...],
            sigma[...],
            jnp.zeros((P_DEV, 128 - SHIFTS - 2 * TILTS - 1), F32),
        ],
        axis=1,
    )
    high = info.astype(BF16)
    rest = info - high.astype(F32)
    middle = rest.astype(BF16)
    low = (rest - middle.astype(F32)).astype(BF16)
    for n, out in enumerate(outs):
        who = member_ref[0] ^ n
        for block in range(NB):
            for part in range(2):
                spot = (block * 2 + part) * COLS
                out[:, spot : spot + COLS] = source[:, column(part, block, who)]
        for spot, piece in enumerate((high, middle, low)):
            out[:, WIDTH + spot * 128 : WIDTH + (spot + 1) * 128] = piece


def split_particles(member, after, particles, shift_ids, wedge, defocus, inv_sigma):
    return pl.pallas_call(
        split_kernel,
        in_specs=[pl.BlockSpec(memory_space=pltpu.SMEM), pl.BlockSpec(memory_space=pl.ANY)]
        + [pl.BlockSpec(memory_space=pltpu.VMEM)] * 5,
        out_specs=[pl.BlockSpec(memory_space=pltpu.VMEM)] * G,
        out_shape=[jax.ShapeDtypeStruct((P_DEV, WIDTH + EXTRA), BF16)] * G,
        cost_estimate=pl.CostEstimate(flops=0, bytes_accessed=5 * MIB, transcendentals=0),
        compiler_params=pltpu.CompilerParams(vmem_limit_bytes=8 * MIB),
        name="split_particles",
    )(member, after, particles, shift_ids, wedge, defocus, inv_sigma[:, None])


def rows_kernel(member_ref, x_ref, high_ref, middle_ref, low_ref, geo_ref, table_ref, rows_ref, pen_ref):
    info = high_ref[...].astype(F32) + middle_ref[...].astype(F32) + low_ref[...].astype(F32)
    lane = lax.broadcasted_iota(jnp.int32, (ROWS, 256), 1) & 127
    ids = jnp.concatenate([info[:, s : s + 1] for s in range(SHIFTS)], axis=0)
    pick = (ids == lane.astype(F32)).astype(BF16)
    at = SHIFTS + 2 * TILTS
    sigma = info[:, at : at + 1]
    small = lax.broadcasted_iota(jnp.int32, (P_DEV, 128), 1)
    first = 2 * (pl.program_id(0) * G + member_ref[0]) + SHIFTS
    weighting = []
    for tilt in range(2):
        kept = jnp.sum(jnp.where(small == first + tilt, info, 0.0), axis=1, keepdims=True)
        focus = jnp.sum(jnp.where(small == first + tilt + TILTS, info, 0.0), axis=1, keepdims=True)
        lanes = slice(tilt * HALF, (tilt + 1) * HALF)
        shell = geo_ref[0, 3:4, lanes]
        transfer = -sine_turns((4.0 * focus * shell + 0.1) * (0.5 / math.pi))
        weight = kept * transfer * sigma
        pen_ref[:, lanes] = (0.5 * weight * transfer).astype(BF16)
        weighting.append(weight)
    for tilt in range(2):
        lanes = slice(tilt * HALF, (tilt + 1) * HALF)
        upper = slice(COLS + tilt * HALF, COLS + (tilt + 1) * HALF)
        real = (weighting[tilt] * x_ref[:, lanes].astype(F32))[None]
        imag = (weighting[tilt] * x_ref[:, upper].astype(F32))[None]
        turned = jnp.dot(
            pick, table_ref[:, tilt * COLS : (tilt + 1) * COLS], preferred_element_type=F32
        ).reshape(SHIFTS, P_DEV, COLS)
        cosine, sine = turned[:, :, :HALF], turned[:, :, HALF:]
        rows_ref[:, lanes] = (real * cosine + imag * sine).reshape(ROWS, HALF).astype(BF16)
        rows_ref[:, upper] = (imag * cosine - real * sine).reshape(ROWS, HALF).astype(BF16)


def make_rows(member, x, geo, table):
    extra = WIDTH // 128
    return pl.pallas_call(
        rows_kernel,
        grid_spec=pltpu.PrefetchScalarGridSpec(
            num_scalar_prefetch=1,
            grid=(NB,),
            in_specs=[
                pl.BlockSpec((P_DEV, 2 * COLS), lambda b, m: (0, b)),
                pl.BlockSpec((P_DEV, 128), lambda b, m: (0, extra)),
                pl.BlockSpec((P_DEV, 128), lambda b, m: (0, extra + 1)),
                pl.BlockSpec((P_DEV, 128), lambda b, m: (0, extra + 2)),
                pl.BlockSpec((1, 8, COLS), lambda b, m: (b * G + m[0], 0, 0)),
                pl.BlockSpec((256, 2 * COLS), lambda b, m: (0, b)),
            ],
            out_specs=[
                pl.BlockSpec((ROWS, 2 * COLS), lambda b, m: (0, b)),
                pl.BlockSpec((P_DEV, COLS), lambda b, m: (0, b)),
            ],
        ),
        out_shape=[
            jax.ShapeDtypeStruct((ROWS, WIDTH), BF16),
            jax.ShapeDtypeStruct((P_DEV, NB * COLS), BF16),
        ],
        cost_estimate=pl.CostEstimate(
            flops=2 * ROWS * 256 * WIDTH, bytes_accessed=9 * MIB, transcendentals=0
        ),
        compiler_params=pltpu.CompilerParams(vmem_limit_bytes=16 * MIB),
        name="shifted_rows",
    )(member, x, x, x, x, geo, table)


def scores_kernel(count, *refs):
    blocks = refs[2 * count : 2 * count + 8]
    outs = refs[2 * count + 8 :]
    stacked = jnp.concatenate([block[...] for block in blocks], axis=0)
    real, imag = stacked[:, :COLS].astype(F32), stacked[:, COLS:].astype(F32)
    power = (real * real + imag * imag).astype(BF16)
    first = pl.program_id(0) == 0
    for n in range(count):
        rows, pen, out = refs[n], refs[count + n], outs[n]
        energy = lax.dot_general(pen[...], power, NT, preferred_element_type=F32)
        fresh = lax.dot_general(rows[...], stacked, NT, preferred_element_type=F32)
        fresh = (fresh.reshape(SHIFTS, P_DEV, 128) - energy[None]).reshape(ROWS, 128)

        @pl.when(first)
        def _(out=out, fresh=fresh):
            out[...] = fresh

        @pl.when(jnp.logical_not(first))
        def _(out=out, fresh=fresh):
            out[...] += fresh


def make_scores(rows, pens, blocks):
    count = len(rows)
    return pl.pallas_call(
        lambda *refs: scores_kernel(count, *refs),
        grid=(NB,),
        in_specs=[pl.BlockSpec((ROWS, 2 * COLS), lambda b: (0, b))] * count
        + [pl.BlockSpec((P_DEV, COLS), lambda b: (0, b))] * count
        + [pl.BlockSpec((16, 2 * COLS), lambda b: (0, b))] * 8,
        out_specs=[pl.BlockSpec((ROWS, 128), lambda b: (0, 0))] * count,
        out_shape=[jax.ShapeDtypeStruct((ROWS, 128), F32)] * count,
        cost_estimate=pl.CostEstimate(
            flops=2 * count * ROWS * 128 * WIDTH, bytes_accessed=(4 * count + 2) * MIB, transcendentals=0
        ),
        compiler_params=pltpu.CompilerParams(vmem_limit_bytes=20 * MIB),
        name="partial_scores",
    )(*rows, *pens, *blocks)


def posterior_kernel(*refs):
    out = refs[-1]
    total = refs[0][...]
    for other in refs[1:-1]:
        total = total + other[...]
    total = total.reshape(SHIFTS, P_DEV, 128)
    peak = jnp.max(jnp.max(total, axis=0), axis=1, keepdims=True)
    expo = jnp.exp(total - peak[None])
    norm = jnp.sum(jnp.sum(expo, axis=0), axis=1, keepdims=True)
    share = (expo / norm[None]).reshape(ROWS, 128)
    out[...] = share.T.astype(BF16)


def make_posterior(parts):
    return pl.pallas_call(
        posterior_kernel,
        out_shape=jax.ShapeDtypeStruct((128, ROWS), BF16),
        name="posterior",
    )(*parts)


def accum_kernel(part, flag_ref, *refs):
    real, imag, posts, outs = refs[:G], refs[G : 2 * G], refs[2 * G : 3 * G], refs[3 * G :]
    sums = []
    for rows in (real, imag):
        total = jnp.dot(posts[0][...], rows[0][...], preferred_element_type=F32)
        for n in range(1, G):
            total = total + jnp.dot(posts[n][...], rows[n][...], preferred_element_type=F32)
        sums.append(total)
    if part == 0:
        for n in range(Y):
            for half, total in enumerate(sums):
                outs[n][:, half * HALF : (half + 1) * HALF] = total[n * 32 : (n + 1) * 32].astype(BF16)
    else:
        for n in range(X):
            low = n & 1
            upper = flag_ref[n] == 1
            for k in range(Y):
                mine = slice(k * 32 + low * 16, k * 32 + low * 16 + 16)
                chosen = jnp.where(upper, sums[1][mine], sums[0][mine])
                outs[n][k * 16 : (k + 1) * 16] = chosen.astype(BF16)


def make_accum(part, flags, rows, posts):
    shape = (32, COLS) if part == 0 else (64, HALF)
    return pl.pallas_call(
        lambda *refs: accum_kernel(part, *refs),
        grid_spec=pltpu.PrefetchScalarGridSpec(
            num_scalar_prefetch=1,
            grid=(NB,),
            in_specs=[pl.BlockSpec((ROWS, HALF), lambda b, f: (0, 4 * b + part))] * G
            + [pl.BlockSpec((ROWS, HALF), lambda b, f: (0, 4 * b + 2 + part))] * G
            + [pl.BlockSpec((128, ROWS), lambda b, f: (0, 0))] * G,
            out_specs=[pl.BlockSpec(shape, lambda b, f: (0, b))] * 4,
        ),
        out_shape=[jax.ShapeDtypeStruct((shape[0], NB * shape[1]), BF16)] * 4,
        cost_estimate=pl.CostEstimate(
            flops=2 * G * ROWS * 128 * NB * COLS, bytes_accessed=(2 * G + 1) * MIB, transcendentals=0
        ),
        compiler_params=pltpu.CompilerParams(vmem_limit_bytes=16 * MIB),
        name="weighted_sums",
    )(flags, *rows, *rows, *posts)


def added(values):
    total = values[0].astype(F32)
    for value in values[1:]:
        total = total + value.astype(F32)
    return total


def per_device(refs, particles, shift_ids, wedge, defocus, inv_sigma):
    dom = lax.axis_index("dom")
    x_at = (dom // 16) * 2 + lax.axis_index("blk") % 2
    member = dom % G
    block = (dom % 16) // G
    member_arr = member.astype(jnp.int32).reshape(1)
    flags = (((x_at + jnp.arange(X)) % X) // 2).astype(jnp.int32)

    gathered = {}
    own = own_columns(member_arr, refs)
    gathered[0, 0] = own
    gathered[1, 0] = send(own, moves(dy=-1))
    gathered[3, 0] = send(own, moves(dy=1))
    gathered[0, 1] = send(own, moves(dx=-1))

    chunks = split_particles(member_arr, own, particles, shift_ids, wedge, defocus, inv_sigma)
    chunks = [chunks[0]] + [send(chunks[n], partners(n)) for n in range(1, G)]

    gathered[2, 0] = send(own, moves(dy=2))
    gathered[1, 1] = send(gathered[1, 0], moves(dx=-1))
    gathered[3, 1] = send(gathered[3, 0], moves(dx=1))
    gathered[2, 1] = send(gathered[2, 0], moves(dx=1))
    blocks = [gathered[ky, kx] for ky in range(Y) for kx in range(2)]

    geo = jnp.asarray(geometry())
    table = make_table(member_arr, geo)
    rows, pens = zip(*[make_rows(member_arr, chunk, geo, table) for chunk in chunks])

    early = make_scores(rows[: G - 1], pens[: G - 1], blocks)
    late = make_scores(rows[G - 1 :], pens[G - 1 :], blocks)
    parts = list(early) + list(late)
    arrived = [send(parts[n], partners(n)) for n in range(1, G)]
    posterior = make_posterior([parts[0]] + arrived)
    posts = [posterior] + [send(posterior, partners(n)) for n in range(1, G)]

    first = make_accum(0, flags, rows, posts)
    first = [first[0]] + [send(first[n], moves(dy=n)) for n in range(1, Y)]
    second = make_accum(1, flags, rows, posts)
    second = [second[0]] + [send(second[n], moves(dx=n)) for n in range(1, X)]

    first = added(first).reshape(2, 16, NB, 2, HALF)
    pieces = []
    for n in range(X):
        piece = lax.dynamic_index_in_dim(first[n & 1], flags[n], axis=2, keepdims=False)
        piece = piece.reshape(16, NB * HALF)
        pieces.append(piece if n == 0 else send(piece.astype(BF16), moves(dx=n)))
    first = added(pieces)

    second = added(second)
    pieces = []
    for n in range(Y):
        piece = second[n * 16 : (n + 1) * 16]
        pieces.append(piece if n == 0 else send(piece.astype(BF16), moves(dy=n)))
    second = added(pieces)

    joined = jnp.concatenate([first.reshape(16, NB, HALF), second.reshape(16, NB, HALF)], axis=2)
    pieces = []
    for n in range(NB):
        piece = lax.dynamic_index_in_dim(joined, (block + n) % NB, axis=1, keepdims=False)
        pieces.append(piece if n == 0 else send(piece.astype(BF16), moves(dz=n * (G // 2))))
    return added(pieces)


def solution(mesh):
    return jax.shard_map(
        per_device,
        mesh=mesh,
        in_specs=(
            P("blk", None),
            P(("blk", "dom"), None),
            P(("blk", "dom"), None),
            P(("blk", "dom"), None),
            P(("blk", "dom"), None),
            P(("blk", "dom")),
        ),
        out_specs=P("blk", "dom"),
        check_vma=False,
    )
```

```python
import math

import jax
import jax.numpy as jnp
import numpy as np
from jax import lax
from jax.experimental import pallas as pl
from jax.experimental.pallas import tpu as pltpu
from jax.sharding import PartitionSpec as P

BOX = 32
TILTS = 32
SHIFTS = 8
P_DEV = 32
Y, X, Z = 4, 4, 8
COLS = 1024
HALF = 512
G = 4
NB = 16 // G
ROWS = P_DEV * SHIFTS
WIDTH = NB * 2 * COLS
EXTRA = 384
AXES = ("blk", "dom")
F32, BF16 = jnp.float32, jnp.bfloat16
NT = (((1,), (1,)), ((), ()))
MIB = 1 << 20


def linear(y, x, z, core):
    y, x, z = y % Y, x % X, z % Z
    return (y * 2 + x % 2) * 32 + (x // 2) * 16 + z * 2 + core


def moves(dy=0, dx=0, dz=0):
    return [
        (linear(y, x, z, c), linear(y + dy, x + dx, z + dz, c))
        for y in range(Y) for x in range(X) for z in range(Z) for c in range(2)
    ]


def partners(k):
    return [
        (linear(y, x, z, c), linear(y, x, z ^ (k >> 1), c ^ (k & 1)))
        for y in range(Y) for x in range(X) for z in range(Z) for c in range(2)
    ]


def send(value, pairs):
    return lax.ppermute(value, AXES, pairs)


def geometry():
    position = np.arange(TILTS * HALF)
    tilt, within = position // HALF, position % HALF
    radial = (within // BOX).astype(np.float64)
    lateral = (within % BOX - BOX // 2).astype(np.float64)
    angle = (tilt - 0.5 * (TILTS - 1)) * (2.0 / TILTS)
    shell = (radial * radial + lateral * lateral) / (0.25 * BOX * BOX)
    zero = np.zeros_like(shell)
    table = np.stack([radial * np.cos(angle), lateral, radial * np.sin(angle), shell] + [zero] * 4)
    return table.reshape(8, 16, COLS).transpose(1, 0, 2).astype(np.float32)


def translations():
    ids = np.arange(128)
    out = np.zeros((128, 8), np.float32)
    for column, digit in enumerate((ids // 25, ids // 5 % 5, ids % 5)):
        out[:, column] = (digit - 2) * 0.5 / BOX
    out[125:] = 0
    return out


def fold(turns):
    turns = turns - jnp.floor(turns + 0.5)
    far = jnp.abs(turns) > 0.25
    near = jnp.where(far, jnp.where(turns > 0, 0.5, -0.5) - turns, turns)
    return near * (2.0 * math.pi), far


def series(square, terms):
    total = jnp.full_like(square, terms[-1])
    for term in terms[-2::-1]:
        total = total * square + term
    return total


SIN_TERMS = [(-1) ** n / math.factorial(2 * n + 1) for n in range(6)]
COS_TERMS = [(-1) ** n / math.factorial(2 * n) for n in range(7)]


def sine_turns(turns):
    angle, _ = fold(turns)
    return angle * series(angle * angle, SIN_TERMS)


def held(value):
    return pltpu.with_memory_space_constraint(value, pltpu.VMEM)


SCALARS = pl.BlockSpec(memory_space=pltpu.SMEM)
WHOLE = pl.BlockSpec(memory_space=pltpu.VMEM)
PLACED = pl.BlockSpec(memory_space=pl.ANY)


def local(kernel, name, outs, scalars, arrays, limit, flops=0, size=0, placed=0, scratch=()):
    return pl.pallas_call(
        kernel,
        in_specs=[SCALARS] * len(scalars) + [PLACED] * placed + [WHOLE] * (len(arrays) - placed),
        out_specs=[WHOLE] * len(outs),
        out_shape=[pltpu.VMEM(shape, kind) for shape, kind in outs],
        scratch_shapes=list(scratch),
        cost_estimate=pl.CostEstimate(flops=flops, bytes_accessed=size, transcendentals=0),
        compiler_params=pltpu.CompilerParams(vmem_limit_bytes=limit * MIB),
        name=name,
    )(*scalars, *arrays[:placed], *[held(value) for value in arrays[placed:]])


def table_kernel(member_ref, geo_ref, shift_ref, out_ref):
    shift = shift_ref[...]

    @pl.loop(0, NB)
    def _(block):
        geo = geo_ref[block * G + member_ref[0]]
        for tilt in range(2):
            part = geo[:, tilt * HALF : (tilt + 1) * HALF]
            turns = shift[:, 0:1] * part[0:1] + shift[:, 1:2] * part[1:2] + shift[:, 2:3] * part[2:3]
            angle, far = fold(turns)
            square = angle * angle
            sine = angle * series(square, SIN_TERMS)
            cosine = series(square, COS_TERMS)
            cosine = jnp.where(far, -cosine, cosine)
            for at, values in enumerate((cosine, sine)):
                high = values.astype(BF16)
                low = (values - high.astype(F32)).astype(BF16)
                spot = pl.multiple_of(block * 2 * COLS + tilt * COLS + at * HALF, HALF)
                out_ref[0:128, pl.ds(spot, HALF)] = high
                out_ref[128:256, pl.ds(spot, HALF)] = low


def make_table(member, geo):
    (table,) = local(
        table_kernel, "phase_table", [((256, WIDTH), BF16)], [member],
        [geo, jnp.asarray(translations())], 8, flops=NB * 128 * COLS * 40, size=5 * MIB,
    )
    return table


def column(part, block, who):
    return pl.ds(pl.multiple_of((part * 16 + block * G + who) * COLS, COLS), COLS)


def pieces_of(source, out, who, sems, base):
    return [
        pltpu.make_async_copy(
            source.at[:, column(part, block, who)],
            out.at[:, pl.ds((block * 2 + part) * COLS, COLS)],
            sems.at[base + block * 2 + part],
        )
        for block in range(NB) for part in range(2)
    ]


def own_kernel(member_ref, source, out, sems):
    copies = pieces_of(source, out, member_ref[0], sems, 0)
    for copy in copies:
        copy.start()
    for copy in copies:
        copy.wait()


def own_columns(member, refs):
    (own,) = local(
        own_kernel, "own_references", [((16, WIDTH), BF16)], [member], [refs], 4, size=MIB // 2,
        placed=1, scratch=[pltpu.SemaphoreType.DMA((2 * NB,))],
    )
    return own


def split_kernel(member_ref, source, after, ids, wedge, focus, sigma, *refs):
    outs, sems = refs[:-1], refs[-1]
    copies = []
    for n in (2, 1, 3, 0):
        copies += pieces_of(source, outs[n], member_ref[0] ^ n, sems, n * 2 * NB)
    for copy in copies:
        copy.start()
    info = jnp.concatenate(
        [
            ids[...].astype(F32),
            wedge[...].astype(F32),
            focus[...],
            sigma[...],
            jnp.zeros((P_DEV, 128 - SHIFTS - 2 * TILTS - 1), F32),
        ],
        axis=1,
    )
    high = info.astype(BF16)
    rest = info - high.astype(F32)
    middle = rest.astype(BF16)
    low = (rest - middle.astype(F32)).astype(BF16)
    for out in outs:
        for spot, piece in enumerate((high, middle, low)):
            out[:, WIDTH + spot * 128 : WIDTH + (spot + 1) * 128] = piece
    for copy in copies:
        copy.wait()


def split_particles(member, after, particles, shift_ids, wedge, defocus, inv_sigma):
    return local(
        split_kernel, "split_particles", [((P_DEV, WIDTH + EXTRA), BF16)] * G, [member],
        [particles, after, shift_ids, wedge, defocus, inv_sigma[:, None]], 4, size=4 * MIB,
        placed=2, scratch=[pltpu.SemaphoreType.DMA((G * 2 * NB,))],
    )


def rows_kernel(member_ref, x_ref, geo_ref, table_ref, rows_ref, pen_ref):
    info = sum(x_ref[:, WIDTH + n * 128 : WIDTH + (n + 1) * 128].astype(F32) for n in range(3))
    lane = lax.broadcasted_iota(jnp.int32, (ROWS, 256), 1) & 127
    ids = jnp.concatenate([info[:, s : s + 1] for s in range(SHIFTS)], axis=0)
    pick = (ids == lane.astype(F32)).astype(BF16)
    at = SHIFTS + 2 * TILTS
    sigma = info[:, at : at + 1]
    small = lax.broadcasted_iota(jnp.int32, (P_DEV, 128), 1)

    @pl.loop(0, NB)
    def _(block):
        first = 2 * (block * G + member_ref[0]) + SHIFTS
        start = pl.multiple_of(block * 2 * COLS, 2 * COLS)
        for tilt in range(2):
            kept = jnp.sum(jnp.where(small == first + tilt, info, 0.0), axis=1, keepdims=True)
            focus = jnp.sum(jnp.where(small == first + tilt + TILTS, info, 0.0), axis=1, keepdims=True)
            shell = geo_ref[block * G + member_ref[0], 3:4, tilt * HALF : (tilt + 1) * HALF]
            transfer = -sine_turns((4.0 * focus * shell + 0.1) * (0.5 / math.pi))
            weight = kept * transfer * sigma
            spot = pl.multiple_of(block * COLS + tilt * HALF, HALF)
            pen_ref[:, pl.ds(spot, HALF)] = (0.5 * weight * transfer).astype(BF16)
            lower, upper = pl.ds(start + tilt * HALF, HALF), pl.ds(start + COLS + tilt * HALF, HALF)
            real = (weight * x_ref[:, lower].astype(F32))[None]
            imag = (weight * x_ref[:, upper].astype(F32))[None]
            turned = jnp.dot(
                pick, table_ref[:, pl.ds(start + tilt * COLS, COLS)], preferred_element_type=F32
            ).reshape(SHIFTS, P_DEV, COLS)
            cosine, sine = turned[:, :, :HALF], turned[:, :, HALF:]
            rows_ref[:, lower] = (real * cosine + imag * sine).reshape(ROWS, HALF).astype(BF16)
            rows_ref[:, upper] = (imag * cosine - real * sine).reshape(ROWS, HALF).astype(BF16)


def make_rows(member, x, geo, table):
    return local(
        rows_kernel, "shifted_rows", [((ROWS, WIDTH), BF16), ((P_DEV, NB * COLS), BF16)], [member],
        [x, geo, table], 12, flops=2 * ROWS * 256 * WIDTH, size=9 * MIB,
    )


def scores_kernel(count, *refs):
    blocks = refs[2 * count : 2 * count + 8]
    outs = refs[2 * count + 8 :]
    stacked = jnp.concatenate([block[...] for block in blocks], axis=0)
    power = []
    for block in range(NB):
        start = block * 2 * COLS
        real = stacked[:, start : start + COLS].astype(F32)
        imag = stacked[:, start + COLS : start + 2 * COLS].astype(F32)
        power.append((real * real + imag * imag).astype(BF16))
    power = jnp.concatenate(power, axis=1)
    pens = jnp.concatenate([pen[...] for pen in refs[count : 2 * count]], axis=0)
    rows = jnp.concatenate([row[...] for row in refs[:count]], axis=0)
    energy = lax.dot_general(pens, power, NT, preferred_element_type=F32)
    total = lax.dot_general(rows, stacked, NT, preferred_element_type=F32)
    for n, out in enumerate(outs):
        mine = total[n * ROWS : (n + 1) * ROWS].reshape(SHIFTS, P_DEV, 128)
        out[...] = (mine - energy[None, n * P_DEV : (n + 1) * P_DEV]).reshape(ROWS, 128)


def make_scores(rows, pens, blocks):
    count = len(rows)
    return local(
        lambda *refs: scores_kernel(count, *refs), "partial_scores", [((ROWS, 128), F32)] * count, [],
        [*rows, *pens, *blocks], 12, flops=2 * count * ROWS * 128 * WIDTH, size=(4 * count + 2) * MIB,
    )


def posterior_kernel(*refs):
    out = refs[-1]
    total = refs[0][...]
    for other in refs[1:-1]:
        total = total + other[...]
    total = total.reshape(SHIFTS, P_DEV, 128)
    peak = jnp.max(jnp.max(total, axis=0), axis=1, keepdims=True)
    expo = jnp.exp(total - peak[None])
    norm = jnp.sum(jnp.sum(expo, axis=0), axis=1, keepdims=True)
    share = (expo / norm[None]).reshape(ROWS, 128)
    out[...] = share.T.astype(BF16)


def make_posterior(parts):
    (out,) = local(posterior_kernel, "posterior", [((128, ROWS), BF16)], [], parts, 4, size=MIB // 2)
    return out


def accum_kernel(part, flag_ref, *refs):
    rows, posts, outs = refs[:G], refs[G : 2 * G], refs[2 * G :]

    @pl.loop(0, NB)
    def _(block):
        sums = []
        for half in range(2):
            start = pl.multiple_of(block * 2 * COLS + half * COLS + part * HALF, HALF)
            total = jnp.dot(posts[0][...], rows[0][:, pl.ds(start, HALF)], preferred_element_type=F32)
            for n in range(1, G):
                total = total + jnp.dot(
                    posts[n][...], rows[n][:, pl.ds(start, HALF)], preferred_element_type=F32
                )
            sums.append(total)
        if part == 0:
            for n in range(Y):
                for half, total in enumerate(sums):
                    spot = pl.multiple_of(block * COLS + half * HALF, HALF)
                    outs[n][:, pl.ds(spot, HALF)] = total[n * 32 : (n + 1) * 32].astype(BF16)
        else:
            for n in range(X):
                low = n & 1
                upper = flag_ref[n] == 1
                spot = pl.multiple_of(block * HALF, HALF)
                for k in range(Y):
                    mine = slice(k * 32 + low * 16, k * 32 + low * 16 + 16)
                    chosen = jnp.where(upper, sums[1][mine], sums[0][mine])
                    outs[n][k * 16 : (k + 1) * 16, pl.ds(spot, HALF)] = chosen.astype(BF16)


def make_accum(part, flags, rows, posts):
    shape = (32, NB * COLS) if part == 0 else (64, NB * HALF)
    return local(
        lambda *refs: accum_kernel(part, *refs), "weighted_sums", [(shape, BF16)] * 4, [flags],
        [*rows, *posts], 8, flops=2 * G * ROWS * 128 * NB * COLS, size=(2 * G + 1) * MIB,
    )


def added(values):
    total = values[0].astype(F32)
    for value in values[1:]:
        total = total + value.astype(F32)
    return total


PIECES = [((16, NB * HALF), F32)] + [((16, NB * HALF), BF16)] * 3


def first_kernel(flag_ref, *refs):
    outs = refs[4:]
    for block in range(NB):
        start = block * COLS
        real = added([ref[:, start : start + HALF] for ref in refs[:4]])
        imag = added([ref[:, start + HALF : start + COLS] for ref in refs[:4]])
        for n, out in enumerate(outs):
            mine = slice((n & 1) * 16, (n & 1) * 16 + 16)
            chosen = jnp.where(flag_ref[n] == 1, imag[mine], real[mine])
            out[:, block * HALF : (block + 1) * HALF] = chosen.astype(out.dtype)


def second_kernel(*refs):
    for n, out in enumerate(refs[4:]):
        out[...] = added([ref[n * 16 : (n + 1) * 16] for ref in refs[:4]]).astype(out.dtype)


def joined_kernel(block_ref, *refs):
    for n, out in enumerate(refs[8:]):
        spot = pl.ds(pl.multiple_of(((block_ref[0] + n) % NB) * HALF, HALF), HALF)
        out[:, :HALF] = added([ref[:, spot] for ref in refs[:4]]).astype(out.dtype)
        out[:, HALF:] = added([ref[:, spot] for ref in refs[4:8]]).astype(out.dtype)


def after(value, *others):
    return lax.optimization_barrier((value, *others))[0]


def per_device(refs, particles, shift_ids, wedge, defocus, inv_sigma):
    dom = lax.axis_index("dom")
    x_at = (dom // 16) * 2 + lax.axis_index("blk") % 2
    member = (dom % G).astype(jnp.int32).reshape(1)
    block = ((dom % 16) // G).astype(jnp.int32).reshape(1)
    flags = (((x_at + jnp.arange(X)) % X) // 2).astype(jnp.int32)
    geo = jnp.asarray(geometry())

    gathered = {}
    own = own_columns(member, refs)
    gathered[0, 0] = own
    gathered[1, 0] = send(own, moves(dy=-1))
    gathered[3, 0] = send(own, moves(dy=1))
    gathered[2, 0] = send(own, moves(dy=2))
    chunks = split_particles(member, own, particles, shift_ids, wedge, defocus, inv_sigma)
    got = {0: chunks[0]}
    got[2] = send(chunks[2], partners(2))
    got[1] = send(chunks[1], partners(1))
    table = make_table(member, geo)
    rows, pens = {}, {}
    rows[0], pens[0] = make_rows(member, got[0], geo, table)
    gathered[0, 1] = send(after(own, got[1]), moves(dx=-1))
    gathered[1, 1] = send(after(gathered[1, 0], rows[0]), moves(dx=-1))
    gathered[3, 1] = send(after(gathered[3, 0], rows[0]), moves(dx=1))
    got[3] = send(after(chunks[3], rows[0]), partners(3))
    rows[1], pens[1] = make_rows(member, got[1], geo, table)
    gathered[2, 1] = send(after(gathered[2, 0], rows[1]), moves(dx=1))
    rows[2], pens[2] = make_rows(member, after(got[2], rows[1]), geo, table)
    blocks = [gathered[ky, kx] for ky in range(Y) for kx in range(2)]

    early = make_scores([rows[n] for n in range(3)], [pens[n] for n in range(3)], blocks)
    rows[3], pens[3] = make_rows(member, after(got[3], rows[2]), geo, table)
    late = make_scores([rows[3]], [pens[3]], blocks)
    parts = list(early) + list(late)
    arrived = [send(parts[n], partners(n)) for n in range(1, G)]
    posterior = make_posterior([parts[0]] + arrived)
    posts = [posterior] + [send(posterior, partners(n)) for n in range(1, G)]
    rows = [rows[n] for n in range(G)]

    first = make_accum(0, flags, rows, posts)
    first = [first[0]] + [send(first[n], moves(dy=n)) for n in range(1, Y)]
    second = make_accum(1, flags, rows, posts)
    second = [second[0]] + [send(second[n], moves(dx=n)) for n in range(1, X)]
    first = local(first_kernel, "first_sums", PIECES, [flags], first, 4, size=MIB)
    first = [first[0]] + [send(first[n], moves(dx=n)) for n in range(1, X)]
    second = local(second_kernel, "second_sums", PIECES, [], second, 4, size=MIB)
    second = [second[0]] + [send(second[n], moves(dy=n)) for n in range(1, Y)]
    outs = [((16, COLS), F32)] + [((16, COLS), BF16)] * (NB - 1)
    ends = local(joined_kernel, "joined_sums", outs, [block], [*first, *second], 4, size=MIB)
    return added([ends[0]] + [send(ends[n], moves(dz=n * (G // 2))) for n in range(1, NB)])


def solution(mesh):
    return jax.shard_map(
        per_device,
        mesh=mesh,
        in_specs=(
            P("blk", None),
            P(("blk", "dom"), None),
            P(("blk", "dom"), None),
            P(("blk", "dom"), None),
            P(("blk", "dom"), None),
            P(("blk", "dom")),
        ),
        out_specs=P("blk", "dom"),
        check_vma=False,
    )
```

```python
import math

import jax
import jax.numpy as jnp
import numpy as np
from jax import lax
from jax.experimental import pallas as pl
from jax.experimental.pallas import tpu as pltpu
from jax.sharding import PartitionSpec as P

BOX = 32
TILTS = 32
SHIFTS = 8
P_DEV = 32
Y, X, Z = 4, 4, 8
COLS = 1024
HALF = 512
G = 4
NB = 16 // G
ROWS = P_DEV * SHIFTS
WIDTH = NB * 2 * COLS
EXTRA = 384
AXES = ("blk", "dom")
F32, BF16 = jnp.float32, jnp.bfloat16
NT = (((1,), (1,)), ((), ()))
MIB = 1 << 20


def linear(y, x, z, core):
    y, x, z = y % Y, x % X, z % Z
    return (y * 2 + x % 2) * 32 + (x // 2) * 16 + z * 2 + core


def moves(dy=0, dx=0, dz=0):
    return [
        (linear(y, x, z, c), linear(y + dy, x + dx, z + dz, c))
        for y in range(Y) for x in range(X) for z in range(Z) for c in range(2)
    ]


def partners(k):
    return [
        (linear(y, x, z, c), linear(y, x, z ^ (k >> 1), c ^ (k & 1)))
        for y in range(Y) for x in range(X) for z in range(Z) for c in range(2)
    ]


def send(value, pairs):
    return lax.ppermute(value, AXES, pairs)


def geometry():
    position = np.arange(TILTS * HALF)
    tilt, within = position // HALF, position % HALF
    radial = (within // BOX).astype(np.float64)
    lateral = (within % BOX - BOX // 2).astype(np.float64)
    angle = (tilt - 0.5 * (TILTS - 1)) * (2.0 / TILTS)
    shell = (radial * radial + lateral * lateral) / (0.25 * BOX * BOX)
    zero = np.zeros_like(shell)
    table = np.stack([radial * np.cos(angle), lateral, radial * np.sin(angle), shell] + [zero] * 4)
    return table.reshape(8, 16, COLS).transpose(1, 0, 2).astype(np.float32)


def fold(turns):
    turns = turns - jnp.floor(turns + 0.5)
    far = jnp.abs(turns) > 0.25
    near = jnp.where(far, jnp.where(turns > 0, 0.5, -0.5) - turns, turns)
    return near * (2.0 * math.pi), far


def series(square, terms):
    total = jnp.full_like(square, terms[-1])
    for term in terms[-2::-1]:
        total = total * square + term
    return total


SIN_TERMS = [(-1) ** n / math.factorial(2 * n + 1) for n in range(6)]
COS_TERMS = [(-1) ** n / math.factorial(2 * n) for n in range(7)]


def sine_turns(turns):
    angle, _ = fold(turns)
    return angle * series(angle * angle, SIN_TERMS)


def held(value):
    return pltpu.with_memory_space_constraint(value, pltpu.VMEM)


SCALARS = pl.BlockSpec(memory_space=pltpu.SMEM)
WHOLE = pl.BlockSpec(memory_space=pltpu.VMEM)
PLACED = pl.BlockSpec(memory_space=pl.ANY)


def local(kernel, name, outs, scalars, arrays, limit, flops=0, size=0, placed=0, scratch=()):
    return pl.pallas_call(
        kernel,
        in_specs=[SCALARS] * len(scalars) + [PLACED] * placed + [WHOLE] * (len(arrays) - placed),
        out_specs=[WHOLE] * len(outs),
        out_shape=[pltpu.VMEM(shape, kind) for shape, kind in outs],
        scratch_shapes=list(scratch),
        cost_estimate=pl.CostEstimate(flops=0, bytes_accessed=0, transcendentals=0),
        compiler_params=pltpu.CompilerParams(vmem_limit_bytes=limit * MIB),
        name=name,
    )(*scalars, *[pltpu.with_memory_space_constraint(value, pltpu.HBM) for value in arrays[:placed]], *[held(value) for value in arrays[placed:]])


def table_kernel(member_ref, geo_ref, out_ref, picked_ref, sems):
    copies = [
        pltpu.make_async_copy(geo_ref.at[block * G + member_ref[0]], picked_ref.at[block], sems.at[block])
        for block in range(NB)
    ]
    for copy in copies:
        copy.start()
    ids = lax.broadcasted_iota(jnp.int32, (128, 1), 0).astype(F32)
    high = jnp.floor((ids + 0.5) * (1 / 25))
    middle = jnp.floor((ids - 25 * high + 0.5) * (1 / 5))
    low = ids - 25 * high - 5 * middle
    move_x, move_y, move_z = ((digit - 2.0) * (0.5 / BOX) for digit in (high, middle, low))
    for copy in copies:
        copy.wait()

    @pl.loop(0, NB)
    def _(block):
        geo = picked_ref[block]
        for tilt in range(2):
            part = geo[:, tilt * HALF : (tilt + 1) * HALF]
            turns = move_x * part[0:1] + move_y * part[1:2] + move_z * part[2:3]
            angle, far = fold(turns)
            square = angle * angle
            sine = angle * series(square, SIN_TERMS)
            cosine = series(square, COS_TERMS)
            cosine = jnp.where(far, -cosine, cosine)
            for at, values in enumerate((cosine, sine)):
                high = values.astype(BF16)
                low = (values - high.astype(F32)).astype(BF16)
                spot = pl.multiple_of(block * 2 * COLS + tilt * COLS + at * HALF, HALF)
                out_ref[0:128, pl.ds(spot, HALF)] = high
                out_ref[128:256, pl.ds(spot, HALF)] = low


def make_table(member, geo):
    return local(
        table_kernel, "phase_table", [((256, WIDTH), BF16), ((NB, 8, COLS), F32)], [member], [geo], 8,
        placed=1, scratch=[pltpu.SemaphoreType.DMA((NB,))],
    )


def column(part, block, who):
    return pl.ds(pl.multiple_of((part * 16 + block * G + who) * COLS, COLS), COLS)


def pieces_of(source, out, who, sems, base):
    return [
        pltpu.make_async_copy(
            source.at[:, column(part, block, who)],
            out.at[:, pl.ds((block * 2 + part) * COLS, COLS)],
            sems.at[base + block * 2 + part],
        )
        for block in range(NB) for part in range(2)
    ]


def own_kernel(member_ref, source, out, sems):
    copies = pieces_of(source, out, member_ref[0], sems, 0)
    for copy in copies:
        copy.start()
    for copy in copies:
        copy.wait()


def own_columns(member, refs):
    (own,) = local(
        own_kernel, "own_references", [((16, WIDTH), BF16)], [member], [refs], 4, size=MIB // 2,
        placed=1, scratch=[pltpu.SemaphoreType.DMA((2 * NB,))],
    )
    return own


def parts_of(values):
    high = values.astype(BF16)
    rest = values - high.astype(F32)
    middle = rest.astype(BF16)
    return high, middle, (rest - middle.astype(F32)).astype(BF16)


def turned_over(values):
    rows, columns = values.shape
    same = lax.broadcasted_iota(jnp.int32, (columns, columns), 0) == lax.broadcasted_iota(
        jnp.int32, (columns, columns), 1
    )
    return sum(
        lax.dot_general(same.astype(BF16), part, NT, preferred_element_type=F32)
        for part in parts_of(values)
    )


def split_kernel(member_ref, source, ids, wedge, focus, sigma, after, *refs):
    outs, (ids_in, wedge_in, focus_in, sigma_in, sems, more) = refs[:G], refs[G:]
    copies = []
    for n in (2, 1, 3, 0):
        copies += pieces_of(source, outs[n], member_ref[0] ^ n, sems, n * 2 * NB)
    settings = [
        pltpu.make_async_copy(at, to, more.at[n])
        for n, (at, to) in enumerate(
            ((ids, ids_in), (wedge, wedge_in), (focus, focus_in), (sigma, sigma_in))
        )
    ]
    for copy in copies + settings:
        copy.start()
    for copy in settings:
        copy.wait()
    first = jnp.concatenate(
        [ids_in[...].astype(F32), jnp.broadcast_to(sigma_in[...], (8, P_DEV))], axis=0
    )
    info = jnp.concatenate(
        [
            turned_over(first),
            wedge_in[...].astype(F32),
            focus_in[...],
            jnp.zeros((P_DEV, 128 - 16 - 2 * TILTS), F32),
        ],
        axis=1,
    )
    for spot, piece in enumerate(parts_of(info)):
        for out in outs:
            out[:, WIDTH + spot * 128 : WIDTH + (spot + 1) * 128] = piece
    for copy in copies:
        copy.wait()


def split_particles(member, after, particles, shift_ids, wedge, defocus, inv_sigma):
    return local(
        split_kernel, "split_particles", [((P_DEV, WIDTH + EXTRA), BF16)] * G, [member],
        [particles, shift_ids.T, wedge, defocus, inv_sigma[None], after], 4, placed=5,
        scratch=[
            pltpu.VMEM((SHIFTS, P_DEV), jnp.int32),
            pltpu.VMEM((P_DEV, TILTS), jnp.int32),
            pltpu.VMEM((P_DEV, TILTS), F32),
            pltpu.VMEM((1, P_DEV), F32),
            pltpu.SemaphoreType.DMA((G * 2 * NB,)),
            pltpu.SemaphoreType.DMA((4,)),
        ],
    )


def rows_kernel(member_ref, x_ref, geo_ref, table_ref, rows_ref, pen_ref):
    info = sum(x_ref[:, WIDTH + n * 128 : WIDTH + (n + 1) * 128].astype(F32) for n in range(3))
    lane = lax.broadcasted_iota(jnp.int32, (ROWS, 256), 1) & 127
    ids = jnp.concatenate([info[:, s : s + 1] for s in range(SHIFTS)], axis=0)
    pick = (ids == lane.astype(F32)).astype(BF16)
    sigma = info[:, SHIFTS : SHIFTS + 1]
    small = lax.broadcasted_iota(jnp.int32, (P_DEV, 128), 1)

    @pl.loop(0, NB)
    def _(block):
        first = 2 * (block * G + member_ref[0]) + 16
        start = pl.multiple_of(block * 2 * COLS, 2 * COLS)
        for tilt in range(2):
            kept = jnp.sum(jnp.where(small == first + tilt, info, 0.0), axis=1, keepdims=True)
            focus = jnp.sum(jnp.where(small == first + tilt + TILTS, info, 0.0), axis=1, keepdims=True)
            shell = geo_ref[block, 3:4, tilt * HALF : (tilt + 1) * HALF]
            transfer = -sine_turns((4.0 * focus * shell + 0.1) * (0.5 / math.pi))
            weight = kept * transfer * sigma
            spot = pl.multiple_of(block * COLS + tilt * HALF, HALF)
            pen_ref[:, pl.ds(spot, HALF)] = (0.5 * weight * transfer).astype(BF16)
            lower, upper = pl.ds(start + tilt * HALF, HALF), pl.ds(start + COLS + tilt * HALF, HALF)
            real = (weight * x_ref[:, lower].astype(F32))[None]
            imag = (weight * x_ref[:, upper].astype(F32))[None]
            turned = jnp.dot(
                pick, table_ref[:, pl.ds(start + tilt * COLS, COLS)], preferred_element_type=F32
            ).reshape(SHIFTS, P_DEV, COLS)
            cosine, sine = turned[:, :, :HALF], turned[:, :, HALF:]
            rows_ref[:, lower] = (real * cosine + imag * sine).reshape(ROWS, HALF).astype(BF16)
            rows_ref[:, upper] = (imag * cosine - real * sine).reshape(ROWS, HALF).astype(BF16)


def make_rows(member, x, geo, table):
    return local(
        rows_kernel, "shifted_rows", [((ROWS, WIDTH), BF16), ((P_DEV, NB * COLS), BF16)], [member],
        [x, geo, table], 12, flops=2 * ROWS * 256 * WIDTH, size=9 * MIB,
    )


def scores_kernel(count, *refs):
    blocks = refs[2 * count : 2 * count + 8]
    outs = refs[2 * count + 8 :]
    stacked = jnp.concatenate([block[...] for block in blocks], axis=0)
    power = []
    for block in range(NB):
        start = block * 2 * COLS
        real = stacked[:, start : start + COLS].astype(F32)
        imag = stacked[:, start + COLS : start + 2 * COLS].astype(F32)
        power.append((real * real + imag * imag).astype(BF16))
    power = jnp.concatenate(power, axis=1)
    pens = jnp.concatenate([pen[...] for pen in refs[count : 2 * count]], axis=0)
    rows = jnp.concatenate([row[...] for row in refs[:count]], axis=0)
    energy = lax.dot_general(pens, power, NT, preferred_element_type=F32)
    total = lax.dot_general(rows, stacked, NT, preferred_element_type=F32)
    for n, out in enumerate(outs):
        mine = total[n * ROWS : (n + 1) * ROWS].reshape(SHIFTS, P_DEV, 128)
        out[...] = (mine - energy[None, n * P_DEV : (n + 1) * P_DEV]).reshape(ROWS, 128)


def make_scores(rows, pens, blocks):
    count = len(rows)
    return local(
        lambda *refs: scores_kernel(count, *refs), "partial_scores", [((ROWS, 128), F32)] * count, [],
        [*rows, *pens, *blocks], 12, flops=2 * count * ROWS * 128 * WIDTH, size=(4 * count + 2) * MIB,
    )


def posterior_kernel(*refs):
    out = refs[-1]
    total = refs[0][...]
    for other in refs[1:-1]:
        total = total + other[...]
    total = total.reshape(SHIFTS, P_DEV, 128)
    peak = jnp.max(jnp.max(total, axis=0), axis=1, keepdims=True)
    expo = jnp.exp(total - peak[None])
    norm = jnp.sum(jnp.sum(expo, axis=0), axis=1, keepdims=True)
    share = (expo / norm[None]).reshape(ROWS, 128)
    out[...] = share.T.astype(BF16)


def make_posterior(parts):
    (out,) = local(posterior_kernel, "posterior", [((128, ROWS), BF16)], [], parts, 4, size=MIB // 2)
    return out


def accum_kernel(part, flag_ref, *refs):
    real, imag, posts, outs = refs[:G], refs[G : 2 * G], refs[2 * G : 3 * G], refs[3 * G :]
    sums = []
    for rows in (real, imag):
        total = jnp.dot(posts[0][...], rows[0][...], preferred_element_type=F32)
        for n in range(1, G):
            total = total + jnp.dot(posts[n][...], rows[n][...], preferred_element_type=F32)
        sums.append(total)
    if part == 0:
        for n in range(Y):
            for half, total in enumerate(sums):
                outs[n][:, half * HALF : (half + 1) * HALF] = total[n * 32 : (n + 1) * 32].astype(BF16)
    else:
        for n in range(X):
            low = n & 1
            upper = flag_ref[n] == 1
            for k in range(Y):
                mine = slice(k * 32 + low * 16, k * 32 + low * 16 + 16)
                chosen = jnp.where(upper, sums[1][mine], sums[0][mine])
                outs[n][k * 16 : (k + 1) * 16] = chosen.astype(BF16)


def make_accum(part, flags, rows, posts):
    shape = (32, COLS) if part == 0 else (64, HALF)
    rows = [pltpu.with_memory_space_constraint(value, pltpu.HBM) for value in rows]
    return pl.pallas_call(
        lambda *refs: accum_kernel(part, *refs),
        grid_spec=pltpu.PrefetchScalarGridSpec(
            num_scalar_prefetch=1,
            grid=(NB,),
            in_specs=[pl.BlockSpec((ROWS, HALF), lambda b, f: (0, 4 * b + part))] * G
            + [pl.BlockSpec((ROWS, HALF), lambda b, f: (0, 4 * b + 2 + part))] * G
            + [pl.BlockSpec((128, ROWS), lambda b, f: (0, 0))] * G,
            out_specs=[pl.BlockSpec(shape, lambda b, f: (0, b))] * 4,
        ),
        out_shape=[pltpu.VMEM((shape[0], NB * shape[1]), BF16)] * 4,
        cost_estimate=pl.CostEstimate(flops=0, bytes_accessed=0, transcendentals=0),
        compiler_params=pltpu.CompilerParams(vmem_limit_bytes=16 * MIB),
        name="weighted_sums",
    )(flags, *rows, *rows, *posts)


def added(values):
    total = values[0].astype(F32)
    for value in values[1:]:
        total = total + value.astype(F32)
    return total


PIECES = [((16, NB * HALF), F32)] + [((16, NB * HALF), BF16)] * 3


def first_kernel(flag_ref, *refs):
    outs = refs[4:]
    for block in range(NB):
        start = block * COLS
        real = added([ref[:, start : start + HALF] for ref in refs[:4]])
        imag = added([ref[:, start + HALF : start + COLS] for ref in refs[:4]])
        for n, out in enumerate(outs):
            mine = slice((n & 1) * 16, (n & 1) * 16 + 16)
            chosen = jnp.where(flag_ref[n] == 1, imag[mine], real[mine])
            out[:, block * HALF : (block + 1) * HALF] = chosen.astype(out.dtype)


def second_kernel(*refs):
    for n, out in enumerate(refs[4:]):
        out[...] = added([ref[n * 16 : (n + 1) * 16] for ref in refs[:4]]).astype(out.dtype)


def joined_kernel(block_ref, *refs):
    for n, out in enumerate(refs[8:]):
        spot = pl.ds(pl.multiple_of(((block_ref[0] + n) % NB) * HALF, HALF), HALF)
        out[:, :HALF] = added([ref[:, spot] for ref in refs[:4]]).astype(out.dtype)
        out[:, HALF:] = added([ref[:, spot] for ref in refs[4:8]]).astype(out.dtype)


def after(value, *others):
    return lax.optimization_barrier((value, *others))[0]


def per_device(refs, particles, shift_ids, wedge, defocus, inv_sigma):
    dom = lax.axis_index("dom")
    x_at = (dom // 16) * 2 + lax.axis_index("blk") % 2
    member = (dom % G).astype(jnp.int32).reshape(1)
    block = ((dom % 16) // G).astype(jnp.int32).reshape(1)
    flags = (((x_at + jnp.arange(X)) % X) // 2).astype(jnp.int32)
    geo = jnp.asarray(geometry())

    gathered = {}
    own = own_columns(member, refs)
    gathered[0, 0] = own
    gathered[1, 0] = send(own, moves(dy=-1))
    gathered[3, 0] = send(own, moves(dy=1))
    chunks = split_particles(member, own, particles, shift_ids, wedge, defocus, inv_sigma)
    got = {0: chunks[0]}
    got[2] = send(chunks[2], partners(2))
    gathered[2, 0] = send(own, moves(dy=2))
    gathered[0, 1] = send(own, moves(dx=-1))
    gathered[1, 1] = send(gathered[1, 0], moves(dx=-1))
    gathered[3, 1] = send(gathered[3, 0], moves(dx=1))
    table, geo = make_table(member, geo)
    rows, pens = {}, {}
    rows[0], pens[0] = make_rows(member, got[0], geo, table)
    wave = [got[2], *[gathered[at] for at in ((1, 0), (3, 0), (2, 0), (0, 1))], rows[0]]
    rows[2], pens[2] = make_rows(member, after(got[2], *wave[1:]), geo, table)
    got[3] = send(after(chunks[3], *wave), partners(3))
    gathered[2, 1] = send(gathered[2, 0], moves(dx=1))
    got[1] = send(after(chunks[1], *wave), partners(1))
    rows[1], pens[1] = make_rows(member, after(got[1], rows[2]), geo, table)
    blocks = [gathered[ky, kx] for ky in range(Y) for kx in range(2)]

    early = make_scores([rows[n] for n in range(3)], [pens[n] for n in range(3)], blocks)
    rows[3], pens[3] = make_rows(member, after(got[3], rows[1]), geo, table)
    late = make_scores([rows[3]], [pens[3]], blocks)
    parts = list(early) + list(late)
    arrived = [send(parts[n], partners(n)) for n in range(1, G)]
    posterior = make_posterior([parts[0]] + arrived)
    posts = [posterior] + [send(posterior, partners(n)) for n in range(1, G)]
    rows = [rows[n] for n in range(G)]

    first = make_accum(0, flags, rows, posts)
    first = [first[0]] + [send(first[n], moves(dy=n)) for n in range(1, Y)]
    second = make_accum(1, flags, rows, posts)
    second = [second[0]] + [send(second[n], moves(dx=n)) for n in range(1, X)]
    first = local(first_kernel, "first_sums", PIECES, [flags], first, 4, size=MIB)
    first = [first[0]] + [send(first[n], moves(dx=n)) for n in range(1, X)]
    second = local(second_kernel, "second_sums", PIECES, [], second, 4, size=MIB)
    second = [second[0]] + [send(second[n], moves(dy=n)) for n in range(1, Y)]
    outs = [((16, COLS), F32)] + [((16, COLS), BF16)] * (NB - 1)
    ends = local(joined_kernel, "joined_sums", outs, [block], [*first, *second], 4, size=MIB)
    return added([ends[0]] + [send(ends[n], moves(dz=n * (G // 2))) for n in range(1, NB)])


def solution(mesh):
    return jax.shard_map(
        per_device,
        mesh=mesh,
        in_specs=(
            P("blk", None),
            P(("blk", "dom"), None),
            P(("blk", "dom"), None),
            P(("blk", "dom"), None),
            P(("blk", "dom"), None),
            P(("blk", "dom")),
        ),
        out_specs=P("blk", "dom"),
        check_vma=False,
    )
```

```python
import math

import jax
import jax.numpy as jnp
import numpy as np
from jax import lax
from jax.experimental import pallas as pl
from jax.experimental.pallas import tpu as pltpu
from jax.sharding import PartitionSpec as P

BOX = 32
TILTS = 32
SHIFTS = 8
P_DEV = 32
Y, X, Z = 4, 4, 8
COLS = 1024
HALF = 512
G = 4
NB = 16 // G
ROWS = P_DEV * SHIFTS
WIDTH = NB * 2 * COLS
EXTRA = 384
AXES = ("blk", "dom")
F32, BF16 = jnp.float32, jnp.bfloat16
NT = (((1,), (1,)), ((), ()))
MIB = 1 << 20


def linear(y, x, z, core):
    y, x, z = y % Y, x % X, z % Z
    return (y * 2 + x % 2) * 32 + (x // 2) * 16 + z * 2 + core


def moves(dy=0, dx=0, dz=0):
    return [
        (linear(y, x, z, c), linear(y + dy, x + dx, z + dz, c))
        for y in range(Y) for x in range(X) for z in range(Z) for c in range(2)
    ]


def partners(k):
    return [
        (linear(y, x, z, c), linear(y, x, z ^ (k >> 1), c ^ (k & 1)))
        for y in range(Y) for x in range(X) for z in range(Z) for c in range(2)
    ]


def send(value, pairs):
    return lax.ppermute(value, AXES, pairs)


def geometry():
    position = np.arange(TILTS * HALF)
    tilt, within = position // HALF, position % HALF
    radial = (within // BOX).astype(np.float64)
    lateral = (within % BOX - BOX // 2).astype(np.float64)
    angle = (tilt - 0.5 * (TILTS - 1)) * (2.0 / TILTS)
    shell = (radial * radial + lateral * lateral) / (0.25 * BOX * BOX)
    zero = np.zeros_like(shell)
    table = np.stack([radial * np.cos(angle), lateral, radial * np.sin(angle), shell] + [zero] * 4)
    return table.reshape(8, 16, COLS).transpose(1, 0, 2).astype(np.float32)


def fold(turns):
    turns = turns - jnp.floor(turns + 0.5)
    far = jnp.abs(turns) > 0.25
    near = jnp.where(far, jnp.where(turns > 0, 0.5, -0.5) - turns, turns)
    return near * (2.0 * math.pi), far


def series(square, terms):
    total = jnp.full_like(square, terms[-1])
    for term in terms[-2::-1]:
        total = total * square + term
    return total


SIN_TERMS = [(-1) ** n / math.factorial(2 * n + 1) for n in range(6)]
COS_TERMS = [(-1) ** n / math.factorial(2 * n) for n in range(7)]


def sine_turns(turns):
    angle, _ = fold(turns)
    return angle * series(angle * angle, SIN_TERMS)


def held(value):
    return pltpu.with_memory_space_constraint(value, pltpu.VMEM)


SCALARS = pl.BlockSpec(memory_space=pltpu.SMEM)
WHOLE = pl.BlockSpec(memory_space=pltpu.VMEM)
PLACED = pl.BlockSpec(memory_space=pl.ANY)


def local(kernel, name, outs, scalars, arrays, limit, placed=0, scratch=()):
    return pl.pallas_call(
        kernel,
        in_specs=[SCALARS] * len(scalars) + [PLACED] * placed + [WHOLE] * (len(arrays) - placed),
        out_specs=[WHOLE] * len(outs),
        out_shape=[pltpu.VMEM(shape, kind) for shape, kind in outs],
        scratch_shapes=list(scratch),
        cost_estimate=pl.CostEstimate(flops=0, bytes_accessed=0, transcendentals=0),
        compiler_params=pltpu.CompilerParams(vmem_limit_bytes=limit * MIB),
        name=name,
    )(
        *scalars,
        *[pltpu.with_memory_space_constraint(value, pltpu.HBM) for value in arrays[:placed]],
        *[held(value) for value in arrays[placed:]],
    )


def table_kernel(member_ref, geo_ref, out_ref, picked_ref, sems):
    copies = [
        pltpu.make_async_copy(geo_ref.at[block * G + member_ref[0]], picked_ref.at[block], sems.at[block])
        for block in range(NB)
    ]
    for copy in copies:
        copy.start()
    ids = lax.broadcasted_iota(jnp.int32, (128, 1), 0).astype(F32)
    high = jnp.floor((ids + 0.5) * (1 / 25))
    middle = jnp.floor((ids - 25 * high + 0.5) * (1 / 5))
    low = ids - 25 * high - 5 * middle
    move_x, move_y, move_z = ((digit - 2.0) * (0.5 / BOX) for digit in (high, middle, low))
    for copy in copies:
        copy.wait()

    @pl.loop(0, NB)
    def _(block):
        geo = picked_ref[block]
        for tilt in range(2):
            part = geo[:, tilt * HALF : (tilt + 1) * HALF]
            turns = move_x * part[0:1] + move_y * part[1:2] + move_z * part[2:3]
            angle, far = fold(turns)
            square = angle * angle
            sine = angle * series(square, SIN_TERMS)
            cosine = series(square, COS_TERMS)
            cosine = jnp.where(far, -cosine, cosine)
            for at, values in enumerate((cosine, sine)):
                high = values.astype(BF16)
                low = (values - high.astype(F32)).astype(BF16)
                spot = pl.multiple_of(block * 2 * COLS + tilt * COLS + at * HALF, HALF)
                out_ref[0:128, pl.ds(spot, HALF)] = high
                out_ref[128:256, pl.ds(spot, HALF)] = low


def make_table(member, geo):
    return local(
        table_kernel, "phase_table", [((256, WIDTH), BF16), ((NB, 8, COLS), F32)], [member], [geo], 8,
        placed=1, scratch=[pltpu.SemaphoreType.DMA((NB,))],
    )


def column(part, block, who):
    return pl.ds(pl.multiple_of((part * 16 + block * G + who) * COLS, COLS), COLS)


def pieces_of(source, out, who, sems, base):
    return [
        pltpu.make_async_copy(
            source.at[:, column(part, block, who)],
            out.at[:, pl.ds((block * 2 + part) * COLS, COLS)],
            sems.at[base + block * 2 + part],
        )
        for block in range(NB) for part in range(2)
    ]


def own_kernel(member_ref, source, out, sems):
    copies = pieces_of(source, out, member_ref[0], sems, 0)
    for copy in copies:
        copy.start()
    for copy in copies:
        copy.wait()


def own_columns(member, refs):
    (own,) = local(
        own_kernel, "own_references", [((16, WIDTH), BF16)], [member], [refs], 4,
        placed=1, scratch=[pltpu.SemaphoreType.DMA((2 * NB,))],
    )
    return own


def parts_of(values):
    high = values.astype(BF16)
    rest = values - high.astype(F32)
    middle = rest.astype(BF16)
    return high, middle, (rest - middle.astype(F32)).astype(BF16)


def turned_over(values):
    rows, columns = values.shape
    same = lax.broadcasted_iota(jnp.int32, (columns, columns), 0) == lax.broadcasted_iota(
        jnp.int32, (columns, columns), 1
    )
    return sum(
        lax.dot_general(same.astype(BF16), part, NT, preferred_element_type=F32)
        for part in parts_of(values)
    )


def split_kernel(member_ref, source, ids, wedge, focus, sigma, after, *refs):
    outs, (ids_in, wedge_in, focus_in, sigma_in, sems, more) = refs[:G], refs[G:]
    copies = []
    for n in (2, 1, 3, 0):
        copies += pieces_of(source, outs[n], member_ref[0] ^ n, sems, n * 2 * NB)
    settings = [
        pltpu.make_async_copy(at, to, more.at[n])
        for n, (at, to) in enumerate(
            ((ids, ids_in), (wedge, wedge_in), (focus, focus_in), (sigma, sigma_in))
        )
    ]
    for copy in copies + settings:
        copy.start()
    for copy in settings:
        copy.wait()
    first = jnp.concatenate(
        [ids_in[...].astype(F32), jnp.broadcast_to(sigma_in[...], (8, P_DEV))], axis=0
    )
    info = jnp.concatenate(
        [
            turned_over(first),
            wedge_in[...].astype(F32),
            focus_in[...],
            jnp.zeros((P_DEV, 128 - 16 - 2 * TILTS), F32),
        ],
        axis=1,
    )
    for spot, piece in enumerate(parts_of(info)):
        for out in outs:
            out[:, WIDTH + spot * 128 : WIDTH + (spot + 1) * 128] = piece
    for copy in copies:
        copy.wait()


def split_particles(member, after, particles, shift_ids, wedge, defocus, inv_sigma):
    return local(
        split_kernel, "split_particles", [((P_DEV, WIDTH + EXTRA), BF16)] * G, [member],
        [particles, shift_ids.T, wedge, defocus, inv_sigma[None], after], 4, placed=5,
        scratch=[
            pltpu.VMEM((SHIFTS, P_DEV), jnp.int32),
            pltpu.VMEM((P_DEV, TILTS), jnp.int32),
            pltpu.VMEM((P_DEV, TILTS), F32),
            pltpu.VMEM((1, P_DEV), F32),
            pltpu.SemaphoreType.DMA((G * 2 * NB,)),
            pltpu.SemaphoreType.DMA((4,)),
        ],
    )


def rows_kernel(member_ref, x_ref, geo_ref, table_ref, rows_ref, pen_ref):
    info = sum(x_ref[:, WIDTH + n * 128 : WIDTH + (n + 1) * 128].astype(F32) for n in range(3))
    lane = lax.broadcasted_iota(jnp.int32, (ROWS, 256), 1) & 127
    ids = jnp.concatenate([info[:, s : s + 1] for s in range(SHIFTS)], axis=0)
    pick = (ids == lane.astype(F32)).astype(BF16)
    sigma = info[:, SHIFTS : SHIFTS + 1]
    small = lax.broadcasted_iota(jnp.int32, (P_DEV, 128), 1)

    @pl.loop(0, NB)
    def _(block):
        first = 2 * (block * G + member_ref[0]) + 16
        start = pl.multiple_of(block * 2 * COLS, 2 * COLS)
        for tilt in range(2):
            kept = jnp.sum(jnp.where(small == first + tilt, info, 0.0), axis=1, keepdims=True)
            focus = jnp.sum(jnp.where(small == first + tilt + TILTS, info, 0.0), axis=1, keepdims=True)
            shell = geo_ref[block, 3:4, tilt * HALF : (tilt + 1) * HALF]
            transfer = -sine_turns((4.0 * focus * shell + 0.1) * (0.5 / math.pi))
            weight = kept * transfer * sigma
            spot = pl.multiple_of(block * COLS + tilt * HALF, HALF)
            pen_ref[:, pl.ds(spot, HALF)] = (0.5 * weight * transfer).astype(BF16)
            lower, upper = pl.ds(start + tilt * HALF, HALF), pl.ds(start + COLS + tilt * HALF, HALF)
            real = (weight * x_ref[:, lower].astype(F32))[None]
            imag = (weight * x_ref[:, upper].astype(F32))[None]
            turned = jnp.dot(
                pick, table_ref[:, pl.ds(start + tilt * COLS, COLS)], preferred_element_type=F32
            ).reshape(SHIFTS, P_DEV, COLS)
            cosine, sine = turned[:, :, :HALF], turned[:, :, HALF:]
            rows_ref[:, lower] = (real * cosine + imag * sine).reshape(ROWS, HALF).astype(BF16)
            rows_ref[:, upper] = (imag * cosine - real * sine).reshape(ROWS, HALF).astype(BF16)


def make_rows(member, x, geo, table):
    return local(
        rows_kernel, "shifted_rows", [((ROWS, WIDTH), BF16), ((P_DEV, NB * COLS), BF16)], [member],
        [x, geo, table], 12,
    )


def scores_kernel(count, *refs):
    blocks = refs[2 * count : 2 * count + 8]
    outs = refs[2 * count + 8 :]
    stacked = jnp.concatenate([block[...] for block in blocks], axis=0)
    power = []
    for block in range(NB):
        start = block * 2 * COLS
        real = stacked[:, start : start + COLS].astype(F32)
        imag = stacked[:, start + COLS : start + 2 * COLS].astype(F32)
        power.append((real * real + imag * imag).astype(BF16))
    power = jnp.concatenate(power, axis=1)
    pens = jnp.concatenate([pen[...] for pen in refs[count : 2 * count]], axis=0)
    rows = jnp.concatenate([row[...] for row in refs[:count]], axis=0)
    energy = lax.dot_general(pens, power, NT, preferred_element_type=F32)
    total = lax.dot_general(rows, stacked, NT, preferred_element_type=F32)
    for n, out in enumerate(outs):
        mine = total[n * ROWS : (n + 1) * ROWS].reshape(SHIFTS, P_DEV, 128)
        out[...] = (mine - energy[None, n * P_DEV : (n + 1) * P_DEV]).reshape(ROWS, 128)


def make_scores(rows, pens, blocks):
    count = len(rows)
    return local(
        lambda *refs: scores_kernel(count, *refs), "partial_scores", [((ROWS, 128), F32)] * count, [],
        [*rows, *pens, *blocks], 12,
    )


def posterior_kernel(*refs):
    out = refs[-1]
    total = refs[0][...]
    for other in refs[1:-1]:
        total = total + other[...]
    total = total.reshape(SHIFTS, P_DEV, 128)
    peak = jnp.max(jnp.max(total, axis=0), axis=1, keepdims=True)
    expo = jnp.exp(total - peak[None])
    norm = jnp.sum(jnp.sum(expo, axis=0), axis=1, keepdims=True)
    share = (expo / norm[None]).reshape(ROWS, 128)
    out[...] = share.T.astype(BF16)


def make_posterior(parts):
    (out,) = local(posterior_kernel, "posterior", [((128, ROWS), BF16)], [], parts, 4)
    return out


def accum_kernel(flag_ref, *refs):
    rows, posts, outs = refs[:G], refs[G : 2 * G], refs[2 * G :]
    for part in range(2):
        sums = []
        for half in range(2):
            lanes = slice(half * COLS + part * HALF, half * COLS + (part + 1) * HALF)
            total = jnp.dot(posts[0][...], rows[0][:, lanes], preferred_element_type=F32)
            for n in range(1, G):
                total = total + jnp.dot(posts[n][...], rows[n][:, lanes], preferred_element_type=F32)
            sums.append(total)
        if part == 0:
            for n in range(Y):
                for half, total in enumerate(sums):
                    outs[n][:, half * HALF : (half + 1) * HALF] = total[n * 32 : (n + 1) * 32].astype(BF16)
        else:
            for n in range(X):
                low = n & 1
                upper = flag_ref[n] == 1
                for k in range(Y):
                    mine = slice(k * 32 + low * 16, k * 32 + low * 16 + 16)
                    chosen = jnp.where(upper, sums[1][mine], sums[0][mine])
                    outs[Y + n][k * 16 : (k + 1) * 16] = chosen.astype(BF16)


def make_accum(flags, rows, posts):
    rows = [pltpu.with_memory_space_constraint(value, pltpu.HBM) for value in rows]
    shapes = [(32, COLS)] * Y + [(64, HALF)] * X
    outs = pl.pallas_call(
        accum_kernel,
        grid_spec=pltpu.PrefetchScalarGridSpec(
            num_scalar_prefetch=1,
            grid=(NB,),
            in_specs=[pl.BlockSpec((ROWS, 2 * COLS), lambda b, f: (0, b))] * G
            + [pl.BlockSpec((128, ROWS), lambda b, f: (0, 0))] * G,
            out_specs=[pl.BlockSpec(shape, lambda b, f: (0, b)) for shape in shapes],
        ),
        out_shape=[pltpu.VMEM((shape[0], NB * shape[1]), BF16) for shape in shapes],
        cost_estimate=pl.CostEstimate(flops=0, bytes_accessed=0, transcendentals=0),
        compiler_params=pltpu.CompilerParams(vmem_limit_bytes=16 * MIB),
        name="weighted_sums",
    )(flags, *rows, *posts)
    return outs[:Y], outs[Y:]


def added(values):
    total = values[0].astype(F32)
    for value in values[1:]:
        total = total + value.astype(F32)
    return total


PIECES = [((16, NB * HALF), F32)] + [((16, NB * HALF), BF16)] * 3


def first_kernel(flag_ref, *refs):
    outs = refs[4:]
    for block in range(NB):
        start = block * COLS
        real = added([ref[:, start : start + HALF] for ref in refs[:4]])
        imag = added([ref[:, start + HALF : start + COLS] for ref in refs[:4]])
        for n, out in enumerate(outs):
            mine = slice((n & 1) * 16, (n & 1) * 16 + 16)
            chosen = jnp.where(flag_ref[n] == 1, imag[mine], real[mine])
            out[:, block * HALF : (block + 1) * HALF] = chosen.astype(out.dtype)


def second_kernel(*refs):
    for n, out in enumerate(refs[4:]):
        out[...] = added([ref[n * 16 : (n + 1) * 16] for ref in refs[:4]]).astype(out.dtype)


def joined_kernel(block_ref, *refs):
    for n, out in enumerate(refs[8:]):
        spot = pl.ds(pl.multiple_of(((block_ref[0] + n) % NB) * HALF, HALF), HALF)
        out[:, :HALF] = added([ref[:, spot] for ref in refs[:4]]).astype(out.dtype)
        out[:, HALF:] = added([ref[:, spot] for ref in refs[4:8]]).astype(out.dtype)


def after(value, *others):
    return lax.optimization_barrier((value, *others))[0]


def per_device(refs, particles, shift_ids, wedge, defocus, inv_sigma):
    dom = lax.axis_index("dom")
    x_at = (dom // 16) * 2 + lax.axis_index("blk") % 2
    member = (dom % G).astype(jnp.int32).reshape(1)
    block = ((dom % 16) // G).astype(jnp.int32).reshape(1)
    flags = (((x_at + jnp.arange(X)) % X) // 2).astype(jnp.int32)
    geo = jnp.asarray(geometry())

    gathered = {}
    own = own_columns(member, refs)
    gathered[0, 0] = own
    gathered[1, 0] = send(own, moves(dy=-1))
    gathered[3, 0] = send(own, moves(dy=1))
    chunks = split_particles(member, own, particles, shift_ids, wedge, defocus, inv_sigma)
    got = {0: chunks[0]}
    got[2] = send(chunks[2], partners(2))
    got[1] = send(chunks[1], partners(1))
    gathered[2, 0] = send(own, moves(dy=2))
    table, geo = make_table(member, geo)
    wave = [got[1], got[2], gathered[1, 0], gathered[3, 0], gathered[2, 0], table]
    gathered[0, 1] = send(after(own, *wave), moves(dx=-1))
    gathered[1, 1] = send(after(gathered[1, 0], *wave), moves(dx=-1))
    gathered[3, 1] = send(after(gathered[3, 0], *wave), moves(dx=1))
    gathered[2, 1] = send(after(gathered[2, 0], *wave), moves(dx=1))
    got[3] = send(after(chunks[3], *wave), partners(3))
    rows, pens = {}, {}
    rows[0], pens[0] = make_rows(member, after(got[0], *wave), geo, table)
    rows[1], pens[1] = make_rows(member, after(got[1], rows[0]), geo, table)
    rows[2], pens[2] = make_rows(member, after(got[2], rows[1]), geo, table)
    rows[3], pens[3] = make_rows(member, after(got[3], rows[2]), geo, table)
    blocks = [gathered[ky, kx] for ky in range(Y) for kx in range(2)]

    rows = [rows[n] for n in range(G)]
    pens = [pens[n] for n in range(G)]
    parts = make_scores(rows, pens, blocks)
    arrived = [send(parts[n], partners(n)) for n in range(1, G)]
    posterior = make_posterior([parts[0], *arrived])
    posts = [posterior] + [send(posterior, partners(n)) for n in range(1, G)]

    first, second = make_accum(flags, rows, posts)
    first = [first[0]] + [send(first[n], moves(dy=n)) for n in range(1, Y)]
    second = [
        second[0],
        send(second[1], moves(dx=1)),
        send(after(second[2], first[1]), moves(dx=2)),
        send(second[3], moves(dx=3)),
    ]
    first = local(first_kernel, "first_sums", PIECES, [flags], first, 4)
    first = [first[0]] + [send(first[n], moves(dx=n)) for n in range(1, X)]
    second = local(second_kernel, "second_sums", PIECES, [], second, 4)
    second = [second[0]] + [send(second[n], moves(dy=n)) for n in range(1, Y)]
    outs = [((16, COLS), F32)] + [((16, COLS), BF16)] * (NB - 1)
    ends = local(joined_kernel, "joined_sums", outs, [block], [*first, *second], 4)
    return added([ends[0]] + [send(ends[n], moves(dz=n * (G // 2))) for n in range(1, NB)])


def solution(mesh):
    return jax.shard_map(
        per_device,
        mesh=mesh,
        in_specs=(
            P("blk", None),
            P(("blk", "dom"), None),
            P(("blk", "dom"), None),
            P(("blk", "dom"), None),
            P(("blk", "dom"), None),
            P(("blk", "dom")),
        ),
        out_specs=P("blk", "dom"),
        check_vma=False,
    )
```

```python
import math

import jax
import jax.numpy as jnp
import numpy as np
from jax import lax
from jax.experimental import pallas as pl
from jax.experimental.pallas import tpu as pltpu
from jax.sharding import PartitionSpec as P

BOX = 32
TILTS = 32
SHIFTS = 8
P_DEV = 32
Y, X, Z = 4, 4, 8
COLS = 1024
HALF = 512
G = 4
NB = 16 // G
ROWS = P_DEV * SHIFTS
WIDTH = NB * 2 * COLS
EXTRA = 384
AXES = ("blk", "dom")
F32, BF16 = jnp.float32, jnp.bfloat16
NT = (((1,), (1,)), ((), ()))
MIB = 1 << 20


def linear(y, x, z, core):
    y, x, z = y % Y, x % X, z % Z
    return (y * 2 + x % 2) * 32 + (x // 2) * 16 + z * 2 + core


def moves(dy=0, dx=0, dz=0):
    return [
        (linear(y, x, z, c), linear(y + dy, x + dx, z + dz, c))
        for y in range(Y) for x in range(X) for z in range(Z) for c in range(2)
    ]


def partners(k):
    return [
        (linear(y, x, z, c), linear(y, x, z ^ (k >> 1), c ^ (k & 1)))
        for y in range(Y) for x in range(X) for z in range(Z) for c in range(2)
    ]


def send(value, pairs):
    return lax.ppermute(value, AXES, pairs)


def geometry():
    position = np.arange(TILTS * HALF)
    tilt, within = position // HALF, position % HALF
    radial = (within // BOX).astype(np.float64)
    lateral = (within % BOX - BOX // 2).astype(np.float64)
    angle = (tilt - 0.5 * (TILTS - 1)) * (2.0 / TILTS)
    shell = (radial * radial + lateral * lateral) / (0.25 * BOX * BOX)
    zero = np.zeros_like(shell)
    table = np.stack([radial * np.cos(angle), lateral, radial * np.sin(angle), shell] + [zero] * 4)
    return table.reshape(8, 16, COLS).transpose(1, 0, 2).astype(np.float32)


def fold(turns):
    turns = turns - jnp.floor(turns + 0.5)
    far = jnp.abs(turns) > 0.25
    near = jnp.where(far, jnp.where(turns > 0, 0.5, -0.5) - turns, turns)
    return near * (2.0 * math.pi), far


def series(square, terms):
    total = jnp.full_like(square, terms[-1])
    for term in terms[-2::-1]:
        total = total * square + term
    return total


SIN_TERMS = [(-1) ** n / math.factorial(2 * n + 1) for n in range(6)]
COS_TERMS = [(-1) ** n / math.factorial(2 * n) for n in range(7)]


def sine_turns(turns):
    angle, _ = fold(turns)
    return angle * series(angle * angle, SIN_TERMS)


def held(value):
    return pltpu.with_memory_space_constraint(value, pltpu.VMEM)


SCALARS = pl.BlockSpec(memory_space=pltpu.SMEM)
WHOLE = pl.BlockSpec(memory_space=pltpu.VMEM)
PLACED = pl.BlockSpec(memory_space=pl.ANY)


def local(kernel, name, outs, scalars, arrays, limit, placed=0, scratch=()):
    return pl.pallas_call(
        kernel,
        in_specs=[SCALARS] * len(scalars) + [PLACED] * placed + [WHOLE] * (len(arrays) - placed),
        out_specs=[WHOLE] * len(outs),
        out_shape=[pltpu.VMEM(shape, kind) for shape, kind in outs],
        scratch_shapes=list(scratch),
        cost_estimate=pl.CostEstimate(flops=0, bytes_accessed=0, transcendentals=0),
        compiler_params=pltpu.CompilerParams(vmem_limit_bytes=limit * MIB),
        name=name,
    )(
        *scalars,
        *[pltpu.with_memory_space_constraint(value, pltpu.HBM) for value in arrays[:placed]],
        *[held(value) for value in arrays[placed:]],
    )


def table_kernel(where_ref, geo_ref, out_ref, picked_ref, sems):
    copies = [
        pltpu.make_async_copy(geo_ref.at[block * G + where_ref[0]], picked_ref.at[block], sems.at[block])
        for block in range(NB)
    ]
    for copy in copies:
        copy.start()
    ids = lax.broadcasted_iota(jnp.int32, (128, 1), 0).astype(F32)
    high = jnp.floor((ids + 0.5) * (1 / 25))
    middle = jnp.floor((ids - 25 * high + 0.5) * (1 / 5))
    low = ids - 25 * high - 5 * middle
    move_x, move_y, move_z = ((digit - 2.0) * (0.5 / BOX) for digit in (high, middle, low))
    for copy in copies:
        copy.wait()

    @pl.loop(0, NB)
    def _(block):
        geo = picked_ref[block]
        for tilt in range(2):
            part = geo[:, tilt * HALF : (tilt + 1) * HALF]
            turns = move_x * part[0:1] + move_y * part[1:2] + move_z * part[2:3]
            angle, far = fold(turns)
            square = angle * angle
            sine = angle * series(square, SIN_TERMS)
            cosine = series(square, COS_TERMS)
            cosine = jnp.where(far, -cosine, cosine)
            for at, values in enumerate((cosine, sine)):
                high = values.astype(BF16)
                low = (values - high.astype(F32)).astype(BF16)
                spot = pl.multiple_of(block * 2 * COLS + tilt * COLS + at * HALF, HALF)
                out_ref[0:128, pl.ds(spot, HALF)] = high
                out_ref[128:256, pl.ds(spot, HALF)] = low


def make_table(where, geo):
    return local(
        table_kernel, "phase_table", [((256, WIDTH), BF16), ((NB, 8, COLS), F32)], [where], [geo], 8,
        placed=1, scratch=[pltpu.SemaphoreType.DMA((NB,))],
    )


def column(part, block, who):
    return pl.ds(pl.multiple_of((part * 16 + block * G + who) * COLS, COLS), COLS)


def pieces_of(source, out, who, sems, base):
    return [
        pltpu.make_async_copy(
            source.at[:, column(part, block, who)],
            out.at[:, pl.ds((block * 2 + part) * COLS, COLS)],
            sems.at[base + block * 2 + part],
        )
        for block in range(NB) for part in range(2)
    ]


def own_kernel(where_ref, source, out, sems):
    copies = pieces_of(source, out, where_ref[0], sems, 0)
    for copy in copies:
        copy.start()
    for copy in copies:
        copy.wait()


def own_columns(where, refs):
    (own,) = local(
        own_kernel, "own_references", [((16, WIDTH), BF16)], [where], [refs], 4,
        placed=1, scratch=[pltpu.SemaphoreType.DMA((2 * NB,))],
    )
    return own


def parts_of(values):
    high = values.astype(BF16)
    rest = values - high.astype(F32)
    middle = rest.astype(BF16)
    return high, middle, (rest - middle.astype(F32)).astype(BF16)


def turned_over(values):
    rows, columns = values.shape
    same = lax.broadcasted_iota(jnp.int32, (columns, columns), 0) == lax.broadcasted_iota(
        jnp.int32, (columns, columns), 1
    )
    return sum(
        lax.dot_general(same.astype(BF16), part, NT, preferred_element_type=F32)
        for part in parts_of(values)
    )


def split_kernel(where_ref, source, ids, wedge, focus, sigma, after, *refs):
    outs, (ids_in, wedge_in, focus_in, sigma_in, sems, more) = refs[:G], refs[G:]
    copies = []
    for n in (2, 1, 3, 0):
        copies += pieces_of(source, outs[n], where_ref[0] ^ n, sems, n * 2 * NB)
    settings = [
        pltpu.make_async_copy(at, to, more.at[n])
        for n, (at, to) in enumerate(
            ((ids, ids_in), (wedge, wedge_in), (focus, focus_in), (sigma, sigma_in))
        )
    ]
    for copy in copies + settings:
        copy.start()
    for copy in settings:
        copy.wait()
    first = jnp.concatenate(
        [ids_in[...].astype(F32), jnp.broadcast_to(sigma_in[...], (8, P_DEV))], axis=0
    )
    info = jnp.concatenate(
        [
            turned_over(first),
            wedge_in[...].astype(F32),
            focus_in[...],
            jnp.zeros((P_DEV, 128 - 16 - 2 * TILTS), F32),
        ],
        axis=1,
    )
    for spot, piece in enumerate(parts_of(info)):
        for out in outs:
            out[:, WIDTH + spot * 128 : WIDTH + (spot + 1) * 128] = piece
    for copy in copies:
        copy.wait()


def split_particles(where, after, particles, shift_ids, wedge, defocus, inv_sigma):
    return local(
        split_kernel, "split_particles", [((P_DEV, WIDTH + EXTRA), BF16)] * G, [where],
        [particles, shift_ids.T, wedge, defocus, inv_sigma[None], after], 4, placed=5,
        scratch=[
            pltpu.VMEM((SHIFTS, P_DEV), jnp.int32),
            pltpu.VMEM((P_DEV, TILTS), jnp.int32),
            pltpu.VMEM((P_DEV, TILTS), F32),
            pltpu.VMEM((1, P_DEV), F32),
            pltpu.SemaphoreType.DMA((G * 2 * NB,)),
            pltpu.SemaphoreType.DMA((4,)),
        ],
    )


def rows_kernel(where_ref, x_ref, geo_ref, table_ref, rows_ref, pen_ref):
    info = sum(x_ref[:, WIDTH + n * 128 : WIDTH + (n + 1) * 128].astype(F32) for n in range(3))
    lane = lax.broadcasted_iota(jnp.int32, (ROWS, 256), 1) & 127
    ids = jnp.concatenate([info[:, s : s + 1] for s in range(SHIFTS)], axis=0)
    pick = (ids == lane.astype(F32)).astype(BF16)
    sigma = info[:, SHIFTS : SHIFTS + 1]
    small = lax.broadcasted_iota(jnp.int32, (P_DEV, 128), 1)

    @pl.loop(0, NB)
    def _(block):
        first = 2 * (block * G + where_ref[0]) + 16
        start = pl.multiple_of(block * 2 * COLS, 2 * COLS)
        for tilt in range(2):
            kept = jnp.sum(jnp.where(small == first + tilt, info, 0.0), axis=1, keepdims=True)
            focus = jnp.sum(jnp.where(small == first + tilt + TILTS, info, 0.0), axis=1, keepdims=True)
            shell = geo_ref[block, 3:4, tilt * HALF : (tilt + 1) * HALF]
            transfer = -sine_turns((4.0 * focus * shell + 0.1) * (0.5 / math.pi))
            weight = kept * transfer * sigma
            spot = pl.multiple_of(block * COLS + tilt * HALF, HALF)
            pen_ref[:, pl.ds(spot, HALF)] = (0.5 * weight * transfer).astype(BF16)
            lower, upper = pl.ds(start + tilt * HALF, HALF), pl.ds(start + COLS + tilt * HALF, HALF)
            real = (weight * x_ref[:, lower].astype(F32))[None]
            imag = (weight * x_ref[:, upper].astype(F32))[None]
            turned = jnp.dot(
                pick, table_ref[:, pl.ds(start + tilt * COLS, COLS)], preferred_element_type=F32
            ).reshape(SHIFTS, P_DEV, COLS)
            cosine, sine = turned[:, :, :HALF], turned[:, :, HALF:]
            rows_ref[:, lower] = (real * cosine + imag * sine).reshape(ROWS, HALF).astype(BF16)
            rows_ref[:, upper] = (imag * cosine - real * sine).reshape(ROWS, HALF).astype(BF16)


def make_rows(where, x, geo, table):
    return local(
        rows_kernel, "shifted_rows", [((ROWS, WIDTH), BF16), ((P_DEV, NB * COLS), BF16)], [where],
        [x, geo, table], 12,
    )


def scores_kernel(count, *refs):
    blocks = refs[2 * count : 2 * count + 8]
    outs = refs[2 * count + 8 :]
    stacked = jnp.concatenate([block[...] for block in blocks], axis=0)
    power = []
    for block in range(NB):
        start = block * 2 * COLS
        real = stacked[:, start : start + COLS].astype(F32)
        imag = stacked[:, start + COLS : start + 2 * COLS].astype(F32)
        power.append((real * real + imag * imag).astype(BF16))
    power = jnp.concatenate(power, axis=1)
    pens = jnp.concatenate([pen[...] for pen in refs[count : 2 * count]], axis=0)
    rows = jnp.concatenate([row[...] for row in refs[:count]], axis=0)
    energy = lax.dot_general(pens, power, NT, preferred_element_type=F32)
    total = lax.dot_general(rows, stacked, NT, preferred_element_type=F32)
    for n, out in enumerate(outs):
        mine = total[n * ROWS : (n + 1) * ROWS].reshape(SHIFTS, P_DEV, 128)
        out[...] = (mine - energy[None, n * P_DEV : (n + 1) * P_DEV]).reshape(ROWS, 128)


def make_scores(rows, pens, blocks):
    count = len(rows)
    return local(
        lambda *refs: scores_kernel(count, *refs), "partial_scores", [((ROWS, 128), F32)] * count, [],
        [*rows, *pens, *blocks], 12,
    )


def posterior_kernel(*refs):
    out = refs[-1]
    total = refs[0][...]
    for other in refs[1:-1]:
        total = total + other[...]
    total = total.reshape(SHIFTS, P_DEV, 128)
    peak = jnp.max(jnp.max(total, axis=0), axis=1, keepdims=True)
    expo = jnp.exp(total - peak[None])
    norm = jnp.sum(jnp.sum(expo, axis=0), axis=1, keepdims=True)
    share = (expo / norm[None]).reshape(ROWS, 128)
    out[...] = share.T.astype(BF16)


def make_posterior(parts):
    (out,) = local(posterior_kernel, "posterior", [((128, ROWS), BF16)], [], parts, 4)
    return out


def accum_kernel(part, where_ref, *refs):
    rows, posts, outs = refs[:G], refs[G : 2 * G], refs[2 * G :]

    @pl.loop(0, NB)
    def _(block):
        sums = []
        for half in range(2):
            start = pl.multiple_of(block * 2 * COLS + half * COLS + part * HALF, HALF)
            total = jnp.dot(posts[0][...], rows[0][:, pl.ds(start, HALF)], preferred_element_type=F32)
            for n in range(1, G):
                total = total + jnp.dot(
                    posts[n][...], rows[n][:, pl.ds(start, HALF)], preferred_element_type=F32
                )
            sums.append(total)
        if part == 0:
            for n in range(Y):
                for half, total in enumerate(sums):
                    spot = pl.multiple_of(block * COLS + half * HALF, HALF)
                    outs[n][:, pl.ds(spot, HALF)] = total[n * 32 : (n + 1) * 32].astype(BF16)
        else:
            for n in range(X):
                low = n & 1
                upper = ((where_ref[2] + n) & (X - 1)) >= 2
                spot = pl.multiple_of(block * HALF, HALF)
                for k in range(Y):
                    mine = slice(k * 32 + low * 16, k * 32 + low * 16 + 16)
                    chosen = jnp.where(upper, sums[1][mine], sums[0][mine])
                    outs[n][k * 16 : (k + 1) * 16, pl.ds(spot, HALF)] = chosen.astype(BF16)


def make_accum(part, where, rows, posts):
    shape = (32, NB * COLS) if part == 0 else (64, NB * HALF)
    return local(
        lambda *refs: accum_kernel(part, *refs), "weighted_sums", [(shape, BF16)] * 4, [where],
        [*rows, *posts], 8,
    )


def added(values):
    total = values[0].astype(F32)
    for value in values[1:]:
        total = total + value.astype(F32)
    return total


PIECES = [((16, NB * HALF), F32)] + [((16, NB * HALF), BF16)] * 3


def first_kernel(where_ref, *refs):
    outs = refs[4:]
    for block in range(NB):
        start = block * COLS
        real = added([ref[:, start : start + HALF] for ref in refs[:4]])
        imag = added([ref[:, start + HALF : start + COLS] for ref in refs[:4]])
        for n, out in enumerate(outs):
            mine = slice((n & 1) * 16, (n & 1) * 16 + 16)
            chosen = jnp.where(((where_ref[2] + n) & (X - 1)) >= 2, imag[mine], real[mine])
            out[:, block * HALF : (block + 1) * HALF] = chosen.astype(out.dtype)


def second_kernel(*refs):
    for n, out in enumerate(refs[4:]):
        out[...] = added([ref[n * 16 : (n + 1) * 16] for ref in refs[:4]]).astype(out.dtype)


def joined_kernel(where_ref, *refs):
    for n, out in enumerate(refs[8:]):
        spot = pl.ds(pl.multiple_of(((where_ref[1] + n) % NB) * HALF, HALF), HALF)
        out[:, :HALF] = added([ref[:, spot] for ref in refs[:4]]).astype(out.dtype)
        out[:, HALF:] = added([ref[:, spot] for ref in refs[4:8]]).astype(out.dtype)


def after(value, *others):
    return lax.optimization_barrier((value, *others))[0]


def per_device(refs, particles, shift_ids, wedge, defocus, inv_sigma):
    dom = lax.axis_index("dom")
    x_at = (dom // 16) * 2 + lax.axis_index("blk") % 2
    where = jnp.stack([dom % G, (dom % 16) // G, x_at]).astype(jnp.int32)
    geo = jnp.asarray(geometry())

    gathered = {}
    own = own_columns(where, refs)
    gathered[0, 0] = own
    gathered[1, 0] = send(own, moves(dy=-1))
    gathered[3, 0] = send(own, moves(dy=1))
    chunks = split_particles(where, own, particles, shift_ids, wedge, defocus, inv_sigma)
    got = {0: chunks[0]}
    got[2] = send(chunks[2], partners(2))
    got[1] = send(chunks[1], partners(1))
    gathered[2, 0] = send(own, moves(dy=2))
    table, geo = make_table(where, geo)
    wave = [got[1], got[2], gathered[1, 0], gathered[3, 0], table]
    gathered[0, 1] = send(after(own, *wave), moves(dx=-1))
    gathered[1, 1] = send(after(gathered[1, 0], *wave), moves(dx=-1))
    gathered[3, 1] = send(after(gathered[3, 0], *wave), moves(dx=1))
    got[3] = send(after(chunks[3], *wave), partners(3))
    rows, pens = {}, {}
    rows[0], pens[0] = make_rows(where, after(got[0], *wave), geo, table)
    gathered[2, 1] = send(after(gathered[2, 0], rows[0]), moves(dx=1))
    rows[1], pens[1] = make_rows(where, after(got[1], rows[0], gathered[2, 0]), geo, table)
    rows[2], pens[2] = make_rows(where, after(got[2], rows[1]), geo, table)
    rows[3], pens[3] = make_rows(where, after(got[3], rows[2]), geo, table)
    blocks = [gathered[ky, kx] for ky in range(Y) for kx in range(2)]

    rows = [rows[n] for n in range(G)]
    pens = [pens[n] for n in range(G)]
    parts = make_scores(rows, pens, blocks)
    arrived = [send(parts[n], partners(n)) for n in range(1, G)]
    posterior = make_posterior([parts[0], *arrived])
    posts = [posterior] + [send(posterior, partners(n)) for n in range(1, G)]

    first = make_accum(0, where, rows, posts)
    first = [first[0]] + [send(first[n], moves(dy=n)) for n in range(1, Y)]
    second = make_accum(1, where, rows, posts)
    second = [
        second[0],
        send(second[1], moves(dx=1)),
        send(after(second[2], first[1]), moves(dx=2)),
        send(second[3], moves(dx=3)),
    ]
    first = local(first_kernel, "first_sums", PIECES, [where], first, 4)
    first = [first[0]] + [send(first[n], moves(dx=n)) for n in range(1, X)]
    second = local(second_kernel, "second_sums", PIECES, [], second, 4)
    second = [second[0]] + [send(second[n], moves(dy=n)) for n in range(1, Y)]
    outs = [((16, COLS), F32)] + [((16, COLS), BF16)] * (NB - 1)
    ends = local(joined_kernel, "joined_sums", outs, [where], [*first, *second], 4)
    return added([ends[0]] + [send(ends[n], moves(dz=n * (G // 2))) for n in range(1, NB)])


def solution(mesh):
    return jax.shard_map(
        per_device,
        mesh=mesh,
        in_specs=(
            P("blk", None),
            P(("blk", "dom"), None),
            P(("blk", "dom"), None),
            P(("blk", "dom"), None),
            P(("blk", "dom"), None),
            P(("blk", "dom")),
        ),
        out_specs=P("blk", "dom"),
        check_vma=False,
    )
```

```python
import math

import jax
import jax.numpy as jnp
import numpy as np
from jax import lax
from jax.experimental import pallas as pl
from jax.experimental.pallas import tpu as pltpu
from jax.sharding import PartitionSpec as P

BOX = 32
TILTS = 32
SHIFTS = 8
P_DEV = 32
Y, X, Z = 4, 4, 8
COLS = 1024
HALF = 512
G = 4
NB = 16 // G
ROWS = P_DEV * SHIFTS
WIDTH = NB * 2 * COLS
EXTRA = 384
AXES = ("blk", "dom")
F32, BF16 = jnp.float32, jnp.bfloat16
NT = (((1,), (1,)), ((), ()))
MIB = 1 << 20


def linear(y, x, z, core):
    y, x, z = y % Y, x % X, z % Z
    return (y * 2 + x % 2) * 32 + (x // 2) * 16 + z * 2 + core


def moves(dy=0, dx=0, dz=0):
    return [
        (linear(y, x, z, c), linear(y + dy, x + dx, z + dz, c))
        for y in range(Y) for x in range(X) for z in range(Z) for c in range(2)
    ]


def partners(k):
    return [
        (linear(y, x, z, c), linear(y, x, z ^ (k >> 1), c ^ (k & 1)))
        for y in range(Y) for x in range(X) for z in range(Z) for c in range(2)
    ]


def send(value, pairs):
    return lax.ppermute(value, AXES, pairs)


def geometry():
    position = np.arange(TILTS * HALF)
    tilt, within = position // HALF, position % HALF
    radial = (within // BOX).astype(np.float64)
    lateral = (within % BOX - BOX // 2).astype(np.float64)
    angle = (tilt - 0.5 * (TILTS - 1)) * (2.0 / TILTS)
    shell = (radial * radial + lateral * lateral) / (0.25 * BOX * BOX)
    zero = np.zeros_like(shell)
    table = np.stack([radial * np.cos(angle), lateral, radial * np.sin(angle), shell] + [zero] * 4)
    return table.reshape(8, 16, COLS).transpose(1, 0, 2).astype(np.float32)


def fold(turns):
    turns = turns - jnp.floor(turns + 0.5)
    far = jnp.abs(turns) > 0.25
    near = jnp.where(far, jnp.where(turns > 0, 0.5, -0.5) - turns, turns)
    return near * (2.0 * math.pi), far


def series(square, terms):
    total = jnp.full_like(square, terms[-1])
    for term in terms[-2::-1]:
        total = total * square + term
    return total


SIN_TERMS = [(-1) ** n / math.factorial(2 * n + 1) for n in range(6)]
COS_TERMS = [(-1) ** n / math.factorial(2 * n) for n in range(7)]


def sine_turns(turns):
    angle, _ = fold(turns)
    return angle * series(angle * angle, SIN_TERMS)


def held(value):
    return pltpu.with_memory_space_constraint(value, pltpu.VMEM)


SCALARS = pl.BlockSpec(memory_space=pltpu.SMEM)
WHOLE = pl.BlockSpec(memory_space=pltpu.VMEM)
PLACED = pl.BlockSpec(memory_space=pl.ANY)


def local(kernel, name, outs, scalars, arrays, limit, placed=0, scratch=()):
    return pl.pallas_call(
        kernel,
        in_specs=[SCALARS] * len(scalars) + [PLACED] * placed + [WHOLE] * (len(arrays) - placed),
        out_specs=[WHOLE] * len(outs),
        out_shape=[pltpu.VMEM(shape, kind) for shape, kind in outs],
        scratch_shapes=list(scratch),
        cost_estimate=pl.CostEstimate(flops=0, bytes_accessed=0, transcendentals=0),
        compiler_params=pltpu.CompilerParams(vmem_limit_bytes=limit * MIB),
        name=name,
    )(
        *scalars,
        *[pltpu.with_memory_space_constraint(value, pltpu.HBM) for value in arrays[:placed]],
        *[held(value) for value in arrays[placed:]],
    )


def table_kernel(member_ref, geo_ref, out_ref, picked_ref, sems):
    copies = [
        pltpu.make_async_copy(geo_ref.at[block * G + member_ref[0]], picked_ref.at[block], sems.at[block])
        for block in range(NB)
    ]
    for copy in copies:
        copy.start()
    ids = lax.broadcasted_iota(jnp.int32, (128, 1), 0).astype(F32)
    high = jnp.floor((ids + 0.5) * (1 / 25))
    middle = jnp.floor((ids - 25 * high + 0.5) * (1 / 5))
    low = ids - 25 * high - 5 * middle
    move_x, move_y, move_z = ((digit - 2.0) * (0.5 / BOX) for digit in (high, middle, low))
    for copy in copies:
        copy.wait()

    @pl.loop(0, NB)
    def _(block):
        geo = picked_ref[block]
        for tilt in range(2):
            part = geo[:, tilt * HALF : (tilt + 1) * HALF]
            turns = move_x * part[0:1] + move_y * part[1:2] + move_z * part[2:3]
            angle, far = fold(turns)
            square = angle * angle
            sine = angle * series(square, SIN_TERMS)
            cosine = series(square, COS_TERMS)
            cosine = jnp.where(far, -cosine, cosine)
            for at, values in enumerate((cosine, sine)):
                high = values.astype(BF16)
                low = (values - high.astype(F32)).astype(BF16)
                spot = pl.multiple_of(block * 2 * COLS + tilt * COLS + at * HALF, HALF)
                out_ref[0:128, pl.ds(spot, HALF)] = high
                out_ref[128:256, pl.ds(spot, HALF)] = low


def make_table(member, geo):
    return local(
        table_kernel, "phase_table", [((256, WIDTH), BF16), ((NB, 8, COLS), F32)], [member], [geo], 8,
        placed=1, scratch=[pltpu.SemaphoreType.DMA((NB,))],
    )


def column(part, block, who):
    return pl.ds(pl.multiple_of((part * 16 + block * G + who) * COLS, COLS), COLS)


def pieces_of(source, out, who, sems, base):
    return [
        pltpu.make_async_copy(
            source.at[:, column(part, block, who)],
            out.at[:, pl.ds((block * 2 + part) * COLS, COLS)],
            sems.at[base + block * 2 + part],
        )
        for block in range(NB) for part in range(2)
    ]


def own_kernel(member_ref, source, after, out, sems):
    copies = pieces_of(source, out, member_ref[0], sems, 0)
    for copy in copies:
        copy.start()
    for copy in copies:
        copy.wait()


def own_columns(member, refs, after):
    (own,) = local(
        own_kernel, "own_references", [((16, WIDTH), BF16)], [member], [refs, after], 4,
        placed=1, scratch=[pltpu.SemaphoreType.DMA((2 * NB,))],
    )
    return own


def parts_of(values):
    high = values.astype(BF16)
    rest = values - high.astype(F32)
    middle = rest.astype(BF16)
    return high, middle, (rest - middle.astype(F32)).astype(BF16)


def turned_over(values):
    rows, columns = values.shape
    same = lax.broadcasted_iota(jnp.int32, (columns, columns), 0) == lax.broadcasted_iota(
        jnp.int32, (columns, columns), 1
    )
    return sum(
        lax.dot_general(same.astype(BF16), part, NT, preferred_element_type=F32)
        for part in parts_of(values)
    )


def split_kernel(member_ref, block_ref, x_ref, source, ids, wedge, focus, sigma, *refs):
    outs, (ids_in, wedge_in, focus_in, sigma_in, sems, more) = refs[:G], refs[G:]
    copies = []
    for n in (2, 1, 3, 0):
        copies += pieces_of(source, outs[n], member_ref[0] ^ n, sems, n * 2 * NB)
    settings = [
        pltpu.make_async_copy(at, to, more.at[n])
        for n, (at, to) in enumerate(
            ((ids, ids_in), (wedge, wedge_in), (focus, focus_in), (sigma, sigma_in))
        )
    ]
    for copy in copies + settings:
        copy.start()
    for copy in settings:
        copy.wait()
    first = jnp.concatenate(
        [ids_in[...].astype(F32), jnp.broadcast_to(sigma_in[...], (8, P_DEV))], axis=0
    )
    info = jnp.concatenate(
        [
            turned_over(first),
            wedge_in[...].astype(F32),
            focus_in[...],
            jnp.zeros((P_DEV, 128 - 16 - 2 * TILTS), F32),
        ],
        axis=1,
    )
    for spot, piece in enumerate(parts_of(info)):
        for out in outs:
            out[:, WIDTH + spot * 128 : WIDTH + (spot + 1) * 128] = piece
    for copy in copies:
        copy.wait()


def split_particles(place, particles, shift_ids, wedge, defocus, inv_sigma):
    return local(
        split_kernel, "split_particles", [((P_DEV, WIDTH + EXTRA), BF16)] * G, place,
        [particles, shift_ids.T, wedge, defocus, inv_sigma[None]], 4, placed=5,
        scratch=[
            pltpu.VMEM((SHIFTS, P_DEV), jnp.int32),
            pltpu.VMEM((P_DEV, TILTS), jnp.int32),
            pltpu.VMEM((P_DEV, TILTS), F32),
            pltpu.VMEM((1, P_DEV), F32),
            pltpu.SemaphoreType.DMA((G * 2 * NB,)),
            pltpu.SemaphoreType.DMA((4,)),
        ],
    )


def rows_kernel(member_ref, x_ref, geo_ref, table_ref, rows_ref, pen_ref):
    info = sum(x_ref[:, WIDTH + n * 128 : WIDTH + (n + 1) * 128].astype(F32) for n in range(3))
    lane = lax.broadcasted_iota(jnp.int32, (ROWS, 256), 1) & 127
    ids = jnp.concatenate([info[:, s : s + 1] for s in range(SHIFTS)], axis=0)
    pick = (ids == lane.astype(F32)).astype(BF16)
    sigma = info[:, SHIFTS : SHIFTS + 1]
    small = lax.broadcasted_iota(jnp.int32, (P_DEV, 128), 1)

    @pl.loop(0, NB)
    def _(block):
        first = 2 * (block * G + member_ref[0]) + 16
        start = pl.multiple_of(block * 2 * COLS, 2 * COLS)
        for tilt in range(2):
            kept = jnp.sum(jnp.where(small == first + tilt, info, 0.0), axis=1, keepdims=True)
            focus = jnp.sum(jnp.where(small == first + tilt + TILTS, info, 0.0), axis=1, keepdims=True)
            shell = geo_ref[block, 3:4, tilt * HALF : (tilt + 1) * HALF]
            transfer = -sine_turns((4.0 * focus * shell + 0.1) * (0.5 / math.pi))
            weight = kept * transfer * sigma
            spot = pl.multiple_of(block * COLS + tilt * HALF, HALF)
            pen_ref[:, pl.ds(spot, HALF)] = (0.5 * weight * transfer).astype(BF16)
            lower, upper = pl.ds(start + tilt * HALF, HALF), pl.ds(start + COLS + tilt * HALF, HALF)
            real = (weight * x_ref[:, lower].astype(F32))[None]
            imag = (weight * x_ref[:, upper].astype(F32))[None]
            turned = jnp.dot(
                pick, table_ref[:, pl.ds(start + tilt * COLS, COLS)], preferred_element_type=F32
            ).reshape(SHIFTS, P_DEV, COLS)
            cosine, sine = turned[:, :, :HALF], turned[:, :, HALF:]
            rows_ref[:, lower] = (real * cosine + imag * sine).reshape(ROWS, HALF).astype(BF16)
            rows_ref[:, upper] = (imag * cosine - real * sine).reshape(ROWS, HALF).astype(BF16)


def make_rows(member, x, geo, table):
    return local(
        rows_kernel, "shifted_rows", [((ROWS, WIDTH), BF16), ((P_DEV, NB * COLS), BF16)], [member],
        [x, geo, table], 12,
    )


def scores_kernel(count, *refs):
    blocks = refs[2 * count : 2 * count + 8]
    outs = refs[2 * count + 8 :]
    stacked = jnp.concatenate([block[...] for block in blocks], axis=0)
    power = []
    for block in range(NB):
        start = block * 2 * COLS
        real = stacked[:, start : start + COLS].astype(F32)
        imag = stacked[:, start + COLS : start + 2 * COLS].astype(F32)
        power.append((real * real + imag * imag).astype(BF16))
    power = jnp.concatenate(power, axis=1)
    pens = jnp.concatenate([pen[...] for pen in refs[count : 2 * count]], axis=0)
    rows = jnp.concatenate([row[...] for row in refs[:count]], axis=0)
    energy = lax.dot_general(pens, power, NT, preferred_element_type=F32)
    total = lax.dot_general(rows, stacked, NT, preferred_element_type=F32)
    for n, out in enumerate(outs):
        mine = total[n * ROWS : (n + 1) * ROWS].reshape(SHIFTS, P_DEV, 128)
        out[...] = (mine - energy[None, n * P_DEV : (n + 1) * P_DEV]).reshape(ROWS, 128)


def make_scores(rows, pens, blocks):
    count = len(rows)
    return local(
        lambda *refs: scores_kernel(count, *refs), "partial_scores", [((ROWS, 128), F32)] * count, [],
        [*rows, *pens, *blocks], 12,
    )


def posterior_kernel(*refs):
    out = refs[-1]
    total = refs[0][...]
    for other in refs[1:-1]:
        total = total + other[...]
    total = total.reshape(SHIFTS, P_DEV, 128)
    peak = jnp.max(jnp.max(total, axis=0), axis=1, keepdims=True)
    expo = jnp.exp(total - peak[None])
    norm = jnp.sum(jnp.sum(expo, axis=0), axis=1, keepdims=True)
    share = (expo / norm[None]).reshape(ROWS, 128)
    out[...] = share.T.astype(BF16)


def make_posterior(parts):
    (out,) = local(posterior_kernel, "posterior", [((128, ROWS), BF16)], [], parts, 4)
    return out


def accum_kernel(part, x_ref, *refs):
    rows, posts, outs = refs[:G], refs[G : 2 * G], refs[2 * G :]

    @pl.loop(0, NB)
    def _(block):
        sums = []
        for half in range(2):
            start = pl.multiple_of(block * 2 * COLS + half * COLS + part * HALF, HALF)
            total = jnp.dot(posts[0][...], rows[0][:, pl.ds(start, HALF)], preferred_element_type=F32)
            for n in range(1, G):
                total = total + jnp.dot(
                    posts[n][...], rows[n][:, pl.ds(start, HALF)], preferred_element_type=F32
                )
            sums.append(total)
        if part == 0:
            for n in range(Y):
                for half, total in enumerate(sums):
                    spot = pl.multiple_of(block * COLS + half * HALF, HALF)
                    outs[n][:, pl.ds(spot, HALF)] = total[n * 32 : (n + 1) * 32].astype(BF16)
        else:
            for n in range(X):
                low = n & 1
                upper = ((x_ref[0] + n) & (X - 1)) >= 2
                spot = pl.multiple_of(block * HALF, HALF)
                for k in range(Y):
                    mine = slice(k * 32 + low * 16, k * 32 + low * 16 + 16)
                    chosen = jnp.where(upper, sums[1][mine], sums[0][mine])
                    outs[n][k * 16 : (k + 1) * 16, pl.ds(spot, HALF)] = chosen.astype(BF16)


def make_accum(part, place, rows, posts):
    shape = (32, NB * COLS) if part == 0 else (64, NB * HALF)
    return local(
        lambda *refs: accum_kernel(part, *refs), "weighted_sums", [(shape, BF16)] * 4, [place],
        [*rows, *posts], 8,
    )


def added(values):
    total = values[0].astype(F32)
    for value in values[1:]:
        total = total + value.astype(F32)
    return total


PIECES = [((16, NB * HALF), F32)] + [((16, NB * HALF), BF16)] * 3


def first_kernel(x_ref, *refs):
    outs = refs[4:]
    for block in range(NB):
        start = block * COLS
        real = added([ref[:, start : start + HALF] for ref in refs[:4]])
        imag = added([ref[:, start + HALF : start + COLS] for ref in refs[:4]])
        for n, out in enumerate(outs):
            mine = slice((n & 1) * 16, (n & 1) * 16 + 16)
            chosen = jnp.where(((x_ref[0] + n) & (X - 1)) >= 2, imag[mine], real[mine])
            out[:, block * HALF : (block + 1) * HALF] = chosen.astype(out.dtype)


def second_kernel(*refs):
    for n, out in enumerate(refs[4:]):
        out[...] = added([ref[n * 16 : (n + 1) * 16] for ref in refs[:4]]).astype(out.dtype)


def joined_kernel(block_ref, *refs):
    for n, out in enumerate(refs[8:]):
        spot = pl.ds(pl.multiple_of(((block_ref[0] + n) % NB) * HALF, HALF), HALF)
        out[:, :HALF] = added([ref[:, spot] for ref in refs[:4]]).astype(out.dtype)
        out[:, HALF:] = added([ref[:, spot] for ref in refs[4:8]]).astype(out.dtype)


def after(value, *others):
    return lax.optimization_barrier((value, *others))[0]


def per_device(refs, particles, shift_ids, wedge, defocus, inv_sigma):
    dom = lax.axis_index("dom")
    x_at = (dom // 16) * 2 + lax.axis_index("blk") % 2
    place = [value.astype(jnp.int32).reshape(1) for value in (dom % G, (dom % 16) // G, x_at)]
    member, block, x_at = place
    geo = jnp.asarray(geometry())

    chunks = split_particles(place, particles, shift_ids, wedge, defocus, inv_sigma)
    got, gathered, rows, pens = {}, {}, {}, {}
    got[2] = send(chunks[2], partners(2))
    got[1] = send(chunks[1], partners(1))
    own = own_columns(member, refs, chunks[2])
    gathered[0, 0] = own
    gathered[1, 0] = send(own, moves(dy=-1))
    gathered[3, 0] = send(own, moves(dy=1))
    gathered[2, 0] = send(own, moves(dy=2))
    table, geo = make_table(member, geo)
    rows[0], pens[0] = make_rows(member, chunks[0], geo, table)
    wave = [got[1], got[2], gathered[1, 0], gathered[3, 0], gathered[2, 0], rows[0]]
    got[3] = send(after(chunks[3], *wave), partners(3))
    gathered[0, 1] = send(after(own, *wave), moves(dx=-1))
    gathered[1, 1] = send(after(gathered[1, 0], *wave), moves(dx=-1))
    gathered[3, 1] = send(after(gathered[3, 0], *wave), moves(dx=1))
    gathered[2, 1] = send(after(gathered[2, 0], *wave), moves(dx=1))
    rows[1], pens[1] = make_rows(member, after(got[1], *wave), geo, table)
    rows[2], pens[2] = make_rows(member, after(got[2], rows[1]), geo, table)
    rows[3], pens[3] = make_rows(member, after(got[3], rows[2]), geo, table)
    blocks = [gathered[ky, kx] for ky in range(Y) for kx in range(2)]

    (second,) = make_scores([rows[2]], [pens[2]], blocks)
    third, other = make_scores([rows[3], rows[1]], [after(pens[3], second), pens[1]], blocks)
    (mine,) = make_scores([rows[0]], [after(pens[0], third)], blocks)
    arrived = [send(value, partners(n)) for value, n in ((second, 2), (third, 3), (other, 1))]
    posterior = make_posterior([mine, *arrived])
    posts = [posterior] + [send(posterior, partners(n)) for n in range(1, G)]
    rows = [rows[n] for n in range(G)]

    first = make_accum(0, x_at, rows, posts)
    first = [first[0]] + [send(first[n], moves(dy=n)) for n in range(1, Y)]
    second = make_accum(1, x_at, rows, posts)
    second = [
        second[0],
        send(second[1], moves(dx=1)),
        send(after(second[2], first[1]), moves(dx=2)),
        send(second[3], moves(dx=3)),
    ]
    first = local(first_kernel, "first_sums", PIECES, [x_at], first, 4)
    first = [first[0]] + [send(first[n], moves(dx=n)) for n in range(1, X)]
    second = local(second_kernel, "second_sums", PIECES, [], second, 4)
    second = [second[0]] + [send(second[n], moves(dy=n)) for n in range(1, Y)]
    outs = [((16, COLS), F32)] + [((16, COLS), BF16)] * (NB - 1)
    ends = local(joined_kernel, "joined_sums", outs, [block], [*first, *second], 4)
    return added([ends[0]] + [send(ends[n], moves(dz=n * (G // 2))) for n in range(1, NB)])


def solution(mesh):
    return jax.shard_map(
        per_device,
        mesh=mesh,
        in_specs=(
            P("blk", None),
            P(("blk", "dom"), None),
            P(("blk", "dom"), None),
            P(("blk", "dom"), None),
            P(("blk", "dom"), None),
            P(("blk", "dom")),
        ),
        out_specs=P("blk", "dom"),
        check_vma=False,
    )
```

```python
import math

import jax
import jax.numpy as jnp
import numpy as np
from jax import lax
from jax.experimental import pallas as pl
from jax.experimental.pallas import tpu as pltpu
from jax.sharding import PartitionSpec as P

BOX = 32
TILTS = 32
SHIFTS = 8
P_DEV = 32
Y, X, Z = 4, 4, 8
COLS = 1024
HALF = 512
G = 4
NB = 16 // G
ROWS = P_DEV * SHIFTS
WIDTH = NB * 2 * COLS
EXTRA = 384
AXES = ("blk", "dom")
F32, BF16 = jnp.float32, jnp.bfloat16
NT = (((1,), (1,)), ((), ()))
MIB = 1 << 20


def linear(y, x, z, core):
    y, x, z = y % Y, x % X, z % Z
    return (y * 2 + x % 2) * 32 + (x // 2) * 16 + z * 2 + core


def moves(dy=0, dx=0, dz=0):
    return [
        (linear(y, x, z, c), linear(y + dy, x + dx, z + dz, c))
        for y in range(Y) for x in range(X) for z in range(Z) for c in range(2)
    ]


def partners(k):
    return [
        (linear(y, x, z, c), linear(y, x, z ^ (k >> 1), c ^ (k & 1)))
        for y in range(Y) for x in range(X) for z in range(Z) for c in range(2)
    ]


def send(value, pairs):
    return lax.ppermute(value, AXES, pairs)


def geometry():
    position = np.arange(TILTS * HALF)
    tilt, within = position // HALF, position % HALF
    radial = (within // BOX).astype(np.float64)
    lateral = (within % BOX - BOX // 2).astype(np.float64)
    angle = (tilt - 0.5 * (TILTS - 1)) * (2.0 / TILTS)
    shell = (radial * radial + lateral * lateral) / (0.25 * BOX * BOX)
    zero = np.zeros_like(shell)
    table = np.stack([radial * np.cos(angle), lateral, radial * np.sin(angle), shell] + [zero] * 4)
    return table.reshape(8, 16, COLS).transpose(1, 0, 2).astype(np.float32)


def fold(turns):
    turns = turns - jnp.floor(turns + 0.5)
    far = jnp.abs(turns) > 0.25
    near = jnp.where(far, jnp.where(turns > 0, 0.5, -0.5) - turns, turns)
    return near * (2.0 * math.pi), far


def series(square, terms):
    total = jnp.full_like(square, terms[-1])
    for term in terms[-2::-1]:
        total = total * square + term
    return total


SIN_TERMS = [(-1) ** n / math.factorial(2 * n + 1) for n in range(6)]
COS_TERMS = [(-1) ** n / math.factorial(2 * n) for n in range(7)]


def sine_turns(turns):
    angle, _ = fold(turns)
    return angle * series(angle * angle, SIN_TERMS)


def held(value):
    return pltpu.with_memory_space_constraint(value, pltpu.VMEM)


SCALARS = pl.BlockSpec(memory_space=pltpu.SMEM)
WHOLE = pl.BlockSpec(memory_space=pltpu.VMEM)
PLACED = pl.BlockSpec(memory_space=pl.ANY)


def local(kernel, name, outs, scalars, arrays, limit, placed=0, scratch=()):
    return pl.pallas_call(
        kernel,
        in_specs=[SCALARS] * len(scalars) + [PLACED] * placed + [WHOLE] * (len(arrays) - placed),
        out_specs=[WHOLE] * len(outs),
        out_shape=[pltpu.VMEM(shape, kind) for shape, kind in outs],
        scratch_shapes=list(scratch),
        cost_estimate=pl.CostEstimate(flops=0, bytes_accessed=0, transcendentals=0),
        compiler_params=pltpu.CompilerParams(vmem_limit_bytes=limit * MIB),
        name=name,
    )(
        *scalars,
        *[pltpu.with_memory_space_constraint(value, pltpu.HBM) for value in arrays[:placed]],
        *[held(value) for value in arrays[placed:]],
    )


def table_kernel(member_ref, geo_ref, out_ref, picked_ref, sems):
    copies = [
        pltpu.make_async_copy(geo_ref.at[block * G + member_ref[0]], picked_ref.at[block], sems.at[block])
        for block in range(NB)
    ]
    for copy in copies:
        copy.start()
    ids = lax.broadcasted_iota(jnp.int32, (128, 1), 0).astype(F32)
    high = jnp.floor((ids + 0.5) * (1 / 25))
    middle = jnp.floor((ids - 25 * high + 0.5) * (1 / 5))
    low = ids - 25 * high - 5 * middle
    move_x, move_y, move_z = ((digit - 2.0) * (0.5 / BOX) for digit in (high, middle, low))
    for copy in copies:
        copy.wait()

    @pl.loop(0, NB)
    def _(block):
        geo = picked_ref[block]
        for tilt in range(2):
            part = geo[:, tilt * HALF : (tilt + 1) * HALF]
            turns = move_x * part[0:1] + move_y * part[1:2] + move_z * part[2:3]
            angle, far = fold(turns)
            square = angle * angle
            sine = angle * series(square, SIN_TERMS)
            cosine = series(square, COS_TERMS)
            cosine = jnp.where(far, -cosine, cosine)
            for at, values in enumerate((cosine, sine)):
                high = values.astype(BF16)
                low = (values - high.astype(F32)).astype(BF16)
                spot = pl.multiple_of(block * 2 * COLS + tilt * COLS + at * HALF, HALF)
                out_ref[0:128, pl.ds(spot, HALF)] = high
                out_ref[128:256, pl.ds(spot, HALF)] = low


def make_table(member, geo):
    return local(
        table_kernel, "phase_table", [((256, WIDTH), BF16), ((NB, 8, COLS), F32)], [member], [geo], 8,
        placed=1, scratch=[pltpu.SemaphoreType.DMA((NB,))],
    )


def column(part, block, who):
    return pl.ds(pl.multiple_of((part * 16 + block * G + who) * COLS, COLS), COLS)


def pieces_of(source, out, who, sems, base):
    return [
        pltpu.make_async_copy(
            source.at[:, column(part, block, who)],
            out.at[:, pl.ds((block * 2 + part) * COLS, COLS)],
            sems.at[base + block * 2 + part],
        )
        for block in range(NB) for part in range(2)
    ]


def own_kernel(member_ref, source, after, out, sems):
    copies = pieces_of(source, out, member_ref[0], sems, 0)
    for copy in copies:
        copy.start()
    for copy in copies:
        copy.wait()


def own_columns(member, refs, after):
    (own,) = local(
        own_kernel, "own_references", [((16, WIDTH), BF16)], [member], [refs, after], 4,
        placed=1, scratch=[pltpu.SemaphoreType.DMA((2 * NB,))],
    )
    return own


def parts_of(values):
    high = values.astype(BF16)
    rest = values - high.astype(F32)
    middle = rest.astype(BF16)
    return high, middle, (rest - middle.astype(F32)).astype(BF16)


def turned_over(values):
    rows, columns = values.shape
    same = lax.broadcasted_iota(jnp.int32, (columns, columns), 0) == lax.broadcasted_iota(
        jnp.int32, (columns, columns), 1
    )
    return sum(
        lax.dot_general(same.astype(BF16), part, NT, preferred_element_type=F32)
        for part in parts_of(values)
    )


def split_kernel(member_ref, block_ref, x_ref, source, ids, wedge, focus, sigma, *refs):
    outs, (ids_in, wedge_in, focus_in, sigma_in, sems, more) = refs[:G], refs[G:]
    copies = []
    for n in (2, 1, 3, 0):
        copies += pieces_of(source, outs[n], member_ref[0] ^ n, sems, n * 2 * NB)
    settings = [
        pltpu.make_async_copy(at, to, more.at[n])
        for n, (at, to) in enumerate(
            ((ids, ids_in), (wedge, wedge_in), (focus, focus_in), (sigma, sigma_in))
        )
    ]
    for copy in copies + settings:
        copy.start()
    for copy in settings:
        copy.wait()
    first = jnp.concatenate(
        [ids_in[...].astype(F32), jnp.broadcast_to(sigma_in[...], (8, P_DEV))], axis=0
    )
    info = jnp.concatenate(
        [
            turned_over(first),
            wedge_in[...].astype(F32),
            focus_in[...],
            jnp.zeros((P_DEV, 128 - 16 - 2 * TILTS), F32),
        ],
        axis=1,
    )
    for spot, piece in enumerate(parts_of(info)):
        for out in outs:
            out[:, WIDTH + spot * 128 : WIDTH + (spot + 1) * 128] = piece
    for copy in copies:
        copy.wait()


def split_particles(place, particles, shift_ids, wedge, defocus, inv_sigma):
    return local(
        split_kernel, "split_particles", [((P_DEV, WIDTH + EXTRA), BF16)] * G, place,
        [particles, shift_ids.T, wedge, defocus, inv_sigma[None]], 4, placed=5,
        scratch=[
            pltpu.VMEM((SHIFTS, P_DEV), jnp.int32),
            pltpu.VMEM((P_DEV, TILTS), jnp.int32),
            pltpu.VMEM((P_DEV, TILTS), F32),
            pltpu.VMEM((1, P_DEV), F32),
            pltpu.SemaphoreType.DMA((G * 2 * NB,)),
            pltpu.SemaphoreType.DMA((4,)),
        ],
    )


def rows_kernel(member_ref, x_ref, geo_ref, table_ref, rows_ref, pen_ref):
    info = sum(x_ref[:, WIDTH + n * 128 : WIDTH + (n + 1) * 128].astype(F32) for n in range(3))
    lane = lax.broadcasted_iota(jnp.int32, (ROWS, 256), 1) & 127
    ids = jnp.concatenate([info[:, s : s + 1] for s in range(SHIFTS)], axis=0)
    pick = (ids == lane.astype(F32)).astype(BF16)
    sigma = info[:, SHIFTS : SHIFTS + 1]
    small = lax.broadcasted_iota(jnp.int32, (P_DEV, 128), 1)

    @pl.loop(0, NB)
    def _(block):
        first = 2 * (block * G + member_ref[0]) + 16
        start = pl.multiple_of(block * 2 * COLS, 2 * COLS)
        for tilt in range(2):
            kept = jnp.sum(jnp.where(small == first + tilt, info, 0.0), axis=1, keepdims=True)
            focus = jnp.sum(jnp.where(small == first + tilt + TILTS, info, 0.0), axis=1, keepdims=True)
            shell = geo_ref[block, 3:4, tilt * HALF : (tilt + 1) * HALF]
            transfer = -sine_turns((4.0 * focus * shell + 0.1) * (0.5 / math.pi))
            weight = kept * transfer * sigma
            spot = pl.multiple_of(block * COLS + tilt * HALF, HALF)
            pen_ref[:, pl.ds(spot, HALF)] = (0.5 * weight * transfer).astype(BF16)
            lower, upper = pl.ds(start + tilt * HALF, HALF), pl.ds(start + COLS + tilt * HALF, HALF)
            real = (weight * x_ref[:, lower].astype(F32))[None]
            imag = (weight * x_ref[:, upper].astype(F32))[None]
            turned = jnp.dot(
                pick, table_ref[:, pl.ds(start + tilt * COLS, COLS)], preferred_element_type=F32
            ).reshape(SHIFTS, P_DEV, COLS)
            cosine, sine = turned[:, :, :HALF], turned[:, :, HALF:]
            rows_ref[:, lower] = (real * cosine + imag * sine).reshape(ROWS, HALF).astype(BF16)
            rows_ref[:, upper] = (imag * cosine - real * sine).reshape(ROWS, HALF).astype(BF16)


def make_rows(member, x, geo, table):
    return local(
        rows_kernel, "shifted_rows", [((ROWS, WIDTH), BF16), ((P_DEV, NB * COLS), BF16)], [member],
        [x, geo, table], 12,
    )


def scores_kernel(count, more, *refs):
    blocks = refs[2 * count : 2 * count + 8]
    added_in = refs[2 * count + 8 : 2 * count + 8 + more]
    outs = refs[2 * count + 8 + more :]
    stacked = jnp.concatenate([block[...] for block in blocks], axis=0)
    power = []
    for block in range(NB):
        start = block * 2 * COLS
        real = stacked[:, start : start + COLS].astype(F32)
        imag = stacked[:, start + COLS : start + 2 * COLS].astype(F32)
        power.append((real * real + imag * imag).astype(BF16))
    power = jnp.concatenate(power, axis=1)
    pens = jnp.concatenate([pen[...] for pen in refs[count : 2 * count]], axis=0)
    rows = jnp.concatenate([row[...] for row in refs[:count]], axis=0)
    energy = lax.dot_general(pens, power, NT, preferred_element_type=F32)
    total = lax.dot_general(rows, stacked, NT, preferred_element_type=F32)
    for n, out in enumerate(outs):
        mine = total[n * ROWS : (n + 1) * ROWS].reshape(SHIFTS, P_DEV, 128)
        mine = (mine - energy[None, n * P_DEV : (n + 1) * P_DEV]).reshape(ROWS, 128)
        for value in added_in:
            mine = mine + value[...]
        out[...] = mine


def make_scores(rows, pens, blocks, plus=()):
    count, more = len(rows), len(plus)
    return local(
        lambda *refs: scores_kernel(count, more, *refs), "partial_scores", [((ROWS, 128), F32)] * count,
        [], [*rows, *pens, *blocks, *plus], 12,
    )


def posterior_kernel(*refs):
    out = refs[-1]
    total = refs[0][...]
    for other in refs[1:-1]:
        total = total + other[...]
    total = total.reshape(SHIFTS, P_DEV, 128)
    peak = jnp.max(jnp.max(total, axis=0), axis=1, keepdims=True)
    expo = jnp.exp(total - peak[None])
    norm = jnp.sum(jnp.sum(expo, axis=0), axis=1, keepdims=True)
    share = (expo / norm[None]).reshape(ROWS, 128)
    out[...] = share.T.astype(BF16)


def make_posterior(parts):
    (out,) = local(posterior_kernel, "posterior", [((128, ROWS), BF16)], [], parts, 4)
    return out


def accum_kernel(part, x_ref, *refs):
    rows, posts, outs = refs[:G], refs[G : 2 * G], refs[2 * G :]

    @pl.loop(0, NB)
    def _(block):
        sums = []
        for half in range(2):
            start = pl.multiple_of(block * 2 * COLS + half * COLS + part * HALF, HALF)
            total = jnp.dot(posts[0][...], rows[0][:, pl.ds(start, HALF)], preferred_element_type=F32)
            for n in range(1, G):
                total = total + jnp.dot(
                    posts[n][...], rows[n][:, pl.ds(start, HALF)], preferred_element_type=F32
                )
            sums.append(total)
        if part == 0:
            for n in range(Y):
                for half, total in enumerate(sums):
                    spot = pl.multiple_of(block * COLS + half * HALF, HALF)
                    outs[n][:, pl.ds(spot, HALF)] = total[n * 32 : (n + 1) * 32].astype(BF16)
        else:
            for n in range(X):
                low = n & 1
                upper = ((x_ref[0] + n) & (X - 1)) >= 2
                spot = pl.multiple_of(block * HALF, HALF)
                for k in range(Y):
                    mine = slice(k * 32 + low * 16, k * 32 + low * 16 + 16)
                    chosen = jnp.where(upper, sums[1][mine], sums[0][mine])
                    outs[n][k * 16 : (k + 1) * 16, pl.ds(spot, HALF)] = chosen.astype(BF16)


def make_accum(part, place, rows, posts):
    shape = (32, NB * COLS) if part == 0 else (64, NB * HALF)
    return local(
        lambda *refs: accum_kernel(part, *refs), "weighted_sums", [(shape, BF16)] * 4, [place],
        [*rows, *posts], 8,
    )


def added(values):
    total = values[0].astype(F32)
    for value in values[1:]:
        total = total + value.astype(F32)
    return total


PIECES = [((16, NB * HALF), F32)] + [((16, NB * HALF), BF16)] * 3


def first_kernel(x_ref, *refs):
    outs = refs[4:]
    for block in range(NB):
        start = block * COLS
        real = added([ref[:, start : start + HALF] for ref in refs[:4]])
        imag = added([ref[:, start + HALF : start + COLS] for ref in refs[:4]])
        for n, out in enumerate(outs):
            mine = slice((n & 1) * 16, (n & 1) * 16 + 16)
            chosen = jnp.where(((x_ref[0] + n) & (X - 1)) >= 2, imag[mine], real[mine])
            out[:, block * HALF : (block + 1) * HALF] = chosen.astype(out.dtype)


def second_kernel(*refs):
    for n, out in enumerate(refs[4:]):
        out[...] = added([ref[n * 16 : (n + 1) * 16] for ref in refs[:4]]).astype(out.dtype)


def joined_kernel(block_ref, *refs):
    for n, out in enumerate(refs[8:]):
        spot = pl.ds(pl.multiple_of(((block_ref[0] + n) % NB) * HALF, HALF), HALF)
        out[:, :HALF] = added([ref[:, spot] for ref in refs[:4]]).astype(out.dtype)
        out[:, HALF:] = added([ref[:, spot] for ref in refs[4:8]]).astype(out.dtype)


def after(value, *others):
    return lax.optimization_barrier((value, *others))[0]


def per_device(refs, particles, shift_ids, wedge, defocus, inv_sigma):
    dom = lax.axis_index("dom")
    x_at = (dom // 16) * 2 + lax.axis_index("blk") % 2
    place = [value.astype(jnp.int32).reshape(1) for value in (dom % G, (dom % 16) // G, x_at)]
    member, block, x_at = place
    geo = jnp.asarray(geometry())

    chunks = split_particles(place, particles, shift_ids, wedge, defocus, inv_sigma)
    got, gathered, rows, pens = {}, {}, {}, {}
    got[2] = send(chunks[2], partners(2))
    got[1] = send(chunks[1], partners(1))
    own = own_columns(member, refs, chunks[2])
    gathered[0, 0] = own
    gathered[1, 0] = send(own, moves(dy=-1))
    gathered[3, 0] = send(own, moves(dy=1))
    gathered[0, 1] = send(own, moves(dx=-1))
    table, geo = make_table(member, geo)
    rows[0], pens[0] = make_rows(member, chunks[0], geo, table)
    wave = [got[1], gathered[1, 0], gathered[3, 0], gathered[0, 1], rows[0]]
    gathered[1, 1] = send(after(gathered[1, 0], *wave), moves(dx=-1))
    gathered[3, 1] = send(after(gathered[3, 0], *wave), moves(dx=1))
    gathered[2, 1] = send(after(gathered[0, 1], *wave), moves(dy=2))
    gathered[2, 0] = send(after(gathered[1, 0], *wave), moves(dy=-1))
    got[3] = send(after(chunks[3], *wave, got[2]), partners(3))
    rows[1], pens[1] = make_rows(member, after(got[1], *wave, got[2]), geo, table)
    rows[2], pens[2] = make_rows(member, after(got[2], rows[1]), geo, table)
    rows[3], pens[3] = make_rows(member, after(got[3], rows[2]), geo, table)
    blocks = [gathered[ky, kx] for ky in range(Y) for kx in range(2)]

    (second,) = make_scores([rows[2]], [after(pens[2], rows[3])], blocks)
    third, other = make_scores([rows[3], rows[1]], [after(pens[3], second), pens[1]], blocks)
    (mine,) = make_scores([rows[0]], [after(pens[0], third)], blocks, [send(second, partners(2))])
    arrived = [send(value, partners(n)) for value, n in ((third, 3), (other, 1))]
    posterior = make_posterior([mine, *arrived])
    posts = [posterior] + [send(posterior, partners(n)) for n in range(1, G)]
    rows = [rows[n] for n in range(G)]

    first = make_accum(0, x_at, rows, posts)
    first = [first[0]] + [send(first[n], moves(dy=n)) for n in range(1, Y)]
    second = make_accum(1, x_at, rows, posts)
    second = [
        second[0],
        send(second[1], moves(dx=1)),
        send(after(second[2], first[1]), moves(dx=2)),
        send(second[3], moves(dx=3)),
    ]
    first = local(first_kernel, "first_sums", PIECES, [x_at], first, 4)
    first = [first[0]] + [send(first[n], moves(dx=n)) for n in range(1, X)]
    second = local(second_kernel, "second_sums", PIECES, [], second, 4)
    second = [second[0]] + [send(second[n], moves(dy=n)) for n in range(1, Y)]
    outs = [((16, COLS), F32)] + [((16, COLS), BF16)] * (NB - 1)
    ends = local(joined_kernel, "joined_sums", outs, [block], [*first, *second], 4)
    return added([ends[0]] + [send(ends[n], moves(dz=n * (G // 2))) for n in range(1, NB)])


def solution(mesh):
    return jax.shard_map(
        per_device,
        mesh=mesh,
        in_specs=(
            P("blk", None),
            P(("blk", "dom"), None),
            P(("blk", "dom"), None),
            P(("blk", "dom"), None),
            P(("blk", "dom"), None),
            P(("blk", "dom")),
        ),
        out_specs=P("blk", "dom"),
        check_vma=False,
    )
```

```python
import math

import jax
import jax.numpy as jnp
import numpy as np
from jax import lax
from jax.experimental import pallas as pl
from jax.experimental.pallas import tpu as pltpu
from jax.sharding import PartitionSpec as P

BOX = 32
TILTS = 32
SHIFTS = 8
P_DEV = 32
Y, X, Z = 4, 4, 8
COLS = 1024
HALF = 512
G = 4
NB = 16 // G
ROWS = P_DEV * SHIFTS
WIDTH = NB * 2 * COLS
EXTRA = 384
AXES = ("blk", "dom")
F32, BF16 = jnp.float32, jnp.bfloat16
NT = (((1,), (1,)), ((), ()))
MIB = 1 << 20


def linear(y, x, z, core):
    y, x, z = y % Y, x % X, z % Z
    return (y * 2 + x % 2) * 32 + (x // 2) * 16 + z * 2 + core


def flips(y=0, x=0, z=0):
    return [
        (linear(i, j, k, c), linear(i ^ y, j ^ x, k ^ z, c))
        for i in range(Y) for j in range(X) for k in range(Z) for c in range(2)
    ]


def partners(k):
    return [
        (linear(y, x, z, c), linear(y, x, z ^ (k >> 1), c ^ (k & 1)))
        for y in range(Y) for x in range(X) for z in range(Z) for c in range(2)
    ]


def send(value, pairs):
    return lax.ppermute(value, AXES, pairs)


def geometry():
    position = np.arange(TILTS * HALF)
    tilt, within = position // HALF, position % HALF
    radial = (within // BOX).astype(np.float64)
    lateral = (within % BOX - BOX // 2).astype(np.float64)
    angle = (tilt - 0.5 * (TILTS - 1)) * (2.0 / TILTS)
    shell = (radial * radial + lateral * lateral) / (0.25 * BOX * BOX)
    zero = np.zeros_like(shell)
    table = np.stack([radial * np.cos(angle), lateral, radial * np.sin(angle), shell] + [zero] * 4)
    return table.reshape(8, 16, COLS).transpose(1, 0, 2).astype(np.float32)


def fold(turns):
    turns = turns - jnp.floor(turns + 0.5)
    far = jnp.abs(turns) > 0.25
    near = jnp.where(far, jnp.where(turns > 0, 0.5, -0.5) - turns, turns)
    return near * (2.0 * math.pi), far


def series(square, terms):
    total = jnp.full_like(square, terms[-1])
    for term in terms[-2::-1]:
        total = total * square + term
    return total


SIN_TERMS = [(-1) ** n / math.factorial(2 * n + 1) for n in range(6)]
COS_TERMS = [(-1) ** n / math.factorial(2 * n) for n in range(7)]


def sine_turns(turns):
    angle, _ = fold(turns)
    return angle * series(angle * angle, SIN_TERMS)


def held(value):
    return pltpu.with_memory_space_constraint(value, pltpu.VMEM)


SCALARS = pl.BlockSpec(memory_space=pltpu.SMEM)
WHOLE = pl.BlockSpec(memory_space=pltpu.VMEM)
PLACED = pl.BlockSpec(memory_space=pl.ANY)


def local(kernel, name, outs, scalars, arrays, limit, placed=0, scratch=()):
    return pl.pallas_call(
        kernel,
        in_specs=[SCALARS] * len(scalars) + [PLACED] * placed + [WHOLE] * (len(arrays) - placed),
        out_specs=[WHOLE] * len(outs),
        out_shape=[pltpu.VMEM(shape, kind) for shape, kind in outs],
        scratch_shapes=list(scratch),
        cost_estimate=pl.CostEstimate(flops=0, bytes_accessed=0, transcendentals=0),
        compiler_params=pltpu.CompilerParams(vmem_limit_bytes=limit * MIB),
        name=name,
    )(
        *scalars,
        *[pltpu.with_memory_space_constraint(value, pltpu.HBM) for value in arrays[:placed]],
        *[held(value) for value in arrays[placed:]],
    )


def table_kernel(member_ref, geo_ref, out_ref, picked_ref, sems):
    copies = [
        pltpu.make_async_copy(geo_ref.at[block * G + member_ref[0]], picked_ref.at[block], sems.at[block])
        for block in range(NB)
    ]
    for copy in copies:
        copy.start()
    ids = lax.broadcasted_iota(jnp.int32, (128, 1), 0).astype(F32)
    high = jnp.floor((ids + 0.5) * (1 / 25))
    middle = jnp.floor((ids - 25 * high + 0.5) * (1 / 5))
    low = ids - 25 * high - 5 * middle
    move_x, move_y, move_z = ((digit - 2.0) * (0.5 / BOX) for digit in (high, middle, low))
    for copy in copies:
        copy.wait()

    @pl.loop(0, NB)
    def _(block):
        geo = picked_ref[block]
        for tilt in range(2):
            part = geo[:, tilt * HALF : (tilt + 1) * HALF]
            turns = move_x * part[0:1] + move_y * part[1:2] + move_z * part[2:3]
            angle, far = fold(turns)
            square = angle * angle
            sine = angle * series(square, SIN_TERMS)
            cosine = series(square, COS_TERMS)
            cosine = jnp.where(far, -cosine, cosine)
            for at, values in enumerate((cosine, sine)):
                high = values.astype(BF16)
                low = (values - high.astype(F32)).astype(BF16)
                spot = pl.multiple_of(block * 2 * COLS + tilt * COLS + at * HALF, HALF)
                out_ref[0:128, pl.ds(spot, HALF)] = high
                out_ref[128:256, pl.ds(spot, HALF)] = low


def make_table(member, geo):
    return local(
        table_kernel, "phase_table", [((256, WIDTH), BF16), ((NB, 8, COLS), F32)], [member], [geo], 8,
        placed=1, scratch=[pltpu.SemaphoreType.DMA((NB,))],
    )


def column(part, block, who):
    return pl.ds(pl.multiple_of((part * 16 + block * G + who) * COLS, COLS), COLS)


def pieces_of(source, out, who, sems, base):
    return [
        pltpu.make_async_copy(
            source.at[:, column(part, block, who)],
            out.at[:, pl.ds((block * 2 + part) * COLS, COLS)],
            sems.at[base + block * 2 + part],
        )
        for block in range(NB) for part in range(2)
    ]


def own_kernel(member_ref, source, after, out, sems):
    copies = pieces_of(source, out, member_ref[0], sems, 0)
    for copy in copies:
        copy.start()
    for copy in copies:
        copy.wait()


def own_columns(member, refs, after):
    (own,) = local(
        own_kernel, "own_references", [((16, WIDTH), BF16)], [member], [refs, after], 4,
        placed=1, scratch=[pltpu.SemaphoreType.DMA((2 * NB,))],
    )
    return own


def parts_of(values):
    high = values.astype(BF16)
    rest = values - high.astype(F32)
    middle = rest.astype(BF16)
    return high, middle, (rest - middle.astype(F32)).astype(BF16)


def turned_over(values):
    rows, columns = values.shape
    same = lax.broadcasted_iota(jnp.int32, (columns, columns), 0) == lax.broadcasted_iota(
        jnp.int32, (columns, columns), 1
    )
    return sum(
        lax.dot_general(same.astype(BF16), part, NT, preferred_element_type=F32)
        for part in parts_of(values)
    )


def split_kernel(member_ref, block_ref, x_ref, source, ids, wedge, focus, sigma, *refs):
    outs, (ids_in, wedge_in, focus_in, sigma_in, sems, more) = refs[:G], refs[G:]
    copies = []
    for n in (2, 1, 3, 0):
        copies += pieces_of(source, outs[n], member_ref[0] ^ n, sems, n * 2 * NB)
    settings = [
        pltpu.make_async_copy(at, to, more.at[n])
        for n, (at, to) in enumerate(
            ((ids, ids_in), (wedge, wedge_in), (focus, focus_in), (sigma, sigma_in))
        )
    ]
    for copy in copies + settings:
        copy.start()
    for copy in settings:
        copy.wait()
    first = jnp.concatenate(
        [ids_in[...].astype(F32), jnp.broadcast_to(sigma_in[...], (8, P_DEV))], axis=0
    )
    info = jnp.concatenate(
        [
            turned_over(first),
            wedge_in[...].astype(F32),
            focus_in[...],
            jnp.zeros((P_DEV, 128 - 16 - 2 * TILTS), F32),
        ],
        axis=1,
    )
    for spot, piece in enumerate(parts_of(info)):
        for out in outs:
            out[:, WIDTH + spot * 128 : WIDTH + (spot + 1) * 128] = piece
    for copy in copies:
        copy.wait()


def split_particles(place, particles, shift_ids, wedge, defocus, inv_sigma):
    return local(
        split_kernel, "split_particles", [((P_DEV, WIDTH + EXTRA), BF16)] * G, place,
        [particles, shift_ids.T, wedge, defocus, inv_sigma[None]], 4, placed=5,
        scratch=[
            pltpu.VMEM((SHIFTS, P_DEV), jnp.int32),
            pltpu.VMEM((P_DEV, TILTS), jnp.int32),
            pltpu.VMEM((P_DEV, TILTS), F32),
            pltpu.VMEM((1, P_DEV), F32),
            pltpu.SemaphoreType.DMA((G * 2 * NB,)),
            pltpu.SemaphoreType.DMA((4,)),
        ],
    )


def rows_kernel(member_ref, x_ref, geo_ref, table_ref, rows_ref, pen_ref):
    info = sum(x_ref[:, WIDTH + n * 128 : WIDTH + (n + 1) * 128].astype(F32) for n in range(3))
    lane = lax.broadcasted_iota(jnp.int32, (ROWS, 256), 1) & 127
    ids = jnp.concatenate([info[:, s : s + 1] for s in range(SHIFTS)], axis=0)
    pick = (ids == lane.astype(F32)).astype(BF16)
    sigma = info[:, SHIFTS : SHIFTS + 1]
    small = lax.broadcasted_iota(jnp.int32, (P_DEV, 128), 1)

    @pl.loop(0, NB)
    def _(block):
        first = 2 * (block * G + member_ref[0]) + 16
        start = pl.multiple_of(block * 2 * COLS, 2 * COLS)
        for tilt in range(2):
            kept = jnp.sum(jnp.where(small == first + tilt, info, 0.0), axis=1, keepdims=True)
            focus = jnp.sum(jnp.where(small == first + tilt + TILTS, info, 0.0), axis=1, keepdims=True)
            shell = geo_ref[block, 3:4, tilt * HALF : (tilt + 1) * HALF]
            transfer = -sine_turns((4.0 * focus * shell + 0.1) * (0.5 / math.pi))
            weight = kept * transfer * sigma
            spot = pl.multiple_of(block * COLS + tilt * HALF, HALF)
            pen_ref[:, pl.ds(spot, HALF)] = (0.5 * weight * transfer).astype(BF16)
            lower, upper = pl.ds(start + tilt * HALF, HALF), pl.ds(start + COLS + tilt * HALF, HALF)
            real = (weight * x_ref[:, lower].astype(F32))[None]
            imag = (weight * x_ref[:, upper].astype(F32))[None]
            turned = jnp.dot(
                pick, table_ref[:, pl.ds(start + tilt * COLS, COLS)], preferred_element_type=F32
            ).reshape(SHIFTS, P_DEV, COLS)
            cosine, sine = turned[:, :, :HALF], turned[:, :, HALF:]
            rows_ref[:, lower] = (real * cosine + imag * sine).reshape(ROWS, HALF).astype(BF16)
            rows_ref[:, upper] = (imag * cosine - real * sine).reshape(ROWS, HALF).astype(BF16)


def make_rows(member, x, geo, table):
    return local(
        rows_kernel, "shifted_rows", [((ROWS, WIDTH), BF16), ((P_DEV, NB * COLS), BF16)], [member],
        [x, geo, table], 12,
    )


def scores_kernel(count, more, *refs):
    blocks = refs[2 * count : 2 * count + 8]
    added_in = refs[2 * count + 8 : 2 * count + 8 + more]
    outs = refs[2 * count + 8 + more :]
    stacked = jnp.concatenate([block[...] for block in blocks], axis=0)
    power = []
    for block in range(NB):
        start = block * 2 * COLS
        real = stacked[:, start : start + COLS].astype(F32)
        imag = stacked[:, start + COLS : start + 2 * COLS].astype(F32)
        power.append((real * real + imag * imag).astype(BF16))
    power = jnp.concatenate(power, axis=1)
    pens = jnp.concatenate([pen[...] for pen in refs[count : 2 * count]], axis=0)
    rows = jnp.concatenate([row[...] for row in refs[:count]], axis=0)
    energy = lax.dot_general(pens, power, NT, preferred_element_type=F32)
    total = lax.dot_general(rows, stacked, NT, preferred_element_type=F32)
    for n, out in enumerate(outs):
        mine = total[n * ROWS : (n + 1) * ROWS].reshape(SHIFTS, P_DEV, 128)
        mine = (mine - energy[None, n * P_DEV : (n + 1) * P_DEV]).reshape(ROWS, 128)
        for value in added_in:
            mine = mine + value[...]
        out[...] = mine


def make_scores(rows, pens, blocks, plus=()):
    count, more = len(rows), len(plus)
    return local(
        lambda *refs: scores_kernel(count, more, *refs), "partial_scores", [((ROWS, 128), F32)] * count,
        [], [*rows, *pens, *blocks, *plus], 12,
    )


def posterior_kernel(*refs):
    out = refs[-1]
    total = refs[0][...]
    for other in refs[1:-1]:
        total = total + other[...]
    total = total.reshape(SHIFTS, P_DEV, 128)
    peak = jnp.max(jnp.max(total, axis=0), axis=1, keepdims=True)
    expo = jnp.exp(total - peak[None])
    norm = jnp.sum(jnp.sum(expo, axis=0), axis=1, keepdims=True)
    share = (expo / norm[None]).reshape(ROWS, 128)
    out[...] = share.T.astype(BF16)


def make_posterior(parts):
    (out,) = local(posterior_kernel, "posterior", [((128, ROWS), BF16)], [], parts, 4)
    return out


def accum_kernel(part, x_ref, *refs):
    rows, posts, outs = refs[:G], refs[G : 2 * G], refs[2 * G :]

    @pl.loop(0, NB)
    def _(block):
        sums = []
        for half in range(2):
            start = pl.multiple_of(block * 2 * COLS + half * COLS + part * HALF, HALF)
            total = jnp.dot(posts[0][...], rows[0][:, pl.ds(start, HALF)], preferred_element_type=F32)
            for n in range(1, G):
                total = total + jnp.dot(
                    posts[n][...], rows[n][:, pl.ds(start, HALF)], preferred_element_type=F32
                )
            sums.append(total)
        if part == 0:
            for n in range(Y):
                for half, total in enumerate(sums):
                    spot = pl.multiple_of(block * COLS + half * HALF, HALF)
                    outs[n][:, pl.ds(spot, HALF)] = total[n * 32 : (n + 1) * 32].astype(BF16)
        else:
            for n in range(X):
                low = n & 1
                upper = (x_ref[0] >> 1) ^ (n >> 1) == 1
                spot = pl.multiple_of(block * HALF, HALF)
                for k in range(Y):
                    mine = slice(k * 32 + low * 16, k * 32 + low * 16 + 16)
                    chosen = jnp.where(upper, sums[1][mine], sums[0][mine])
                    outs[n][k * 16 : (k + 1) * 16, pl.ds(spot, HALF)] = chosen.astype(BF16)


def make_accum(part, place, rows, posts):
    shape = (32, NB * COLS) if part == 0 else (64, NB * HALF)
    return local(
        lambda *refs: accum_kernel(part, *refs), "weighted_sums", [(shape, BF16)] * 4, [place],
        [*rows, *posts], 8,
    )


def added(values):
    total = values[0].astype(F32)
    for value in values[1:]:
        total = total + value.astype(F32)
    return total


PIECES = [((16, NB * HALF), F32)] + [((16, NB * HALF), BF16)] * 3


def first_kernel(x_ref, *refs):
    outs = refs[4:]
    for block in range(NB):
        start = block * COLS
        real = added([ref[:, start : start + HALF] for ref in refs[:4]])
        imag = added([ref[:, start + HALF : start + COLS] for ref in refs[:4]])
        for n, out in enumerate(outs):
            mine = slice((n & 1) * 16, (n & 1) * 16 + 16)
            chosen = jnp.where((x_ref[0] >> 1) ^ (n >> 1) == 1, imag[mine], real[mine])
            out[:, block * HALF : (block + 1) * HALF] = chosen.astype(out.dtype)


def second_kernel(*refs):
    for n, out in enumerate(refs[4:]):
        out[...] = added([ref[n * 16 : (n + 1) * 16] for ref in refs[:4]]).astype(out.dtype)


def joined_kernel(block_ref, *refs):
    for n, out in enumerate(refs[8:]):
        spot = pl.ds(pl.multiple_of((block_ref[0] ^ n) * HALF, HALF), HALF)
        out[:, :HALF] = added([ref[:, spot] for ref in refs[:4]]).astype(out.dtype)
        out[:, HALF:] = added([ref[:, spot] for ref in refs[4:8]]).astype(out.dtype)


def after(value, *others):
    return lax.optimization_barrier((value, *others))[0]


def per_device(refs, particles, shift_ids, wedge, defocus, inv_sigma):
    dom = lax.axis_index("dom")
    x_at = (dom // 16) * 2 + lax.axis_index("blk") % 2
    place = [value.astype(jnp.int32).reshape(1) for value in (dom % G, (dom % 16) // G, x_at)]
    member, block, x_at = place
    geo = jnp.asarray(geometry())

    chunks = split_particles(place, particles, shift_ids, wedge, defocus, inv_sigma)
    got, gathered, rows, pens = {}, {}, {}, {}
    got[2] = send(chunks[2], partners(2))
    got[1] = send(chunks[1], partners(1))
    own = own_columns(member, refs, chunks[2])
    gathered[0, 0] = own
    gathered[1, 0] = send(own, flips(y=1))
    gathered[3, 0] = send(own, flips(y=3))
    gathered[0, 1] = send(own, flips(x=1))
    table, geo = make_table(member, geo)
    rows[0], pens[0] = make_rows(member, chunks[0], geo, table)
    wave = [got[1], gathered[1, 0], gathered[3, 0], gathered[0, 1], rows[0]]
    gathered[1, 1] = send(after(gathered[1, 0], *wave), flips(x=1))
    gathered[3, 1] = send(after(gathered[3, 0], *wave), flips(x=3))
    gathered[2, 1] = send(after(gathered[0, 1], *wave), flips(y=2))
    gathered[2, 0] = send(after(gathered[1, 0], *wave), flips(y=3))
    got[3] = send(after(chunks[3], *wave, got[2]), partners(3))
    rows[1], pens[1] = make_rows(member, after(got[1], *wave, got[2]), geo, table)
    rows[2], pens[2] = make_rows(member, after(got[2], rows[1]), geo, table)
    rows[3], pens[3] = make_rows(member, after(got[3], rows[2]), geo, table)
    blocks = [gathered[ky, kx] for ky in range(Y) for kx in range(2)]

    (second,) = make_scores([rows[2]], [after(pens[2], rows[3])], blocks)
    third, other = make_scores([rows[3], rows[1]], [after(pens[3], second), pens[1]], blocks)
    (mine,) = make_scores([rows[0]], [after(pens[0], third)], blocks, [send(second, partners(2))])
    arrived = [send(value, partners(n)) for value, n in ((third, 3), (other, 1))]
    posterior = make_posterior([mine, *arrived])
    posts = [posterior] + [send(posterior, partners(n)) for n in range(1, G)]
    rows = [rows[n] for n in range(G)]

    first = make_accum(0, x_at, rows, posts)
    first = [first[0]] + [send(first[n], flips(y=n)) for n in range(1, Y)]
    second = make_accum(1, x_at, rows, posts)
    second = [
        second[0],
        send(second[1], flips(x=1)),
        send(after(second[2], first[1]), flips(x=2)),
        send(second[3], flips(x=3)),
    ]
    first = local(first_kernel, "first_sums", PIECES, [x_at], first, 4)
    first = [first[0]] + [send(first[n], flips(x=n)) for n in range(1, X)]
    second = local(second_kernel, "second_sums", PIECES, [], second, 4)
    second = [second[0]] + [send(second[n], flips(y=n)) for n in range(1, Y)]
    outs = [((16, COLS), F32)] + [((16, COLS), BF16)] * (NB - 1)
    ends = local(joined_kernel, "joined_sums", outs, [block], [*first, *second], 4)
    return added([ends[0]] + [send(ends[n], flips(z=n * (G // 2))) for n in range(1, NB)])


def solution(mesh):
    return jax.shard_map(
        per_device,
        mesh=mesh,
        in_specs=(
            P("blk", None),
            P(("blk", "dom"), None),
            P(("blk", "dom"), None),
            P(("blk", "dom"), None),
            P(("blk", "dom"), None),
            P(("blk", "dom")),
        ),
        out_specs=P("blk", "dom"),
        check_vma=False,
    )
```

```python
import math

import jax
import jax.numpy as jnp
import numpy as np
from jax import lax
from jax.experimental import pallas as pl
from jax.experimental.pallas import tpu as pltpu
from jax.sharding import PartitionSpec as P

BOX = 32
TILTS = 32
SHIFTS = 8
P_DEV = 32
Y, X, Z = 4, 4, 8
COLS = 1024
HALF = 512
G = 4
NB = 16 // G
ROWS = P_DEV * SHIFTS
WIDTH = NB * 2 * COLS
EXTRA = 384
AXES = ("blk", "dom")
F32, BF16 = jnp.float32, jnp.bfloat16
NT = (((1,), (1,)), ((), ()))
MIB = 1 << 20


def linear(y, x, z, core):
    y, x, z = y % Y, x % X, z % Z
    return (y * 2 + x % 2) * 32 + (x // 2) * 16 + z * 2 + core


def flips(y=0, x=0, z=0):
    return [
        (linear(i, j, k, c), linear(i ^ y, j ^ x, k ^ z, c))
        for i in range(Y) for j in range(X) for k in range(Z) for c in range(2)
    ]


def crossed(n, core):
    return [
        (linear(i, j, k, c), linear(i ^ (n if c == core else 0), j ^ (0 if c == core else n), k, c))
        for i in range(Y) for j in range(X) for k in range(Z) for c in range(2)
    ]


def partners(k):
    return [
        (linear(y, x, z, c), linear(y, x, z ^ (k >> 1), c ^ (k & 1)))
        for y in range(Y) for x in range(X) for z in range(Z) for c in range(2)
    ]


def send(value, pairs):
    return lax.ppermute(value, AXES, pairs)


def geometry():
    position = np.arange(TILTS * HALF)
    tilt, within = position // HALF, position % HALF
    radial = (within // BOX).astype(np.float64)
    lateral = (within % BOX - BOX // 2).astype(np.float64)
    angle = (tilt - 0.5 * (TILTS - 1)) * (2.0 / TILTS)
    shell = (radial * radial + lateral * lateral) / (0.25 * BOX * BOX)
    zero = np.zeros_like(shell)
    table = np.stack([radial * np.cos(angle), lateral, radial * np.sin(angle), shell] + [zero] * 4)
    return table.reshape(8, 16, COLS).transpose(1, 0, 2).astype(np.float32)


def fold(turns):
    turns = turns - jnp.floor(turns + 0.5)
    far = jnp.abs(turns) > 0.25
    near = jnp.where(far, jnp.where(turns > 0, 0.5, -0.5) - turns, turns)
    return near * (2.0 * math.pi), far


def series(square, terms):
    total = jnp.full_like(square, terms[-1])
    for term in terms[-2::-1]:
        total = total * square + term
    return total


SIN_TERMS = [(-1) ** n / math.factorial(2 * n + 1) for n in range(6)]
COS_TERMS = [(-1) ** n / math.factorial(2 * n) for n in range(7)]


def sine_turns(turns):
    angle, _ = fold(turns)
    return angle * series(angle * angle, SIN_TERMS)


def held(value):
    return pltpu.with_memory_space_constraint(value, pltpu.VMEM)


SCALARS = pl.BlockSpec(memory_space=pltpu.SMEM)
WHOLE = pl.BlockSpec(memory_space=pltpu.VMEM)
PLACED = pl.BlockSpec(memory_space=pl.ANY)


def local(kernel, name, outs, scalars, arrays, limit, placed=0, scratch=()):
    return pl.pallas_call(
        kernel,
        in_specs=[SCALARS] * len(scalars) + [PLACED] * placed + [WHOLE] * (len(arrays) - placed),
        out_specs=[WHOLE] * len(outs),
        out_shape=[pltpu.VMEM(shape, kind) for shape, kind in outs],
        scratch_shapes=list(scratch),
        cost_estimate=pl.CostEstimate(flops=0, bytes_accessed=0, transcendentals=0),
        compiler_params=pltpu.CompilerParams(vmem_limit_bytes=limit * MIB),
        name=name,
    )(
        *scalars,
        *[pltpu.with_memory_space_constraint(value, pltpu.HBM) for value in arrays[:placed]],
        *[held(value) for value in arrays[placed:]],
    )


def table_kernel(member_ref, geo_ref, out_ref, picked_ref, sems):
    copies = [
        pltpu.make_async_copy(geo_ref.at[block * G + member_ref[0]], picked_ref.at[block], sems.at[block])
        for block in range(NB)
    ]
    for copy in copies:
        copy.start()
    ids = lax.broadcasted_iota(jnp.int32, (128, 1), 0).astype(F32)
    high = jnp.floor((ids + 0.5) * (1 / 25))
    middle = jnp.floor((ids - 25 * high + 0.5) * (1 / 5))
    low = ids - 25 * high - 5 * middle
    move_x, move_y, move_z = ((digit - 2.0) * (0.5 / BOX) for digit in (high, middle, low))
    for copy in copies:
        copy.wait()

    @pl.loop(0, NB)
    def _(block):
        geo = picked_ref[block]
        for tilt in range(2):
            part = geo[:, tilt * HALF : (tilt + 1) * HALF]
            turns = move_x * part[0:1] + move_y * part[1:2] + move_z * part[2:3]
            angle, far = fold(turns)
            square = angle * angle
            sine = angle * series(square, SIN_TERMS)
            cosine = series(square, COS_TERMS)
            cosine = jnp.where(far, -cosine, cosine)
            for at, values in enumerate((cosine, sine)):
                high = values.astype(BF16)
                low = (values - high.astype(F32)).astype(BF16)
                spot = pl.multiple_of(block * 2 * COLS + tilt * COLS + at * HALF, HALF)
                out_ref[0:128, pl.ds(spot, HALF)] = high
                out_ref[128:256, pl.ds(spot, HALF)] = low


def make_table(member, geo):
    return local(
        table_kernel, "phase_table", [((256, WIDTH), BF16), ((NB, 8, COLS), F32)], [member], [geo], 8,
        placed=1, scratch=[pltpu.SemaphoreType.DMA((NB,))],
    )


def column(part, block, who):
    return pl.ds(pl.multiple_of((part * 16 + block * G + who) * COLS, COLS), COLS)


def pieces_of(source, out, who, sems, base):
    return [
        pltpu.make_async_copy(
            source.at[:, column(part, block, who)],
            out.at[:, pl.ds((block * 2 + part) * COLS, COLS)],
            sems.at[base + block * 2 + part],
        )
        for block in range(NB) for part in range(2)
    ]


def own_kernel(member_ref, source, after, out, sems):
    copies = pieces_of(source, out, member_ref[0], sems, 0)
    for copy in copies:
        copy.start()
    for copy in copies:
        copy.wait()


def own_columns(member, refs, after):
    (own,) = local(
        own_kernel, "own_references", [((16, WIDTH), BF16)], [member], [refs, after], 4,
        placed=1, scratch=[pltpu.SemaphoreType.DMA((2 * NB,))],
    )
    return own


def parts_of(values):
    high = values.astype(BF16)
    rest = values - high.astype(F32)
    middle = rest.astype(BF16)
    return high, middle, (rest - middle.astype(F32)).astype(BF16)


def turned_over(values):
    rows, columns = values.shape
    same = lax.broadcasted_iota(jnp.int32, (columns, columns), 0) == lax.broadcasted_iota(
        jnp.int32, (columns, columns), 1
    )
    return sum(
        lax.dot_general(same.astype(BF16), part, NT, preferred_element_type=F32)
        for part in parts_of(values)
    )


def split_kernel(member_ref, block_ref, x_ref, source, ids, wedge, focus, sigma, *refs):
    outs, (ids_in, wedge_in, focus_in, sigma_in, sems, more) = refs[:G], refs[G:]
    copies = []
    for n in (2, 1, 3, 0):
        copies += pieces_of(source, outs[n], member_ref[0] ^ n, sems, n * 2 * NB)
    settings = [
        pltpu.make_async_copy(at, to, more.at[n])
        for n, (at, to) in enumerate(
            ((ids, ids_in), (wedge, wedge_in), (focus, focus_in), (sigma, sigma_in))
        )
    ]
    for copy in copies + settings:
        copy.start()
    for copy in settings:
        copy.wait()
    first = jnp.concatenate(
        [ids_in[...].astype(F32), jnp.broadcast_to(sigma_in[...], (8, P_DEV))], axis=0
    )
    info = jnp.concatenate(
        [
            turned_over(first),
            wedge_in[...].astype(F32),
            focus_in[...],
            jnp.zeros((P_DEV, 128 - 16 - 2 * TILTS), F32),
        ],
        axis=1,
    )
    for spot, piece in enumerate(parts_of(info)):
        for out in outs:
            out[:, WIDTH + spot * 128 : WIDTH + (spot + 1) * 128] = piece
    for copy in copies:
        copy.wait()


def split_particles(place, particles, shift_ids, wedge, defocus, inv_sigma):
    return local(
        split_kernel, "split_particles", [((P_DEV, WIDTH + EXTRA), BF16)] * G, place,
        [particles, shift_ids.T, wedge, defocus, inv_sigma[None]], 4, placed=5,
        scratch=[
            pltpu.VMEM((SHIFTS, P_DEV), jnp.int32),
            pltpu.VMEM((P_DEV, TILTS), jnp.int32),
            pltpu.VMEM((P_DEV, TILTS), F32),
            pltpu.VMEM((1, P_DEV), F32),
            pltpu.SemaphoreType.DMA((G * 2 * NB,)),
            pltpu.SemaphoreType.DMA((4,)),
        ],
    )


def rows_kernel(member_ref, x_ref, geo_ref, table_ref, rows_ref, pen_ref):
    info = sum(x_ref[:, WIDTH + n * 128 : WIDTH + (n + 1) * 128].astype(F32) for n in range(3))
    lane = lax.broadcasted_iota(jnp.int32, (ROWS, 256), 1) & 127
    ids = jnp.concatenate([info[:, s : s + 1] for s in range(SHIFTS)], axis=0)
    pick = (ids == lane.astype(F32)).astype(BF16)
    sigma = info[:, SHIFTS : SHIFTS + 1]
    small = lax.broadcasted_iota(jnp.int32, (P_DEV, 128), 1)

    @pl.loop(0, NB)
    def _(block):
        first = 2 * (block * G + member_ref[0]) + 16
        start = pl.multiple_of(block * 2 * COLS, 2 * COLS)
        for tilt in range(2):
            kept = jnp.sum(jnp.where(small == first + tilt, info, 0.0), axis=1, keepdims=True)
            focus = jnp.sum(jnp.where(small == first + tilt + TILTS, info, 0.0), axis=1, keepdims=True)
            shell = geo_ref[block, 3:4, tilt * HALF : (tilt + 1) * HALF]
            transfer = -sine_turns((4.0 * focus * shell + 0.1) * (0.5 / math.pi))
            weight = kept * transfer * sigma
            spot = pl.multiple_of(block * COLS + tilt * HALF, HALF)
            pen_ref[:, pl.ds(spot, HALF)] = (0.5 * weight * transfer).astype(BF16)
            lower, upper = pl.ds(start + tilt * HALF, HALF), pl.ds(start + COLS + tilt * HALF, HALF)
            real = (weight * x_ref[:, lower].astype(F32))[None]
            imag = (weight * x_ref[:, upper].astype(F32))[None]
            turned = jnp.dot(
                pick, table_ref[:, pl.ds(start + tilt * COLS, COLS)], preferred_element_type=F32
            ).reshape(SHIFTS, P_DEV, COLS)
            cosine, sine = turned[:, :, :HALF], turned[:, :, HALF:]
            rows_ref[:, lower] = (real * cosine + imag * sine).reshape(ROWS, HALF).astype(BF16)
            rows_ref[:, upper] = (imag * cosine - real * sine).reshape(ROWS, HALF).astype(BF16)


def make_rows(member, x, geo, table):
    return local(
        rows_kernel, "shifted_rows", [((ROWS, WIDTH), BF16), ((P_DEV, NB * COLS), BF16)], [member],
        [x, geo, table], 12,
    )


def scores_kernel(count, *refs):
    blocks = refs[2 * count : 2 * count + 8]
    outs = refs[2 * count + 8 :]
    stacked = jnp.concatenate([block[...] for block in blocks], axis=0)
    power = []
    for block in range(NB):
        start = block * 2 * COLS
        real = stacked[:, start : start + COLS].astype(F32)
        imag = stacked[:, start + COLS : start + 2 * COLS].astype(F32)
        power.append((real * real + imag * imag).astype(BF16))
    power = jnp.concatenate(power, axis=1)
    pens = jnp.concatenate([pen[...] for pen in refs[count : 2 * count]], axis=0)
    rows = jnp.concatenate([row[...] for row in refs[:count]], axis=0)
    energy = lax.dot_general(pens, power, NT, preferred_element_type=F32)
    total = lax.dot_general(rows, stacked, NT, preferred_element_type=F32)
    for n, out in enumerate(outs):
        mine = total[n * ROWS : (n + 1) * ROWS].reshape(SHIFTS, P_DEV, 128)
        out[...] = (mine - energy[None, n * P_DEV : (n + 1) * P_DEV]).reshape(ROWS, 128)


def make_scores(rows, pens, blocks):
    count = len(rows)
    return local(
        lambda *refs: scores_kernel(count, *refs), "partial_scores", [((ROWS, 128), F32)] * count,
        [], [*rows, *pens, *blocks], 12,
    )


def sum_kernel(*refs):
    refs[-1][...] = refs[0][...] + refs[1][...] + refs[2][...]


def posterior_kernel(*refs):
    out = refs[-1]
    total = refs[0][...]
    for other in refs[1:-1]:
        total = total + other[...]
    total = total.reshape(SHIFTS, P_DEV, 128)
    peak = jnp.max(jnp.max(total, axis=0), axis=1, keepdims=True)
    expo = jnp.exp(total - peak[None])
    norm = jnp.sum(jnp.sum(expo, axis=0), axis=1, keepdims=True)
    share = (expo / norm[None]).reshape(ROWS, 128)
    out[...] = share.T.astype(BF16)


def make_posterior(parts):
    (out,) = local(posterior_kernel, "posterior", [((128, ROWS), BF16)], [], parts, 4)
    return out


def accum_kernel(part, member_ref, x_ref, *refs):
    rows, posts, outs = refs[:G], refs[G : 2 * G], refs[2 * G :]
    along_y = (member_ref[0] & 1) == part
    high = x_ref[0] >> 1

    @pl.loop(0, NB)
    def _(block):
        sums = []
        for half in range(2):
            start = pl.multiple_of(block * 2 * COLS + half * COLS + part * HALF, HALF)
            total = jnp.dot(posts[0][...], rows[0][:, pl.ds(start, HALF)], preferred_element_type=F32)
            for n in range(1, G):
                total = total + jnp.dot(
                    posts[n][...], rows[n][:, pl.ds(start, HALF)], preferred_element_type=F32
                )
            sums.append(total)
        spot = pl.ds(pl.multiple_of(block * HALF, HALF), HALF)
        for n, out in enumerate(outs):
            upper = high ^ (n >> 1) == 1
            for group in range(4):
                at = n * 32 + (group >> 1) * 16
                for_y = sums[group & 1][at : at + 16]
                at = group * 32 + (n & 1) * 16
                for_x = jnp.where(upper, sums[1][at : at + 16], sums[0][at : at + 16])
                out[group * 16 : (group + 1) * 16, spot] = jnp.where(along_y, for_y, for_x).astype(BF16)


def make_accum(part, member, x_at, rows, posts):
    return local(
        lambda *refs: accum_kernel(part, *refs), "weighted_sums", [((64, NB * HALF), BF16)] * 4,
        [member, x_at], [*rows, *posts], 8,
    )


def added(values):
    total = values[0].astype(F32)
    for value in values[1:]:
        total = total + value.astype(F32)
    return total


PIECES = [((16, NB * HALF), F32)] + [((16, NB * HALF), BF16)] * 3


def turn_kernel(part, member_ref, x_ref, *refs):
    along_y = (member_ref[0] & 1) == part
    for n, out in enumerate(refs[4:]):
        group = jnp.where(along_y, (n & 1) * 2 + ((x_ref[0] >> 1) ^ (n >> 1)), n)
        mine = pl.ds(pl.multiple_of(group * 16, 16), 16)
        out[...] = added([ref[mine, :] for ref in refs[:4]]).astype(out.dtype)


def make_turn(part, member, x_at, values):
    return local(
        lambda *refs: turn_kernel(part, *refs), "turned_sums", PIECES, [member, x_at], values, 4
    )


def joined_kernel(block_ref, *refs):
    for n, out in enumerate(refs[8:]):
        spot = pl.ds(pl.multiple_of((block_ref[0] ^ n) * HALF, HALF), HALF)
        out[:, :HALF] = added([ref[:, spot] for ref in refs[:4]]).astype(out.dtype)
        out[:, HALF:] = added([ref[:, spot] for ref in refs[4:8]]).astype(out.dtype)


def after(value, *others):
    return lax.optimization_barrier((value, *others))[0]


def per_device(refs, particles, shift_ids, wedge, defocus, inv_sigma):
    dom = lax.axis_index("dom")
    x_at = (dom // 16) * 2 + lax.axis_index("blk") % 2
    place = [value.astype(jnp.int32).reshape(1) for value in (dom % G, (dom % 16) // G, x_at)]
    member, block, x_at = place
    geo = jnp.asarray(geometry())

    chunks = split_particles(place, particles, shift_ids, wedge, defocus, inv_sigma)
    got, gathered, rows, pens = {}, {}, {}, {}
    got[2] = send(chunks[2], partners(2))
    got[1] = send(chunks[1], partners(1))
    own = own_columns(member, refs, chunks[2])
    gathered[0, 0] = own
    gathered[1, 0] = send(own, flips(y=1))
    gathered[3, 0] = send(own, flips(y=3))
    gathered[0, 1] = send(own, flips(x=1))
    table, geo = make_table(member, geo)
    rows[0], pens[0] = make_rows(member, chunks[0], geo, table)
    wave = [got[1], gathered[1, 0], gathered[3, 0], gathered[0, 1], rows[0]]
    gathered[1, 1] = send(after(gathered[1, 0], *wave), flips(x=1))
    gathered[3, 1] = send(after(gathered[3, 0], *wave), flips(x=3))
    gathered[2, 1] = send(after(gathered[0, 1], *wave), flips(y=2))
    gathered[2, 0] = send(after(gathered[1, 0], *wave), flips(y=3))
    got[3] = send(after(chunks[3], *wave, got[2]), partners(3))
    rows[1], pens[1] = make_rows(member, after(got[1], *wave, got[2]), geo, table)
    rows[2], pens[2] = make_rows(member, after(got[2], rows[1]), geo, table)
    rows[3], pens[3] = make_rows(member, after(got[3], rows[2]), geo, table)
    blocks = [gathered[ky, kx] for ky in range(Y) for kx in range(2)]

    (second,) = make_scores([rows[2]], [after(pens[2], rows[3])], blocks)
    (third,) = make_scores([rows[3]], [after(pens[3], second)], blocks)
    mine, other = make_scores([rows[0], rows[1]], [after(pens[0], third), pens[1]], blocks)
    near = [mine, send(second, partners(2)), send(third, partners(3))]
    (near,) = local(sum_kernel, "score_sums", [((ROWS, 128), F32)], [], near, 4)
    posterior = make_posterior([near, send(other, partners(1))])
    posts = [posterior] + [send(posterior, partners(n)) for n in range(1, G)]
    rows = [rows[n] for n in range(G)]

    first = make_accum(0, member, x_at, rows, posts)
    first = [first[0]] + [send(first[n], crossed(n, 0)) for n in range(1, 4)]
    second = make_accum(1, member, x_at, rows, posts)
    second = [
        second[0],
        send(second[1], crossed(1, 1)),
        send(after(second[2], first[1]), crossed(2, 1)),
        send(second[3], crossed(3, 1)),
    ]
    first = make_turn(0, member, x_at, first)
    first = [first[0]] + [send(first[n], crossed(n, 1)) for n in range(1, 4)]
    second = make_turn(1, member, x_at, second)
    second = [second[0]] + [send(second[n], crossed(n, 0)) for n in range(1, 4)]
    outs = [((16, COLS), F32)] + [((16, COLS), BF16)] * (NB - 1)
    ends = local(joined_kernel, "joined_sums", outs, [block], [*first, *second], 4)
    return added([ends[0]] + [send(ends[n], flips(z=n * (G // 2))) for n in range(1, NB)])


def solution(mesh):
    return jax.shard_map(
        per_device,
        mesh=mesh,
        in_specs=(
            P("blk", None),
            P(("blk", "dom"), None),
            P(("blk", "dom"), None),
            P(("blk", "dom"), None),
            P(("blk", "dom"), None),
            P(("blk", "dom")),
        ),
        out_specs=P("blk", "dom"),
        check_vma=False,
    )
```

```python
import math

import jax
import jax.numpy as jnp
import numpy as np
from jax import lax
from jax.experimental import pallas as pl
from jax.experimental.pallas import tpu as pltpu
from jax.sharding import PartitionSpec as P

BOX = 32
TILTS = 32
SHIFTS = 8
P_DEV = 32
Y, X, Z = 4, 4, 8
COLS = 1024
HALF = 512
G = 4
NB = 16 // G
ROWS = P_DEV * SHIFTS
WIDTH = NB * 2 * COLS
EXTRA = 384
AXES = ("blk", "dom")
F32, BF16 = jnp.float32, jnp.bfloat16
NT = (((1,), (1,)), ((), ()))
MIB = 1 << 20


def linear(y, x, z, core):
    y, x, z = y % Y, x % X, z % Z
    return (y * 2 + x % 2) * 32 + (x // 2) * 16 + z * 2 + core


def flips(y=0, x=0, z=0):
    return [
        (linear(i, j, k, c), linear(i ^ y, j ^ x, k ^ z, c))
        for i in range(Y) for j in range(X) for k in range(Z) for c in range(2)
    ]


def crossed(n, core):
    return [
        (linear(i, j, k, c), linear(i ^ (n if c == core else 0), j ^ (0 if c == core else n), k, c))
        for i in range(Y) for j in range(X) for k in range(Z) for c in range(2)
    ]


def partners(k):
    return [
        (linear(y, x, z, c), linear(y, x, z ^ (k >> 1), c ^ (k & 1)))
        for y in range(Y) for x in range(X) for z in range(Z) for c in range(2)
    ]


def send(value, pairs):
    return lax.ppermute(value, AXES, pairs)


def geometry():
    position = np.arange(TILTS * HALF)
    tilt, within = position // HALF, position % HALF
    radial = (within // BOX).astype(np.float64)
    lateral = (within % BOX - BOX // 2).astype(np.float64)
    angle = (tilt - 0.5 * (TILTS - 1)) * (2.0 / TILTS)
    shell = (radial * radial + lateral * lateral) / (0.25 * BOX * BOX)
    zero = np.zeros_like(shell)
    table = np.stack([radial * np.cos(angle), lateral, radial * np.sin(angle), shell] + [zero] * 4)
    return table.reshape(8, 16, COLS).transpose(1, 0, 2).astype(np.float32)


def fold(turns):
    turns = turns - jnp.floor(turns + 0.5)
    far = jnp.abs(turns) > 0.25
    near = jnp.where(far, jnp.where(turns > 0, 0.5, -0.5) - turns, turns)
    return near * (2.0 * math.pi), far


def series(square, terms):
    total = jnp.full_like(square, terms[-1])
    for term in terms[-2::-1]:
        total = total * square + term
    return total


SIN_TERMS = [(-1) ** n / math.factorial(2 * n + 1) for n in range(6)]
COS_TERMS = [(-1) ** n / math.factorial(2 * n) for n in range(7)]


def sine_turns(turns):
    angle, _ = fold(turns)
    return angle * series(angle * angle, SIN_TERMS)


def held(value):
    return pltpu.with_memory_space_constraint(value, pltpu.VMEM)


SCALARS = pl.BlockSpec(memory_space=pltpu.SMEM)
WHOLE = pl.BlockSpec(memory_space=pltpu.VMEM)
PLACED = pl.BlockSpec(memory_space=pl.ANY)


def local(kernel, name, outs, scalars, arrays, limit, placed=0, scratch=()):
    return pl.pallas_call(
        kernel,
        in_specs=[SCALARS] * len(scalars) + [PLACED] * placed + [WHOLE] * (len(arrays) - placed),
        out_specs=[WHOLE] * len(outs),
        out_shape=[pltpu.VMEM(shape, kind) for shape, kind in outs],
        scratch_shapes=list(scratch),
        cost_estimate=pl.CostEstimate(flops=0, bytes_accessed=0, transcendentals=0),
        compiler_params=pltpu.CompilerParams(vmem_limit_bytes=limit * MIB),
        name=name,
    )(
        *scalars,
        *[pltpu.with_memory_space_constraint(value, pltpu.HBM) for value in arrays[:placed]],
        *[held(value) for value in arrays[placed:]],
    )


def table_kernel(member_ref, geo_ref, out_ref, picked_ref, sems):
    copies = [
        pltpu.make_async_copy(geo_ref.at[block * G + member_ref[0]], picked_ref.at[block], sems.at[block])
        for block in range(NB)
    ]
    for copy in copies:
        copy.start()
    ids = lax.broadcasted_iota(jnp.int32, (128, 1), 0).astype(F32)
    high = jnp.floor((ids + 0.5) * (1 / 25))
    middle = jnp.floor((ids - 25 * high + 0.5) * (1 / 5))
    low = ids - 25 * high - 5 * middle
    move_x, move_y, move_z = ((digit - 2.0) * (0.5 / BOX) for digit in (high, middle, low))
    for copy in copies:
        copy.wait()

    @pl.loop(0, NB)
    def _(block):
        geo = picked_ref[block]
        for tilt in range(2):
            part = geo[:, tilt * HALF : (tilt + 1) * HALF]
            turns = move_x * part[0:1] + move_y * part[1:2] + move_z * part[2:3]
            angle, far = fold(turns)
            square = angle * angle
            sine = angle * series(square, SIN_TERMS)
            cosine = series(square, COS_TERMS)
            cosine = jnp.where(far, -cosine, cosine)
            for at, values in enumerate((cosine, sine)):
                high = values.astype(BF16)
                low = (values - high.astype(F32)).astype(BF16)
                spot = pl.multiple_of(block * 2 * COLS + tilt * COLS + at * HALF, HALF)
                out_ref[0:128, pl.ds(spot, HALF)] = high
                out_ref[128:256, pl.ds(spot, HALF)] = low


def make_table(member, geo):
    return local(
        table_kernel, "phase_table", [((256, WIDTH), BF16), ((NB, 8, COLS), F32)], [member], [geo], 8,
        placed=1, scratch=[pltpu.SemaphoreType.DMA((NB,))],
    )


def column(part, block, who):
    return pl.ds(pl.multiple_of((part * 16 + block * G + who) * COLS, COLS), COLS)


def pieces_of(source, out, who, sems, base):
    return [
        pltpu.make_async_copy(
            source.at[:, column(part, block, who)],
            out.at[:, pl.ds((block * 2 + part) * COLS, COLS)],
            sems.at[base + block * 2 + part],
        )
        for block in range(NB) for part in range(2)
    ]


def own_kernel(member_ref, source, after, out, sems):
    copies = pieces_of(source, out, member_ref[0], sems, 0)
    for copy in copies:
        copy.start()
    for copy in copies:
        copy.wait()


def own_columns(member, refs, after):
    (own,) = local(
        own_kernel, "own_references", [((16, WIDTH), BF16)], [member], [refs, after], 4,
        placed=1, scratch=[pltpu.SemaphoreType.DMA((2 * NB,))],
    )
    return own


def parts_of(values):
    high = values.astype(BF16)
    rest = values - high.astype(F32)
    middle = rest.astype(BF16)
    return high, middle, (rest - middle.astype(F32)).astype(BF16)


def turned_over(values):
    rows, columns = values.shape
    same = lax.broadcasted_iota(jnp.int32, (columns, columns), 0) == lax.broadcasted_iota(
        jnp.int32, (columns, columns), 1
    )
    return sum(
        lax.dot_general(same.astype(BF16), part, NT, preferred_element_type=F32)
        for part in parts_of(values)
    )


def split_kernel(member_ref, block_ref, x_ref, source, ids, wedge, focus, sigma, *refs):
    outs, (ids_in, wedge_in, focus_in, sigma_in, sems, more) = refs[:G], refs[G:]
    copies = []
    for n in (2, 1, 3, 0):
        copies += pieces_of(source, outs[n], member_ref[0] ^ n, sems, n * 2 * NB)
    settings = [
        pltpu.make_async_copy(at, to, more.at[n])
        for n, (at, to) in enumerate(
            ((ids, ids_in), (wedge, wedge_in), (focus, focus_in), (sigma, sigma_in))
        )
    ]
    for copy in copies + settings:
        copy.start()
    for copy in settings:
        copy.wait()
    first = jnp.concatenate(
        [ids_in[...].astype(F32), jnp.broadcast_to(sigma_in[...], (8, P_DEV))], axis=0
    )
    info = jnp.concatenate(
        [
            turned_over(first),
            wedge_in[...].astype(F32),
            focus_in[...],
            jnp.zeros((P_DEV, 128 - 16 - 2 * TILTS), F32),
        ],
        axis=1,
    )
    for spot, piece in enumerate(parts_of(info)):
        for out in outs:
            out[:, WIDTH + spot * 128 : WIDTH + (spot + 1) * 128] = piece
    for copy in copies:
        copy.wait()


def split_particles(place, particles, shift_ids, wedge, defocus, inv_sigma):
    return local(
        split_kernel, "split_particles", [((P_DEV, WIDTH + EXTRA), BF16)] * G, place,
        [particles, shift_ids.T, wedge, defocus, inv_sigma[None]], 4, placed=5,
        scratch=[
            pltpu.VMEM((SHIFTS, P_DEV), jnp.int32),
            pltpu.VMEM((P_DEV, TILTS), jnp.int32),
            pltpu.VMEM((P_DEV, TILTS), F32),
            pltpu.VMEM((1, P_DEV), F32),
            pltpu.SemaphoreType.DMA((G * 2 * NB,)),
            pltpu.SemaphoreType.DMA((4,)),
        ],
    )


def rows_kernel(member_ref, x_ref, geo_ref, table_ref, rows_ref, pen_ref):
    info = sum(x_ref[:, WIDTH + n * 128 : WIDTH + (n + 1) * 128].astype(F32) for n in range(3))
    lane = lax.broadcasted_iota(jnp.int32, (ROWS, 256), 1) & 127
    ids = jnp.concatenate([info[:, s : s + 1] for s in range(SHIFTS)], axis=0)
    pick = (ids == lane.astype(F32)).astype(BF16)
    sigma = info[:, SHIFTS : SHIFTS + 1]
    small = lax.broadcasted_iota(jnp.int32, (P_DEV, 128), 1)

    @pl.loop(0, NB)
    def _(block):
        first = 2 * (block * G + member_ref[0]) + 16
        start = pl.multiple_of(block * 2 * COLS, 2 * COLS)
        for tilt in range(2):
            kept = jnp.sum(jnp.where(small == first + tilt, info, 0.0), axis=1, keepdims=True)
            focus = jnp.sum(jnp.where(small == first + tilt + TILTS, info, 0.0), axis=1, keepdims=True)
            shell = geo_ref[block, 3:4, tilt * HALF : (tilt + 1) * HALF]
            transfer = -sine_turns((4.0 * focus * shell + 0.1) * (0.5 / math.pi))
            weight = kept * transfer * sigma
            spot = pl.multiple_of(block * COLS + tilt * HALF, HALF)
            pen_ref[:, pl.ds(spot, HALF)] = (0.5 * weight * transfer).astype(BF16)
            lower, upper = pl.ds(start + tilt * HALF, HALF), pl.ds(start + COLS + tilt * HALF, HALF)
            real = (weight * x_ref[:, lower].astype(F32))[None]
            imag = (weight * x_ref[:, upper].astype(F32))[None]
            turned = jnp.dot(
                pick, table_ref[:, pl.ds(start + tilt * COLS, COLS)], preferred_element_type=F32
            ).reshape(SHIFTS, P_DEV, COLS)
            cosine, sine = turned[:, :, :HALF], turned[:, :, HALF:]
            rows_ref[:, lower] = (real * cosine + imag * sine).reshape(ROWS, HALF).astype(BF16)
            rows_ref[:, upper] = (imag * cosine - real * sine).reshape(ROWS, HALF).astype(BF16)


def make_rows(member, x, geo, table):
    return local(
        rows_kernel, "shifted_rows", [((ROWS, WIDTH), BF16), ((P_DEV, NB * COLS), BF16)], [member],
        [x, geo, table], 12,
    )


def scores_kernel(count, fresh, *refs):
    blocks = refs[2 * count : 2 * count + 8]
    outs = refs[2 * count + 8 :]
    stacked = jnp.concatenate([block[...] for block in blocks], axis=0)
    if fresh:
        for block in range(NB):
            start = block * 2 * COLS
            real = stacked[:, start : start + COLS].astype(F32)
            imag = stacked[:, start + COLS : start + 2 * COLS].astype(F32)
            outs[-1][:, block * COLS : (block + 1) * COLS] = (real * real + imag * imag).astype(BF16)
        power, outs = outs[-1][...], outs[:-1]
    else:
        power, outs = outs[0][...], outs[1:]
    pens = jnp.concatenate([pen[...] for pen in refs[count : 2 * count]], axis=0)
    rows = jnp.concatenate([row[...] for row in refs[:count]], axis=0)
    energy = lax.dot_general(pens, power, NT, preferred_element_type=F32)
    total = lax.dot_general(rows, stacked, NT, preferred_element_type=F32)
    for n, out in enumerate(outs):
        mine = total[n * ROWS : (n + 1) * ROWS].reshape(SHIFTS, P_DEV, 128)
        out[...] = (mine - energy[None, n * P_DEV : (n + 1) * P_DEV]).reshape(ROWS, 128)


def make_scores(rows, pens, blocks, power=None):
    count, fresh = len(rows), power is None
    outs = [((ROWS, 128), F32)] * count + [((128, NB * COLS), BF16)] * fresh
    return local(
        lambda *refs: scores_kernel(count, fresh, *refs), "partial_scores", outs, [],
        [*rows, *pens, *blocks] + ([] if fresh else [power]), 12,
    )


def sum_kernel(*refs):
    refs[-1][...] = refs[0][...] + refs[1][...] + refs[2][...]


def posterior_kernel(*refs):
    out = refs[-1]
    total = refs[0][...]
    for other in refs[1:-1]:
        total = total + other[...]
    total = total.reshape(SHIFTS, P_DEV, 128)
    peak = jnp.max(jnp.max(total, axis=0), axis=1, keepdims=True)
    expo = jnp.exp(total - peak[None])
    norm = jnp.sum(jnp.sum(expo, axis=0), axis=1, keepdims=True)
    share = (expo / norm[None]).reshape(ROWS, 128)
    out[...] = share.T.astype(BF16)


def make_posterior(parts):
    (out,) = local(posterior_kernel, "posterior", [((128, ROWS), BF16)], [], parts, 4)
    return out


def accum_kernel(part, member_ref, x_ref, *refs):
    rows, posts, outs = refs[:G], refs[G : 2 * G], refs[2 * G :]
    along_y = (member_ref[0] & 1) == part
    high = x_ref[0] >> 1

    @pl.loop(0, NB)
    def _(block):
        sums = []
        for half in range(2):
            start = pl.multiple_of(block * 2 * COLS + half * COLS + part * HALF, HALF)
            total = jnp.dot(posts[0][...], rows[0][:, pl.ds(start, HALF)], preferred_element_type=F32)
            for n in range(1, G):
                total = total + jnp.dot(
                    posts[n][...], rows[n][:, pl.ds(start, HALF)], preferred_element_type=F32
                )
            sums.append(total)
        spot = pl.ds(pl.multiple_of(block * HALF, HALF), HALF)
        for n, out in enumerate(outs):
            upper = high ^ (n >> 1) == 1
            for group in range(4):
                at = n * 32 + (group >> 1) * 16
                for_y = sums[group & 1][at : at + 16]
                at = group * 32 + (n & 1) * 16
                for_x = jnp.where(upper, sums[1][at : at + 16], sums[0][at : at + 16])
                out[group * 16 : (group + 1) * 16, spot] = jnp.where(along_y, for_y, for_x).astype(BF16)


def make_accum(part, member, x_at, rows, posts):
    return local(
        lambda *refs: accum_kernel(part, *refs), "weighted_sums", [((64, NB * HALF), BF16)] * 4,
        [member, x_at], [*rows, *posts], 8,
    )


def added(values):
    total = values[0].astype(F32)
    for value in values[1:]:
        total = total + value.astype(F32)
    return total


PIECES = [((16, NB * HALF), F32)] + [((16, NB * HALF), BF16)] * 3


def turn_kernel(part, member_ref, x_ref, *refs):
    along_y = (member_ref[0] & 1) == part
    for n, out in enumerate(refs[4:]):
        group = jnp.where(along_y, (n & 1) * 2 + ((x_ref[0] >> 1) ^ (n >> 1)), n)
        mine = pl.ds(pl.multiple_of(group * 16, 16), 16)
        out[...] = added([ref[mine, :] for ref in refs[:4]]).astype(out.dtype)


def make_turn(part, member, x_at, values):
    return local(
        lambda *refs: turn_kernel(part, *refs), "turned_sums", PIECES, [member, x_at], values, 4
    )


def joined_kernel(block_ref, *refs):
    for n, out in enumerate(refs[8:]):
        spot = pl.ds(pl.multiple_of((block_ref[0] ^ n) * HALF, HALF), HALF)
        out[:, :HALF] = added([ref[:, spot] for ref in refs[:4]]).astype(out.dtype)
        out[:, HALF:] = added([ref[:, spot] for ref in refs[4:8]]).astype(out.dtype)


def after(value, *others):
    return lax.optimization_barrier((value, *others))[0]


def per_device(refs, particles, shift_ids, wedge, defocus, inv_sigma):
    dom = lax.axis_index("dom")
    x_at = (dom // 16) * 2 + lax.axis_index("blk") % 2
    place = [value.astype(jnp.int32).reshape(1) for value in (dom % G, (dom % 16) // G, x_at)]
    member, block, x_at = place
    geo = jnp.asarray(geometry())

    chunks = split_particles(place, particles, shift_ids, wedge, defocus, inv_sigma)
    got, gathered, rows, pens = {}, {}, {}, {}
    got[2] = send(chunks[2], partners(2))
    got[1] = send(chunks[1], partners(1))
    own = own_columns(member, refs, chunks[2])
    gathered[0, 0] = own
    gathered[1, 0] = send(own, flips(y=1))
    gathered[3, 0] = send(own, flips(y=3))
    gathered[0, 1] = send(own, flips(x=1))
    table, geo = make_table(member, geo)
    rows[0], pens[0] = make_rows(member, chunks[0], geo, table)
    wave = [got[1], gathered[1, 0], gathered[3, 0], gathered[0, 1], rows[0]]
    gathered[1, 1] = send(after(gathered[1, 0], *wave), flips(x=1))
    gathered[3, 1] = send(after(gathered[3, 0], *wave), flips(x=3))
    gathered[2, 1] = send(after(gathered[0, 1], *wave), flips(y=2))
    gathered[2, 0] = send(after(gathered[1, 0], *wave), flips(y=3))
    got[3] = send(after(chunks[3], *wave, got[2]), partners(3))
    rows[1], pens[1] = make_rows(member, after(got[1], *wave, got[2]), geo, table)
    rows[2], pens[2] = make_rows(member, after(got[2], rows[1]), geo, table)
    rows[3], pens[3] = make_rows(member, after(got[3], rows[2]), geo, table)
    blocks = [gathered[ky, kx] for ky in range(Y) for kx in range(2)]

    second, power = make_scores([rows[2]], [after(pens[2], rows[3])], blocks)
    (third,) = make_scores([rows[3]], [after(pens[3], second)], blocks, power)
    mine, other = make_scores([rows[0], rows[1]], [after(pens[0], third), pens[1]], blocks, power)
    near = [mine, send(second, partners(2)), send(third, partners(3))]
    (near,) = local(sum_kernel, "score_sums", [((ROWS, 128), F32)], [], near, 4)
    posterior = make_posterior([near, send(other, partners(1))])
    posts = {n: send(posterior, partners(n)) for n in (3, 2, 1)}
    posts = [posterior] + [posts[n] for n in range(1, G)]
    rows = [rows[n] for n in range(G)]

    first = make_accum(0, member, x_at, rows, posts)
    first = [first[0]] + [send(first[n], crossed(n, 0)) for n in (2, 1, 3)]
    second = make_accum(1, member, x_at, rows, posts)
    second = [second[0]] + [send(second[n], crossed(n, 1)) for n in (2, 1, 3)]
    first = make_turn(0, member, x_at, first)
    first = [first[0]] + [send(first[n], crossed(n, 1)) for n in (2, 1, 3)]
    second = make_turn(1, member, x_at, second)
    second = [second[0]] + [send(second[n], crossed(n, 0)) for n in (2, 1, 3)]
    outs = [((16, COLS), F32)] + [((16, COLS), BF16)] * (NB - 1)
    ends = local(joined_kernel, "joined_sums", outs, [block], [*first, *second], 4)
    return added([ends[0]] + [send(ends[n], flips(z=n * (G // 2))) for n in (2, 1, 3)])


def solution(mesh):
    return jax.shard_map(
        per_device,
        mesh=mesh,
        in_specs=(
            P("blk", None),
            P(("blk", "dom"), None),
            P(("blk", "dom"), None),
            P(("blk", "dom"), None),
            P(("blk", "dom"), None),
            P(("blk", "dom")),
        ),
        out_specs=P("blk", "dom"),
        check_vma=False,
    )
```

```python
import math

import jax
import jax.numpy as jnp
import numpy as np
from jax import lax
from jax.experimental import pallas as pl
from jax.experimental.pallas import tpu as pltpu
from jax.sharding import PartitionSpec as P

BOX = 32
TILTS = 32
SHIFTS = 8
P_DEV = 32
Y, X, Z = 4, 4, 8
COLS = 1024
HALF = 512
G = 4
NB = 16 // G
ROWS = P_DEV * SHIFTS
WIDTH = NB * 2 * COLS
EXTRA = 384
AXES = ("blk", "dom")
F32, BF16 = jnp.float32, jnp.bfloat16
NT = (((1,), (1,)), ((), ()))
MIB = 1 << 20


def linear(y, x, z, core):
    y, x, z = y % Y, x % X, z % Z
    return (y * 2 + x % 2) * 32 + (x // 2) * 16 + z * 2 + core


def flips(y=0, x=0, z=0):
    return [
        (linear(i, j, k, c), linear(i ^ y, j ^ x, k ^ z, c))
        for i in range(Y) for j in range(X) for k in range(Z) for c in range(2)
    ]


def crossed(n, core):
    return [
        (linear(i, j, k, c), linear(i ^ (n if c == core else 0), j ^ (0 if c == core else n), k, c))
        for i in range(Y) for j in range(X) for k in range(Z) for c in range(2)
    ]


def partners(k):
    return [
        (linear(y, x, z, c), linear(y, x, z ^ (k >> 1), c ^ (k & 1)))
        for y in range(Y) for x in range(X) for z in range(Z) for c in range(2)
    ]


def send(value, pairs):
    return lax.ppermute(value, AXES, pairs)


def geometry():
    position = np.arange(TILTS * HALF)
    tilt, within = position // HALF, position % HALF
    radial = (within // BOX).astype(np.float64)
    lateral = (within % BOX - BOX // 2).astype(np.float64)
    angle = (tilt - 0.5 * (TILTS - 1)) * (2.0 / TILTS)
    shell = (radial * radial + lateral * lateral) / (0.25 * BOX * BOX)
    zero = np.zeros_like(shell)
    table = np.stack([radial * np.cos(angle), lateral, radial * np.sin(angle), shell] + [zero] * 4)
    return table.reshape(8, 16, COLS).transpose(1, 0, 2).astype(np.float32)


def fold(turns):
    turns = turns - jnp.floor(turns + 0.5)
    far = jnp.abs(turns) > 0.25
    near = jnp.where(far, jnp.where(turns > 0, 0.5, -0.5) - turns, turns)
    return near * (2.0 * math.pi), far


def series(square, terms):
    total = jnp.full_like(square, terms[-1])
    for term in terms[-2::-1]:
        total = total * square + term
    return total


SIN_TERMS = [(-1) ** n / math.factorial(2 * n + 1) for n in range(6)]
COS_TERMS = [(-1) ** n / math.factorial(2 * n) for n in range(7)]


def sine_turns(turns):
    angle, _ = fold(turns)
    return angle * series(angle * angle, SIN_TERMS)


def held(value):
    return pltpu.with_memory_space_constraint(value, pltpu.VMEM)


SCALARS = pl.BlockSpec(memory_space=pltpu.SMEM)
WHOLE = pl.BlockSpec(memory_space=pltpu.VMEM)
PLACED = pl.BlockSpec(memory_space=pl.ANY)


def local(kernel, name, outs, scalars, arrays, limit, placed=0, scratch=()):
    return pl.pallas_call(
        kernel,
        in_specs=[SCALARS] * len(scalars) + [PLACED] * placed + [WHOLE] * (len(arrays) - placed),
        out_specs=[WHOLE] * len(outs),
        out_shape=[pltpu.VMEM(shape, kind) for shape, kind in outs],
        scratch_shapes=list(scratch),
        cost_estimate=pl.CostEstimate(flops=0, bytes_accessed=0, transcendentals=0),
        compiler_params=pltpu.CompilerParams(vmem_limit_bytes=limit * MIB),
        name=name,
    )(
        *scalars,
        *[pltpu.with_memory_space_constraint(value, pltpu.HBM) for value in arrays[:placed]],
        *[held(value) for value in arrays[placed:]],
    )


def table_kernel(member_ref, geo_ref, out_ref, picked_ref, sems):
    copies = [
        pltpu.make_async_copy(geo_ref.at[block * G + member_ref[0]], picked_ref.at[block], sems.at[block])
        for block in range(NB)
    ]
    for copy in copies:
        copy.start()
    ids = lax.broadcasted_iota(jnp.int32, (128, 1), 0).astype(F32)
    high = jnp.floor((ids + 0.5) * (1 / 25))
    middle = jnp.floor((ids - 25 * high + 0.5) * (1 / 5))
    low = ids - 25 * high - 5 * middle
    move_x, move_y, move_z = ((digit - 2.0) * (0.5 / BOX) for digit in (high, middle, low))
    for copy in copies:
        copy.wait()

    @pl.loop(0, NB)
    def _(block):
        geo = picked_ref[block]
        for tilt in range(2):
            part = geo[:, tilt * HALF : (tilt + 1) * HALF]
            turns = move_x * part[0:1] + move_y * part[1:2] + move_z * part[2:3]
            angle, far = fold(turns)
            square = angle * angle
            sine = angle * series(square, SIN_TERMS)
            cosine = series(square, COS_TERMS)
            cosine = jnp.where(far, -cosine, cosine)
            for at, values in enumerate((cosine, sine)):
                high = values.astype(BF16)
                low = (values - high.astype(F32)).astype(BF16)
                spot = pl.multiple_of(block * 2 * COLS + tilt * COLS + at * HALF, HALF)
                out_ref[0:128, pl.ds(spot, HALF)] = high
                out_ref[128:256, pl.ds(spot, HALF)] = low


def make_table(member, geo):
    return local(
        table_kernel, "phase_table", [((256, WIDTH), BF16), ((NB, 8, COLS), F32)], [member], [geo], 8,
        placed=1, scratch=[pltpu.SemaphoreType.DMA((NB,))],
    )


def column(part, block, who):
    return pl.ds(pl.multiple_of((part * 16 + block * G + who) * COLS, COLS), COLS)


def pieces_of(source, out, who, sems, base):
    return [
        pltpu.make_async_copy(
            source.at[:, column(part, block, who)],
            out.at[:, pl.ds((block * 2 + part) * COLS, COLS)],
            sems.at[base + block * 2 + part],
        )
        for block in range(NB) for part in range(2)
    ]


def own_kernel(member_ref, source, after, out, sems):
    copies = pieces_of(source, out, member_ref[0], sems, 0)
    for copy in copies:
        copy.start()
    for copy in copies:
        copy.wait()


def own_columns(member, refs, after):
    (own,) = local(
        own_kernel, "own_references", [((16, WIDTH), BF16)], [member], [refs, after], 4,
        placed=1, scratch=[pltpu.SemaphoreType.DMA((2 * NB,))],
    )
    return own


def parts_of(values):
    high = values.astype(BF16)
    rest = values - high.astype(F32)
    middle = rest.astype(BF16)
    return high, middle, (rest - middle.astype(F32)).astype(BF16)


def turned_over(values):
    rows, columns = values.shape
    same = lax.broadcasted_iota(jnp.int32, (columns, columns), 0) == lax.broadcasted_iota(
        jnp.int32, (columns, columns), 1
    )
    return sum(
        lax.dot_general(same.astype(BF16), part, NT, preferred_element_type=F32)
        for part in parts_of(values)
    )


def split_kernel(member_ref, block_ref, x_ref, source, ids, wedge, focus, sigma, *refs):
    outs, (ids_in, wedge_in, focus_in, sigma_in, sems, more) = refs[:G], refs[G:]
    copies = []
    for n in (2, 1, 3, 0):
        copies += pieces_of(source, outs[n], member_ref[0] ^ n, sems, n * 2 * NB)
    settings = [
        pltpu.make_async_copy(at, to, more.at[n])
        for n, (at, to) in enumerate(
            ((ids, ids_in), (wedge, wedge_in), (focus, focus_in), (sigma, sigma_in))
        )
    ]
    for copy in copies + settings:
        copy.start()
    for copy in settings:
        copy.wait()
    first = jnp.concatenate(
        [ids_in[...].astype(F32), jnp.broadcast_to(sigma_in[...], (8, P_DEV))], axis=0
    )
    info = jnp.concatenate(
        [
            turned_over(first),
            wedge_in[...].astype(F32),
            focus_in[...],
            jnp.zeros((P_DEV, 128 - 16 - 2 * TILTS), F32),
        ],
        axis=1,
    )
    for spot, piece in enumerate(parts_of(info)):
        for out in outs:
            out[:, WIDTH + spot * 128 : WIDTH + (spot + 1) * 128] = piece
    for copy in copies:
        copy.wait()


def split_particles(place, particles, shift_ids, wedge, defocus, inv_sigma):
    return local(
        split_kernel, "split_particles", [((P_DEV, WIDTH + EXTRA), BF16)] * G, place,
        [particles, shift_ids.T, wedge, defocus, inv_sigma[None]], 4, placed=5,
        scratch=[
            pltpu.VMEM((SHIFTS, P_DEV), jnp.int32),
            pltpu.VMEM((P_DEV, TILTS), jnp.int32),
            pltpu.VMEM((P_DEV, TILTS), F32),
            pltpu.VMEM((1, P_DEV), F32),
            pltpu.SemaphoreType.DMA((G * 2 * NB,)),
            pltpu.SemaphoreType.DMA((4,)),
        ],
    )


def rows_kernel(member_ref, x_ref, geo_ref, table_ref, rows_ref, pen_ref):
    info = sum(x_ref[:, WIDTH + n * 128 : WIDTH + (n + 1) * 128].astype(F32) for n in range(3))
    lane = lax.broadcasted_iota(jnp.int32, (ROWS, 256), 1) & 127
    ids = jnp.concatenate([info[:, s : s + 1] for s in range(SHIFTS)], axis=0)
    pick = (ids == lane.astype(F32)).astype(BF16)
    sigma = info[:, SHIFTS : SHIFTS + 1]
    small = lax.broadcasted_iota(jnp.int32, (P_DEV, 128), 1)

    @pl.loop(0, NB)
    def _(block):
        first = 2 * (block * G + member_ref[0]) + 16
        start = pl.multiple_of(block * 2 * COLS, 2 * COLS)
        for tilt in range(2):
            kept = jnp.sum(jnp.where(small == first + tilt, info, 0.0), axis=1, keepdims=True)
            focus = jnp.sum(jnp.where(small == first + tilt + TILTS, info, 0.0), axis=1, keepdims=True)
            shell = geo_ref[block, 3:4, tilt * HALF : (tilt + 1) * HALF]
            transfer = -sine_turns((4.0 * focus * shell + 0.1) * (0.5 / math.pi))
            weight = kept * transfer * sigma
            spot = pl.multiple_of(block * COLS + tilt * HALF, HALF)
            pen_ref[:, pl.ds(spot, HALF)] = (0.5 * weight * transfer).astype(BF16)
            lower, upper = pl.ds(start + tilt * HALF, HALF), pl.ds(start + COLS + tilt * HALF, HALF)
            real = (weight * x_ref[:, lower].astype(F32))[None]
            imag = (weight * x_ref[:, upper].astype(F32))[None]
            turned = jnp.dot(
                pick, table_ref[:, pl.ds(start + tilt * COLS, COLS)], preferred_element_type=F32
            ).reshape(SHIFTS, P_DEV, COLS)
            cosine, sine = turned[:, :, :HALF], turned[:, :, HALF:]
            rows_ref[:, lower] = (real * cosine + imag * sine).reshape(ROWS, HALF).astype(BF16)
            rows_ref[:, upper] = (imag * cosine - real * sine).reshape(ROWS, HALF).astype(BF16)


def make_rows(member, x, geo, table):
    return local(
        rows_kernel, "shifted_rows", [((ROWS, WIDTH), BF16), ((P_DEV, NB * COLS), BF16)], [member],
        [x, geo, table], 12,
    )


ARRIVAL = [(2, 1), (2, 0), (1, 1), (3, 1), (0, 1), (1, 0), (3, 0), (0, 0)]


def scores_kernel(count, fresh, *refs):
    blocks = refs[2 * count : 2 * count + 8]
    outs = refs[2 * count + 8 :]
    stacked = dict(zip(ARRIVAL, blocks))
    stacked = jnp.concatenate([stacked[at][...] for at in sorted(ARRIVAL)], axis=0)
    if fresh:
        for block in range(NB):
            start = block * 2 * COLS
            real = stacked[:, start : start + COLS].astype(F32)
            imag = stacked[:, start + COLS : start + 2 * COLS].astype(F32)
            outs[-1][:, block * COLS : (block + 1) * COLS] = (real * real + imag * imag).astype(BF16)
        power, outs = outs[-1][...], outs[:-1]
    else:
        power, outs = outs[0][...], outs[1:]
    pens = jnp.concatenate([pen[...] for pen in refs[count : 2 * count]], axis=0)
    rows = jnp.concatenate([row[...] for row in refs[:count]], axis=0)
    energy = lax.dot_general(pens, power, NT, preferred_element_type=F32)
    total = lax.dot_general(rows, stacked, NT, preferred_element_type=F32)
    for n, out in enumerate(outs):
        mine = total[n * ROWS : (n + 1) * ROWS].reshape(SHIFTS, P_DEV, 128)
        out[...] = (mine - energy[None, n * P_DEV : (n + 1) * P_DEV]).reshape(ROWS, 128)


def make_scores(rows, pens, blocks, power=None):
    count, fresh = len(rows), power is None
    outs = [((ROWS, 128), F32)] * count + [((128, NB * COLS), BF16)] * fresh
    return local(
        lambda *refs: scores_kernel(count, fresh, *refs), "partial_scores", outs, [],
        [*rows, *pens, *blocks] + ([] if fresh else [power]), 12,
    )


def sum_kernel(*refs):
    refs[-1][...] = refs[0][...] + refs[1][...] + refs[2][...]


def posterior_kernel(*refs):
    out = refs[-1]
    total = refs[0][...]
    for other in refs[1:-1]:
        total = total + other[...]
    total = total.reshape(SHIFTS, P_DEV, 128)
    peak = jnp.max(jnp.max(total, axis=0), axis=1, keepdims=True)
    expo = jnp.exp(total - peak[None])
    norm = jnp.sum(jnp.sum(expo, axis=0), axis=1, keepdims=True)
    share = (expo / norm[None]).reshape(ROWS, 128)
    out[...] = share.T.astype(BF16)


def make_posterior(parts):
    (out,) = local(posterior_kernel, "posterior", [((128, ROWS), BF16)], [], parts, 4)
    return out


def accum_kernel(part, member_ref, x_ref, *refs):
    rows, posts, outs = refs[:G], refs[G : 2 * G], refs[2 * G :]
    along_y = (member_ref[0] & 1) == part
    high = x_ref[0] >> 1

    @pl.loop(0, NB)
    def _(block):
        sums = []
        for half in range(2):
            start = pl.multiple_of(block * 2 * COLS + half * COLS + part * HALF, HALF)
            total = jnp.dot(posts[0][...], rows[0][:, pl.ds(start, HALF)], preferred_element_type=F32)
            for n in range(1, G):
                total = total + jnp.dot(
                    posts[n][...], rows[n][:, pl.ds(start, HALF)], preferred_element_type=F32
                )
            sums.append(total)
        spot = pl.ds(pl.multiple_of(block * HALF, HALF), HALF)
        for n, out in enumerate(outs):
            upper = high ^ (n >> 1) == 1
            for group in range(4):
                at = n * 32 + (group >> 1) * 16
                for_y = sums[group & 1][at : at + 16]
                at = group * 32 + (n & 1) * 16
                for_x = jnp.where(upper, sums[1][at : at + 16], sums[0][at : at + 16])
                out[group * 16 : (group + 1) * 16, spot] = jnp.where(along_y, for_y, for_x).astype(BF16)


def make_accum(part, member, x_at, rows, posts):
    return local(
        lambda *refs: accum_kernel(part, *refs), "weighted_sums", [((64, NB * HALF), BF16)] * 4,
        [member, x_at], [*rows, *posts], 8,
    )


def added(values):
    total = values[0].astype(F32)
    for value in values[1:]:
        total = total + value.astype(F32)
    return total


PIECES = [((16, NB * HALF), F32)] + [((16, NB * HALF), BF16)] * 3


def turn_kernel(part, member_ref, x_ref, *refs):
    along_y = (member_ref[0] & 1) == part
    for n, out in enumerate(refs[4:]):
        group = jnp.where(along_y, (n & 1) * 2 + ((x_ref[0] >> 1) ^ (n >> 1)), n)
        mine = pl.ds(pl.multiple_of(group * 16, 16), 16)
        out[...] = added([ref[mine, :] for ref in refs[:4]]).astype(out.dtype)


def make_turn(part, member, x_at, values):
    return local(
        lambda *refs: turn_kernel(part, *refs), "turned_sums", PIECES, [member, x_at], values, 4
    )


def joined_kernel(block_ref, *refs):
    for n, out in enumerate(refs[8:]):
        spot = pl.ds(pl.multiple_of((block_ref[0] ^ n) * HALF, HALF), HALF)
        out[:, :HALF] = added([ref[:, spot] for ref in refs[:4]]).astype(out.dtype)
        out[:, HALF:] = added([ref[:, spot] for ref in refs[4:8]]).astype(out.dtype)


def after(value, *others):
    return lax.optimization_barrier((value, *others))[0]


def per_device(refs, particles, shift_ids, wedge, defocus, inv_sigma):
    dom = lax.axis_index("dom")
    x_at = (dom // 16) * 2 + lax.axis_index("blk") % 2
    place = [value.astype(jnp.int32).reshape(1) for value in (dom % G, (dom % 16) // G, x_at)]
    member, block, x_at = place
    geo = jnp.asarray(geometry())

    chunks = split_particles(place, particles, shift_ids, wedge, defocus, inv_sigma)
    got, gathered, rows, pens = {}, {}, {}, {}
    got[2] = send(chunks[2], partners(2))
    got[1] = send(chunks[1], partners(1))
    own = own_columns(member, refs, chunks[2])
    gathered[0, 0] = own
    gathered[1, 0] = send(own, flips(y=1))
    gathered[3, 0] = send(own, flips(y=3))
    gathered[0, 1] = send(own, flips(x=1))
    table, geo = make_table(member, geo)
    rows[0], pens[0] = make_rows(member, chunks[0], geo, table)
    wave = [got[1], gathered[1, 0], gathered[3, 0], gathered[0, 1], rows[0]]
    gathered[2, 1] = send(after(gathered[0, 1], *wave), flips(y=2))
    gathered[2, 0] = send(after(gathered[1, 0], *wave), flips(y=3))
    gathered[1, 1] = send(after(gathered[1, 0], *wave), flips(x=1))
    gathered[3, 1] = send(after(gathered[3, 0], *wave), flips(x=3))
    got[3] = send(after(chunks[3], got[2], *wave), partners(3))
    rows[2], pens[2] = make_rows(member, after(got[2], *wave), geo, table)
    rows[1], pens[1] = make_rows(member, after(got[1], rows[2]), geo, table)
    blocks = [gathered[at] for at in ARRIVAL]

    second, power = make_scores([rows[2]], [after(pens[2], rows[1])], blocks)
    rows[3], pens[3] = make_rows(member, after(got[3], second), geo, table)
    (third,) = make_scores([rows[3]], [after(pens[3], second)], blocks, power)
    mine, other = make_scores([rows[0], rows[1]], [after(pens[0], third), pens[1]], blocks, power)
    near = [mine, send(second, partners(2)), send(third, partners(3))]
    (near,) = local(sum_kernel, "score_sums", [((ROWS, 128), F32)], [], near, 4)
    posterior = make_posterior([near, send(other, partners(1))])
    posts = {n: send(posterior, partners(n)) for n in (3, 2, 1)}
    posts = [posterior] + [posts[n] for n in range(1, G)]
    rows = [rows[n] for n in range(G)]

    first = make_accum(0, member, x_at, rows, posts)
    first = [first[0]] + [send(first[n], crossed(n, 0)) for n in (2, 1, 3)]
    second = make_accum(1, member, x_at, rows, posts)
    second = [second[0]] + [send(second[n], crossed(n, 1)) for n in (2, 1, 3)]
    first = make_turn(0, member, x_at, first)
    first = [first[0]] + [send(first[n], crossed(n, 1)) for n in (2, 1, 3)]
    second = make_turn(1, member, x_at, second)
    second = [second[0]] + [send(second[n], crossed(n, 0)) for n in (2, 1, 3)]
    outs = [((16, COLS), F32)] + [((16, COLS), BF16)] * (NB - 1)
    ends = local(joined_kernel, "joined_sums", outs, [block], [*first, *second], 4)
    return added([ends[0]] + [send(ends[n], flips(z=n * (G // 2))) for n in (2, 1, 3)])


def solution(mesh):
    return jax.shard_map(
        per_device,
        mesh=mesh,
        in_specs=(
            P("blk", None),
            P(("blk", "dom"), None),
            P(("blk", "dom"), None),
            P(("blk", "dom"), None),
            P(("blk", "dom"), None),
            P(("blk", "dom")),
        ),
        out_specs=P("blk", "dom"),
        check_vma=False,
    )
```

```python
import math

import jax
import jax.numpy as jnp
import numpy as np
from jax import lax
from jax.experimental import pallas as pl
from jax.experimental.pallas import tpu as pltpu
from jax.sharding import PartitionSpec as P

BOX = 32
TILTS = 32
SHIFTS = 8
P_DEV = 32
Y, X, Z = 4, 4, 8
COLS = 1024
HALF = 512
G = 4
NB = 16 // G
ROWS = P_DEV * SHIFTS
WIDTH = NB * 2 * COLS
EXTRA = 384
AXES = ("blk", "dom")
F32, BF16 = jnp.float32, jnp.bfloat16
NT = (((1,), (1,)), ((), ()))
MIB = 1 << 20


def linear(y, x, z, core):
    y, x, z = y % Y, x % X, z % Z
    return (y * 2 + x % 2) * 32 + (x // 2) * 16 + z * 2 + core


def flips(y=0, x=0, z=0):
    return [
        (linear(i, j, k, c), linear(i ^ y, j ^ x, k ^ z, c))
        for i in range(Y) for j in range(X) for k in range(Z) for c in range(2)
    ]


def crossed(n, core):
    return [
        (linear(i, j, k, c), linear(i ^ (n if c == core else 0), j ^ (0 if c == core else n), k, c))
        for i in range(Y) for j in range(X) for k in range(Z) for c in range(2)
    ]


def second_hop():
    return [
        (linear(i, j, k, c), linear(i ^ (1 if c else 3), j, k, c))
        for i in range(Y) for j in range(X) for k in range(Z) for c in range(2)
    ]


def partners(k):
    return [
        (linear(y, x, z, c), linear(y, x, z ^ (k >> 1), c ^ (k & 1)))
        for y in range(Y) for x in range(X) for z in range(Z) for c in range(2)
    ]


def send(value, pairs):
    return lax.ppermute(value, AXES, pairs)


def geometry():
    position = np.arange(TILTS * HALF)
    tilt, within = position // HALF, position % HALF
    radial = (within // BOX).astype(np.float64)
    lateral = (within % BOX - BOX // 2).astype(np.float64)
    angle = (tilt - 0.5 * (TILTS - 1)) * (2.0 / TILTS)
    shell = (radial * radial + lateral * lateral) / (0.25 * BOX * BOX)
    zero = np.zeros_like(shell)
    table = np.stack([radial * np.cos(angle), lateral, radial * np.sin(angle), shell] + [zero] * 4)
    return table.reshape(8, 16, COLS).transpose(1, 0, 2).astype(np.float32)


def fold(turns):
    turns = turns - jnp.floor(turns + 0.5)
    far = jnp.abs(turns) > 0.25
    near = jnp.where(far, jnp.where(turns > 0, 0.5, -0.5) - turns, turns)
    return near * (2.0 * math.pi), far


def series(square, terms):
    total = jnp.full_like(square, terms[-1])
    for term in terms[-2::-1]:
        total = total * square + term
    return total


SIN_TERMS = [(-1) ** n / math.factorial(2 * n + 1) for n in range(6)]
COS_TERMS = [(-1) ** n / math.factorial(2 * n) for n in range(7)]


def sine_turns(turns):
    angle, _ = fold(turns)
    return angle * series(angle * angle, SIN_TERMS)


def held(value):
    return pltpu.with_memory_space_constraint(value, pltpu.VMEM)


SCALARS = pl.BlockSpec(memory_space=pltpu.SMEM)
WHOLE = pl.BlockSpec(memory_space=pltpu.VMEM)
PLACED = pl.BlockSpec(memory_space=pl.ANY)


def local(kernel, name, outs, scalars, arrays, limit, placed=0, scratch=()):
    return pl.pallas_call(
        kernel,
        in_specs=[SCALARS] * len(scalars) + [PLACED] * placed + [WHOLE] * (len(arrays) - placed),
        out_specs=[WHOLE] * len(outs),
        out_shape=[pltpu.VMEM(shape, kind) for shape, kind in outs],
        scratch_shapes=list(scratch),
        cost_estimate=pl.CostEstimate(flops=0, bytes_accessed=0, transcendentals=0),
        compiler_params=pltpu.CompilerParams(vmem_limit_bytes=limit * MIB),
        name=name,
    )(
        *scalars,
        *[pltpu.with_memory_space_constraint(value, pltpu.HBM) for value in arrays[:placed]],
        *[held(value) for value in arrays[placed:]],
    )


def table_kernel(member_ref, geo_ref, out_ref, picked_ref, sems):
    copies = [
        pltpu.make_async_copy(geo_ref.at[block * G + member_ref[0]], picked_ref.at[block], sems.at[block])
        for block in range(NB)
    ]
    for copy in copies:
        copy.start()
    ids = lax.broadcasted_iota(jnp.int32, (128, 1), 0).astype(F32)
    high = jnp.floor((ids + 0.5) * (1 / 25))
    middle = jnp.floor((ids - 25 * high + 0.5) * (1 / 5))
    low = ids - 25 * high - 5 * middle
    move_x, move_y, move_z = ((digit - 2.0) * (0.5 / BOX) for digit in (high, middle, low))
    for copy in copies:
        copy.wait()

    @pl.loop(0, NB)
    def _(block):
        geo = picked_ref[block]
        for tilt in range(2):
            part = geo[:, tilt * HALF : (tilt + 1) * HALF]
            turns = move_x * part[0:1] + move_y * part[1:2] + move_z * part[2:3]
            angle, far = fold(turns)
            square = angle * angle
            sine = angle * series(square, SIN_TERMS)
            cosine = series(square, COS_TERMS)
            cosine = jnp.where(far, -cosine, cosine)
            for at, values in enumerate((cosine, sine)):
                high = values.astype(BF16)
                low = (values - high.astype(F32)).astype(BF16)
                spot = pl.multiple_of(block * 2 * COLS + tilt * COLS + at * HALF, HALF)
                out_ref[0:128, pl.ds(spot, HALF)] = high
                out_ref[128:256, pl.ds(spot, HALF)] = low


def make_table(member, geo):
    return local(
        table_kernel, "phase_table", [((256, WIDTH), BF16), ((NB, 8, COLS), F32)], [member], [geo], 8,
        placed=1, scratch=[pltpu.SemaphoreType.DMA((NB,))],
    )


def column(part, block, who):
    return pl.ds(pl.multiple_of((part * 16 + block * G + who) * COLS, COLS), COLS)


def pieces_of(source, out, who, sems, base):
    return [
        pltpu.make_async_copy(
            source.at[:, column(part, block, who)],
            out.at[:, pl.ds((block * 2 + part) * COLS, COLS)],
            sems.at[base + block * 2 + part],
        )
        for block in range(NB) for part in range(2)
    ]


def own_kernel(member_ref, source, after, out, sems):
    copies = pieces_of(source, out, member_ref[0], sems, 0)
    for copy in copies:
        copy.start()
    for copy in copies:
        copy.wait()


def own_columns(member, refs, after):
    (own,) = local(
        own_kernel, "own_references", [((16, WIDTH), BF16)], [member], [refs, after], 4,
        placed=1, scratch=[pltpu.SemaphoreType.DMA((2 * NB,))],
    )
    return own


def relay_kernel(member_ref, one, other, out):
    @pl.when(member_ref[0] & 1 == 0)
    def _():
        out[...] = one[...]

    @pl.when(member_ref[0] & 1 == 1)
    def _():
        out[...] = other[...]


def pair_kernel(one, other, out):
    out[16:32] = one[...]
    out[0:16] = other[...]


def parts_of(values):
    high = values.astype(BF16)
    rest = values - high.astype(F32)
    middle = rest.astype(BF16)
    return high, middle, (rest - middle.astype(F32)).astype(BF16)


def turned_over(values):
    rows, columns = values.shape
    same = lax.broadcasted_iota(jnp.int32, (columns, columns), 0) == lax.broadcasted_iota(
        jnp.int32, (columns, columns), 1
    )
    return sum(
        lax.dot_general(same.astype(BF16), part, NT, preferred_element_type=F32)
        for part in parts_of(values)
    )


def split_kernel(member_ref, block_ref, x_ref, source, ids, wedge, focus, sigma, *refs):
    outs, (ids_in, wedge_in, focus_in, sigma_in, sems, more) = refs[:G], refs[G:]
    copies = []
    for n in (2, 1, 3, 0):
        copies += pieces_of(source, outs[n], member_ref[0] ^ n, sems, n * 2 * NB)
    settings = [
        pltpu.make_async_copy(at, to, more.at[n])
        for n, (at, to) in enumerate(
            ((ids, ids_in), (wedge, wedge_in), (focus, focus_in), (sigma, sigma_in))
        )
    ]
    for copy in copies + settings:
        copy.start()
    for copy in settings:
        copy.wait()
    first = jnp.concatenate(
        [ids_in[...].astype(F32), jnp.broadcast_to(sigma_in[...], (8, P_DEV))], axis=0
    )
    info = jnp.concatenate(
        [
            turned_over(first),
            wedge_in[...].astype(F32),
            focus_in[...],
            jnp.zeros((P_DEV, 128 - 16 - 2 * TILTS), F32),
        ],
        axis=1,
    )
    for spot, piece in enumerate(parts_of(info)):
        for out in outs:
            out[:, WIDTH + spot * 128 : WIDTH + (spot + 1) * 128] = piece
    for copy in copies:
        copy.wait()


def split_particles(place, particles, shift_ids, wedge, defocus, inv_sigma):
    return local(
        split_kernel, "split_particles", [((P_DEV, WIDTH + EXTRA), BF16)] * G, place,
        [particles, shift_ids.T, wedge, defocus, inv_sigma[None]], 4, placed=5,
        scratch=[
            pltpu.VMEM((SHIFTS, P_DEV), jnp.int32),
            pltpu.VMEM((P_DEV, TILTS), jnp.int32),
            pltpu.VMEM((P_DEV, TILTS), F32),
            pltpu.VMEM((1, P_DEV), F32),
            pltpu.SemaphoreType.DMA((G * 2 * NB,)),
            pltpu.SemaphoreType.DMA((4,)),
        ],
    )


def rows_kernel(member_ref, x_ref, geo_ref, table_ref, rows_ref, pen_ref):
    info = sum(x_ref[:, WIDTH + n * 128 : WIDTH + (n + 1) * 128].astype(F32) for n in range(3))
    lane = lax.broadcasted_iota(jnp.int32, (ROWS, 256), 1) & 127
    ids = jnp.concatenate([info[:, s : s + 1] for s in range(SHIFTS)], axis=0)
    pick = (ids == lane.astype(F32)).astype(BF16)
    sigma = info[:, SHIFTS : SHIFTS + 1]
    small = lax.broadcasted_iota(jnp.int32, (P_DEV, 128), 1)

    @pl.loop(0, NB)
    def _(block):
        first = 2 * (block * G + member_ref[0]) + 16
        start = pl.multiple_of(block * 2 * COLS, 2 * COLS)
        for tilt in range(2):
            kept = jnp.sum(jnp.where(small == first + tilt, info, 0.0), axis=1, keepdims=True)
            focus = jnp.sum(jnp.where(small == first + tilt + TILTS, info, 0.0), axis=1, keepdims=True)
            shell = geo_ref[block, 3:4, tilt * HALF : (tilt + 1) * HALF]
            transfer = -sine_turns((4.0 * focus * shell + 0.1) * (0.5 / math.pi))
            weight = kept * transfer * sigma
            spot = pl.multiple_of(block * COLS + tilt * HALF, HALF)
            pen_ref[:, pl.ds(spot, HALF)] = (0.5 * weight * transfer).astype(BF16)
            lower, upper = pl.ds(start + tilt * HALF, HALF), pl.ds(start + COLS + tilt * HALF, HALF)
            real = (weight * x_ref[:, lower].astype(F32))[None]
            imag = (weight * x_ref[:, upper].astype(F32))[None]
            turned = jnp.dot(
                pick, table_ref[:, pl.ds(start + tilt * COLS, COLS)], preferred_element_type=F32
            ).reshape(SHIFTS, P_DEV, COLS)
            cosine, sine = turned[:, :, :HALF], turned[:, :, HALF:]
            rows_ref[:, lower] = (real * cosine + imag * sine).reshape(ROWS, HALF).astype(BF16)
            rows_ref[:, upper] = (imag * cosine - real * sine).reshape(ROWS, HALF).astype(BF16)


def make_rows(member, x, geo, table):
    return local(
        rows_kernel, "shifted_rows", [((ROWS, WIDTH), BF16), ((P_DEV, NB * COLS), BF16)], [member],
        [x, geo, table], 12,
    )


ARRIVAL = [(2, 0), (1, 1), (3, 1), (0, 1), (1, 0), (3, 0), (0, 0)]


def scores_kernel(count, fresh, *refs):
    blocks = refs[2 * count : 2 * count + 7]
    outs = refs[2 * count + 7 :]
    stacked = dict(zip(ARRIVAL, blocks))
    stacked = jnp.concatenate([stacked[at][...] for at in sorted(ARRIVAL)], axis=0)
    if fresh:
        for block in range(NB):
            start = block * 2 * COLS
            real = stacked[:, start : start + COLS].astype(F32)
            imag = stacked[:, start + COLS : start + 2 * COLS].astype(F32)
            outs[-1][:, block * COLS : (block + 1) * COLS] = (real * real + imag * imag).astype(BF16)
        power, outs = outs[-1][...], outs[:-1]
    else:
        power, outs = outs[0][...], outs[1:]
    pens = jnp.concatenate([pen[...] for pen in refs[count : 2 * count]], axis=0)
    rows = jnp.concatenate([row[...] for row in refs[:count]], axis=0)
    energy = lax.dot_general(pens, power, NT, preferred_element_type=F32)
    total = lax.dot_general(rows, stacked, NT, preferred_element_type=F32)
    for n, out in enumerate(outs):
        mine = total[n * ROWS : (n + 1) * ROWS].reshape(SHIFTS, P_DEV, 128)
        out[...] = (mine - energy[None, n * P_DEV : (n + 1) * P_DEV]).reshape(ROWS, 128)


def make_scores(rows, pens, blocks, power=None):
    count, fresh = len(rows), power is None
    outs = [((ROWS, 128), F32)] * count + [((128, NB * COLS), BF16)] * fresh
    return local(
        lambda *refs: scores_kernel(count, fresh, *refs), "partial_scores", outs, [],
        [*rows, *pens, *blocks] + ([] if fresh else [power]), 12,
    )


def sum_kernel(*refs):
    refs[-1][...] = refs[0][...] + refs[1][...] + refs[2][...]


def posterior_kernel(*refs):
    out = refs[-1]
    total = refs[0][...]
    for other in refs[1:-1]:
        total = total + other[...]
    total = total.reshape(SHIFTS, P_DEV, 128)
    peak = jnp.max(jnp.max(total, axis=0), axis=1, keepdims=True)
    expo = jnp.exp(total - peak[None])
    norm = jnp.sum(jnp.sum(expo, axis=0), axis=1, keepdims=True)
    share = (expo / norm[None]).reshape(ROWS, 128)
    out[...] = share.T.astype(BF16)


def make_posterior(parts):
    (out,) = local(posterior_kernel, "posterior", [((128, ROWS), BF16)], [], parts, 4)
    return out


def accum_kernel(part, member_ref, x_ref, *refs):
    rows, posts, outs = refs[:G], refs[G : 2 * G], refs[2 * G :]
    along_y = (member_ref[0] & 1) == part
    high = x_ref[0] >> 1

    @pl.loop(0, NB)
    def _(block):
        sums = []
        for half in range(2):
            start = pl.multiple_of(block * 2 * COLS + half * COLS + part * HALF, HALF)
            total = jnp.dot(posts[0][...], rows[0][:, pl.ds(start, HALF)], preferred_element_type=F32)
            for n in range(1, G):
                total = total + jnp.dot(
                    posts[n][...], rows[n][:, pl.ds(start, HALF)], preferred_element_type=F32
                )
            sums.append(total)
        spot = pl.ds(pl.multiple_of(block * HALF, HALF), HALF)
        for n, out in enumerate(outs):
            upper = high ^ (n >> 1) == 1
            for group in range(4):
                at = n * 32 + (group >> 1) * 16
                for_y = sums[group & 1][at : at + 16]
                at = group * 32 + (n & 1) * 16
                for_x = jnp.where(upper, sums[1][at : at + 16], sums[0][at : at + 16])
                out[group * 16 : (group + 1) * 16, spot] = jnp.where(along_y, for_y, for_x).astype(BF16)


def make_accum(part, member, x_at, rows, posts):
    return local(
        lambda *refs: accum_kernel(part, *refs), "weighted_sums", [((64, NB * HALF), BF16)] * 4,
        [member, x_at], [*rows, *posts], 8,
    )


def added(values):
    total = values[0].astype(F32)
    for value in values[1:]:
        total = total + value.astype(F32)
    return total


PIECES = [((16, NB * HALF), F32)] + [((16, NB * HALF), BF16)] * 3


def turn_kernel(part, member_ref, x_ref, *refs):
    along_y = (member_ref[0] & 1) == part
    for n, out in enumerate(refs[4:]):
        group = jnp.where(along_y, (n & 1) * 2 + ((x_ref[0] >> 1) ^ (n >> 1)), n)
        mine = pl.ds(pl.multiple_of(group * 16, 16), 16)
        out[...] = added([ref[mine, :] for ref in refs[:4]]).astype(out.dtype)


def make_turn(part, member, x_at, values):
    return local(
        lambda *refs: turn_kernel(part, *refs), "turned_sums", PIECES, [member, x_at], values, 4
    )


def joined_kernel(block_ref, *refs):
    for n, out in enumerate(refs[8:]):
        spot = pl.ds(pl.multiple_of((block_ref[0] ^ n) * HALF, HALF), HALF)
        out[:, :HALF] = added([ref[:, spot] for ref in refs[:4]]).astype(out.dtype)
        out[:, HALF:] = added([ref[:, spot] for ref in refs[4:8]]).astype(out.dtype)


def after(value, *others):
    return lax.optimization_barrier((value, *others))[0]


def per_device(refs, particles, shift_ids, wedge, defocus, inv_sigma):
    dom = lax.axis_index("dom")
    x_at = (dom // 16) * 2 + lax.axis_index("blk") % 2
    place = [value.astype(jnp.int32).reshape(1) for value in (dom % G, (dom % 16) // G, x_at)]
    member, block, x_at = place
    geo = jnp.asarray(geometry())

    chunks = split_particles(place, particles, shift_ids, wedge, defocus, inv_sigma)
    got, gathered, rows, pens = {}, {}, {}, {}
    got[2] = send(chunks[2], partners(2))
    got[1] = send(chunks[1], partners(1))
    own = own_columns(member, refs, chunks[2])
    gathered[0, 0] = own
    gathered[1, 0] = send(own, flips(y=1))
    gathered[3, 0] = send(own, flips(y=3))
    gathered[0, 1] = send(own, flips(x=1))
    table, geo = make_table(member, geo)
    rows[0], pens[0] = make_rows(member, chunks[0], geo, table)
    wave = [got[1], gathered[1, 0], gathered[3, 0], gathered[0, 1], rows[0]]
    gathered[2, 1] = send(after(gathered[0, 1], *wave), flips(y=2))
    relayed = [gathered[1, 0], after(gathered[3, 0], *wave)]
    (relay,) = local(relay_kernel, "relay", [((16, WIDTH), BF16)], [member], relayed, 2)
    gathered[2, 0] = send(relay, second_hop())
    gathered[1, 1] = send(after(gathered[1, 0], relay), flips(x=1))
    gathered[3, 1] = send(after(gathered[3, 0], relay), flips(x=3))
    got[3] = send(after(chunks[3], got[2], *wave), partners(3))
    rows[2], pens[2] = make_rows(member, after(got[2], *wave), geo, table)
    rows[1], pens[1] = make_rows(member, after(got[1], rows[2]), geo, table)
    far = [gathered[2, 1], gathered[2, 0]]
    (gathered[2, 0],) = local(pair_kernel, "pair", [((32, WIDTH), BF16)], [], far, 2)
    blocks = [gathered[at] for at in ARRIVAL]

    second, power = make_scores([rows[2]], [after(pens[2], rows[1])], blocks)
    rows[3], pens[3] = make_rows(member, after(got[3], second), geo, table)
    (third,) = make_scores([rows[3]], [after(pens[3], second)], blocks, power)
    mine, other = make_scores([rows[0], rows[1]], [after(pens[0], third), pens[1]], blocks, power)
    near = [mine, send(second, partners(2)), send(third, partners(3))]
    (near,) = local(sum_kernel, "score_sums", [((ROWS, 128), F32)], [], near, 4)
    posterior = make_posterior([near, send(other, partners(1))])
    posts = {n: send(posterior, partners(n)) for n in (3, 2, 1)}
    posts = [posterior] + [posts[n] for n in range(1, G)]
    rows = [rows[n] for n in range(G)]

    first = make_accum(0, member, x_at, rows, posts)
    first = [first[0]] + [send(first[n], crossed(n, 0)) for n in (2, 1, 3)]
    second = make_accum(1, member, x_at, rows, posts)
    second = [second[0]] + [send(second[n], crossed(n, 1)) for n in (2, 1, 3)]
    first = make_turn(0, member, x_at, first)
    first = [first[0]] + [send(first[n], crossed(n, 1)) for n in (2, 1, 3)]
    second = make_turn(1, member, x_at, second)
    second = [second[0]] + [send(second[n], crossed(n, 0)) for n in (2, 1, 3)]
    outs = [((16, COLS), F32)] + [((16, COLS), BF16)] * (NB - 1)
    ends = local(joined_kernel, "joined_sums", outs, [block], [*first, *second], 4)
    return added([ends[0]] + [send(ends[n], flips(z=n * (G // 2))) for n in (2, 1, 3)])


def solution(mesh):
    return jax.shard_map(
        per_device,
        mesh=mesh,
        in_specs=(
            P("blk", None),
            P(("blk", "dom"), None),
            P(("blk", "dom"), None),
            P(("blk", "dom"), None),
            P(("blk", "dom"), None),
            P(("blk", "dom")),
        ),
        out_specs=P("blk", "dom"),
        check_vma=False,
    )
```

```python
import math

import jax
import jax.numpy as jnp
import numpy as np
from jax import lax
from jax.experimental import pallas as pl
from jax.experimental.pallas import tpu as pltpu
from jax.sharding import PartitionSpec as P

BOX = 32
TILTS = 32
SHIFTS = 8
P_DEV = 32
Y, X, Z = 4, 4, 8
COLS = 1024
HALF = 512
G = 4
NB = 16 // G
ROWS = P_DEV * SHIFTS
WIDTH = NB * 2 * COLS
EXTRA = 128
AXES = ("blk", "dom")
F32, BF16 = jnp.float32, jnp.bfloat16
NT = (((1,), (1,)), ((), ()))
MIB = 1 << 20


def linear(y, x, z, core):
    y, x, z = y % Y, x % X, z % Z
    return (y * 2 + x % 2) * 32 + (x // 2) * 16 + z * 2 + core


def flips(y=0, x=0, z=0):
    return [
        (linear(i, j, k, c), linear(i ^ y, j ^ x, k ^ z, c))
        for i in range(Y) for j in range(X) for k in range(Z) for c in range(2)
    ]


def crossed(n, core):
    return [
        (linear(i, j, k, c), linear(i ^ (n if c == core else 0), j ^ (0 if c == core else n), k, c))
        for i in range(Y) for j in range(X) for k in range(Z) for c in range(2)
    ]


def second_hop():
    return [
        (linear(i, j, k, c), linear(i ^ (1 if c else 3), j, k, c))
        for i in range(Y) for j in range(X) for k in range(Z) for c in range(2)
    ]


def partners(k):
    return [
        (linear(y, x, z, c), linear(y, x, z ^ (k >> 1), c ^ (k & 1)))
        for y in range(Y) for x in range(X) for z in range(Z) for c in range(2)
    ]


def send(value, pairs):
    return lax.ppermute(value, AXES, pairs)


def geometry():
    position = np.arange(TILTS * HALF)
    tilt, within = position // HALF, position % HALF
    radial = (within // BOX).astype(np.float64)
    lateral = (within % BOX - BOX // 2).astype(np.float64)
    angle = (tilt - 0.5 * (TILTS - 1)) * (2.0 / TILTS)
    shell = (radial * radial + lateral * lateral) / (0.25 * BOX * BOX)
    zero = np.zeros_like(shell)
    table = np.stack([radial * np.cos(angle), lateral, radial * np.sin(angle), shell] + [zero] * 4)
    return table.reshape(8, 16, COLS).transpose(1, 0, 2).astype(np.float32)


def fold(turns):
    turns = turns - jnp.floor(turns + 0.5)
    far = jnp.abs(turns) > 0.25
    near = jnp.where(far, jnp.where(turns > 0, 0.5, -0.5) - turns, turns)
    return near * (2.0 * math.pi), far


def series(square, terms):
    total = jnp.full_like(square, terms[-1])
    for term in terms[-2::-1]:
        total = total * square + term
    return total


SIN_TERMS = [(-1) ** n / math.factorial(2 * n + 1) for n in range(6)]
COS_TERMS = [(-1) ** n / math.factorial(2 * n) for n in range(7)]


def sine_turns(turns):
    angle, _ = fold(turns)
    return angle * series(angle * angle, SIN_TERMS)


def held(value):
    return pltpu.with_memory_space_constraint(value, pltpu.VMEM)


SCALARS = pl.BlockSpec(memory_space=pltpu.SMEM)
WHOLE = pl.BlockSpec(memory_space=pltpu.VMEM)
PLACED = pl.BlockSpec(memory_space=pl.ANY)


def local(kernel, name, outs, scalars, arrays, limit, placed=0, scratch=()):
    return pl.pallas_call(
        kernel,
        in_specs=[SCALARS] * len(scalars) + [PLACED] * placed + [WHOLE] * (len(arrays) - placed),
        out_specs=[WHOLE] * len(outs),
        out_shape=[pltpu.VMEM(shape, kind) for shape, kind in outs],
        scratch_shapes=list(scratch),
        cost_estimate=pl.CostEstimate(flops=0, bytes_accessed=0, transcendentals=0),
        compiler_params=pltpu.CompilerParams(vmem_limit_bytes=limit * MIB),
        name=name,
    )(
        *scalars,
        *[pltpu.with_memory_space_constraint(value, pltpu.HBM) for value in arrays[:placed]],
        *[held(value) for value in arrays[placed:]],
    )


def table_kernel(member_ref, geo_ref, out_ref, picked_ref, sems):
    copies = [
        pltpu.make_async_copy(geo_ref.at[block * G + member_ref[0]], picked_ref.at[block], sems.at[block])
        for block in range(NB)
    ]
    for copy in copies:
        copy.start()
    ids = lax.broadcasted_iota(jnp.int32, (128, 1), 0).astype(F32)
    high = jnp.floor((ids + 0.5) * (1 / 25))
    middle = jnp.floor((ids - 25 * high + 0.5) * (1 / 5))
    low = ids - 25 * high - 5 * middle
    move_x, move_y, move_z = ((digit - 2.0) * (0.5 / BOX) for digit in (high, middle, low))
    for copy in copies:
        copy.wait()

    @pl.loop(0, NB)
    def _(block):
        geo = picked_ref[block]
        for tilt in range(2):
            part = geo[:, tilt * HALF : (tilt + 1) * HALF]
            turns = move_x * part[0:1] + move_y * part[1:2] + move_z * part[2:3]
            angle, far = fold(turns)
            square = angle * angle
            sine = angle * series(square, SIN_TERMS)
            cosine = series(square, COS_TERMS)
            cosine = jnp.where(far, -cosine, cosine)
            for at, values in enumerate((cosine, sine)):
                high = values.astype(BF16)
                low = (values - high.astype(F32)).astype(BF16)
                spot = pl.multiple_of(block * 2 * COLS + tilt * COLS + at * HALF, HALF)
                out_ref[0:128, pl.ds(spot, HALF)] = high
                out_ref[128:256, pl.ds(spot, HALF)] = low


def make_table(member, geo):
    return local(
        table_kernel, "phase_table", [((256, WIDTH), BF16), ((NB, 8, COLS), F32)], [member], [geo], 8,
        placed=1, scratch=[pltpu.SemaphoreType.DMA((NB,))],
    )


def column(part, block, who):
    return pl.ds(pl.multiple_of((part * 16 + block * G + who) * COLS, COLS), COLS)


def pieces_of(source, out, who, sems, base):
    return [
        pltpu.make_async_copy(
            source.at[:, column(part, block, who)],
            out.at[:, pl.ds((block * 2 + part) * COLS, COLS)],
            sems.at[base + block * 2 + part],
        )
        for block in range(NB) for part in range(2)
    ]


def own_kernel(member_ref, source, after, out, sems):
    copies = pieces_of(source, out, member_ref[0], sems, 0)
    for copy in copies:
        copy.start()
    for copy in copies:
        copy.wait()


def own_columns(member, refs, after):
    (own,) = local(
        own_kernel, "own_references", [((16, WIDTH), BF16)], [member], [refs, after], 4,
        placed=1, scratch=[pltpu.SemaphoreType.DMA((2 * NB,))],
    )
    return own


def relay_kernel(member_ref, one, other, out):
    @pl.when(member_ref[0] & 1 == 0)
    def _():
        out[...] = one[...]

    @pl.when(member_ref[0] & 1 == 1)
    def _():
        out[...] = other[...]


def pair_kernel(one, other, out):
    out[16:32] = one[...]
    out[0:16] = other[...]


def parts_of(values):
    high = values.astype(BF16)
    rest = values - high.astype(F32)
    middle = rest.astype(BF16)
    return high, middle, (rest - middle.astype(F32)).astype(BF16)


def turned_over(values):
    rows, columns = values.shape
    same = lax.broadcasted_iota(jnp.int32, (columns, columns), 0) == lax.broadcasted_iota(
        jnp.int32, (columns, columns), 1
    )
    return sum(
        lax.dot_general(same.astype(BF16), part, NT, preferred_element_type=F32)
        for part in parts_of(values)
    )


def split_kernel(member_ref, block_ref, x_ref, source, ids, wedge, focus, sigma, *refs):
    outs, (ids_in, wedge_in, focus_in, sigma_in, sems, more) = refs[:G], refs[G:]
    copies = []
    for n in (2, 1, 3, 0):
        copies += pieces_of(source, outs[n], member_ref[0] ^ n, sems, n * 2 * NB)
    settings = [
        pltpu.make_async_copy(at, to, more.at[n])
        for n, (at, to) in enumerate(
            ((ids, ids_in), (wedge, wedge_in), (focus, focus_in), (sigma, sigma_in))
        )
    ]
    for copy in copies + settings:
        copy.start()
    for copy in settings:
        copy.wait()
    first = jnp.concatenate(
        [ids_in[...].astype(F32), jnp.broadcast_to(sigma_in[...], (8, P_DEV))], axis=0
    )
    turned = turned_over(first)
    pieces = [turned[:, :SHIFTS], *parts_of(turned[:, SHIFTS : SHIFTS + 1]), jnp.zeros((P_DEV, 5), F32)]
    pieces += [*parts_of(wedge_in[...].astype(F32) * focus_in[...]), jnp.zeros((P_DEV, 16), F32)]
    info = jnp.concatenate([piece.astype(F32) for piece in pieces], axis=1).astype(BF16)
    for out in outs:
        out[:, WIDTH:] = info
    for copy in copies:
        copy.wait()


def split_particles(place, particles, shift_ids, wedge, defocus, inv_sigma):
    return local(
        split_kernel, "split_particles", [((P_DEV, WIDTH + EXTRA), BF16)] * G, place,
        [particles, shift_ids.T, wedge, defocus, inv_sigma[None]], 4, placed=5,
        scratch=[
            pltpu.VMEM((SHIFTS, P_DEV), jnp.int32),
            pltpu.VMEM((P_DEV, TILTS), jnp.int32),
            pltpu.VMEM((P_DEV, TILTS), F32),
            pltpu.VMEM((1, P_DEV), F32),
            pltpu.SemaphoreType.DMA((G * 2 * NB,)),
            pltpu.SemaphoreType.DMA((4,)),
        ],
    )


def rows_kernel(member_ref, x_ref, geo_ref, table_ref, rows_ref, pen_ref):
    info = x_ref[:, WIDTH:].astype(F32)
    lane = lax.broadcasted_iota(jnp.int32, (ROWS, 256), 1) & 127
    ids = jnp.concatenate([info[:, s : s + 1] for s in range(SHIFTS)], axis=0)
    pick = (ids == lane.astype(F32)).astype(BF16)
    sigma = sum(info[:, SHIFTS + n : SHIFTS + n + 1] for n in range(3))
    small = lax.broadcasted_iota(jnp.int32, (P_DEV, 128), 1)

    @pl.loop(0, NB, unroll=True)
    def _(block):
        first = 2 * (block * G + member_ref[0]) + 16
        start = pl.multiple_of(block * 2 * COLS, 2 * COLS)
        for tilt in range(2):
            at = first + tilt
            mine = (small == at) | (small == at + TILTS) | (small == at + 2 * TILTS)
            focus = jnp.sum(jnp.where(mine, info, 0.0), axis=1, keepdims=True)
            kept = jnp.where(focus > 0.5, 1.0, 0.0)
            shell = geo_ref[block, 3:4, tilt * HALF : (tilt + 1) * HALF]
            transfer = -sine_turns((4.0 * focus * shell + 0.1) * (0.5 / math.pi))
            weight = kept * transfer * sigma
            spot = pl.multiple_of(block * COLS + tilt * HALF, HALF)
            pen_ref[:, pl.ds(spot, HALF)] = (0.5 * weight * transfer).astype(BF16)
            lower, upper = pl.ds(start + tilt * HALF, HALF), pl.ds(start + COLS + tilt * HALF, HALF)
            real = (weight * x_ref[:, lower].astype(F32))[None]
            imag = (weight * x_ref[:, upper].astype(F32))[None]
            real, imag = real[0], imag[0]
            for part in range(0, HALF, 256):
                lanes = slice(part, part + 256)
                at = start + tilt * COLS + part
                cosine = jnp.dot(pick, table_ref[:, pl.ds(at, 256)], preferred_element_type=F32)
                sine = jnp.dot(pick, table_ref[:, pl.ds(at + HALF, 256)], preferred_element_type=F32)
                cosine, sine = cosine.reshape(SHIFTS, P_DEV, 256), sine.reshape(SHIFTS, P_DEV, 256)
                one, two = real[None, :, lanes], imag[None, :, lanes]
                low = pl.ds(start + tilt * HALF + part, 256)
                high = pl.ds(start + COLS + tilt * HALF + part, 256)
                rows_ref[:, low] = (one * cosine + two * sine).reshape(ROWS, 256).astype(BF16)
                rows_ref[:, high] = (two * cosine - one * sine).reshape(ROWS, 256).astype(BF16)


def make_rows(member, x, geo, table):
    return local(
        rows_kernel, "shifted_rows", [((ROWS, WIDTH), BF16), ((P_DEV, NB * COLS), BF16)], [member],
        [x, geo, table], 12,
    )


ARRIVAL = [(2, 0), (1, 1), (3, 1), (0, 1), (1, 0), (3, 0), (0, 0)]


def scores_kernel(count, fresh, *refs):
    blocks = refs[2 * count : 2 * count + 7]
    outs = refs[2 * count + 7 :]
    stacked = dict(zip(ARRIVAL, blocks))
    stacked = jnp.concatenate([stacked[at][...] for at in sorted(ARRIVAL)], axis=0)
    if fresh:
        for block in range(NB):
            start = block * 2 * COLS
            real = stacked[:, start : start + COLS].astype(F32)
            imag = stacked[:, start + COLS : start + 2 * COLS].astype(F32)
            outs[-1][:, block * COLS : (block + 1) * COLS] = (real * real + imag * imag).astype(BF16)
        power, outs = outs[-1][...], outs[:-1]
    else:
        power, outs = outs[0][...], outs[1:]
    pens = jnp.concatenate([pen[...] for pen in refs[count : 2 * count]], axis=0)
    rows = jnp.concatenate([row[...] for row in refs[:count]], axis=0)
    energy = lax.dot_general(pens, power, NT, preferred_element_type=F32)
    total = lax.dot_general(rows, stacked, NT, preferred_element_type=F32)
    for n, out in enumerate(outs):
        mine = total[n * ROWS : (n + 1) * ROWS].reshape(SHIFTS, P_DEV, 128)
        out[...] = (mine - energy[None, n * P_DEV : (n + 1) * P_DEV]).reshape(ROWS, 128)


def make_scores(rows, pens, blocks, power=None):
    count, fresh = len(rows), power is None
    outs = [((ROWS, 128), F32)] * count + [((128, NB * COLS), BF16)] * fresh
    return local(
        lambda *refs: scores_kernel(count, fresh, *refs), "partial_scores", outs, [],
        [*rows, *pens, *blocks] + ([] if fresh else [power]), 12,
    )


def sum_kernel(*refs):
    refs[-1][...] = refs[0][...] + refs[1][...] + refs[2][...]


def posterior_kernel(*refs):
    out = refs[-1]
    total = refs[0][...]
    for other in refs[1:-1]:
        total = total + other[...]
    total = total.reshape(SHIFTS, P_DEV, 128)
    peak = jnp.max(jnp.max(total, axis=0), axis=1, keepdims=True)
    expo = jnp.exp(total - peak[None])
    norm = jnp.sum(jnp.sum(expo, axis=0), axis=1, keepdims=True)
    share = (expo / norm[None]).reshape(ROWS, 128)
    out[...] = share.T.astype(BF16)


def make_posterior(parts):
    (out,) = local(posterior_kernel, "posterior", [((128, ROWS), BF16)], [], parts, 4)
    return out


def accum_kernel(part, member_ref, x_ref, *refs):
    rows, posts, outs = refs[:G], refs[G : 2 * G], refs[2 * G :]
    along_y = (member_ref[0] & 1) == part
    high = x_ref[0] >> 1

    @pl.loop(0, NB, unroll=True)
    def _(block):
        sums = []
        for half in range(2):
            start = pl.multiple_of(block * 2 * COLS + half * COLS + part * HALF, HALF)
            total = jnp.dot(posts[0][...], rows[0][:, pl.ds(start, HALF)], preferred_element_type=F32)
            for n in range(1, G):
                total = total + jnp.dot(
                    posts[n][...], rows[n][:, pl.ds(start, HALF)], preferred_element_type=F32
                )
            sums.append(total)
        spot = pl.ds(pl.multiple_of(block * HALF, HALF), HALF)
        for n, out in enumerate(outs):
            upper = high ^ (n >> 1) == 1
            for group in range(4):
                at = n * 32 + (group >> 1) * 16
                for_y = sums[group & 1][at : at + 16]
                at = group * 32 + (n & 1) * 16
                for_x = jnp.where(upper, sums[1][at : at + 16], sums[0][at : at + 16])
                out[group * 16 : (group + 1) * 16, spot] = jnp.where(along_y, for_y, for_x).astype(BF16)


def make_accum(part, member, x_at, rows, posts):
    return local(
        lambda *refs: accum_kernel(part, *refs), "weighted_sums", [((64, NB * HALF), BF16)] * 4,
        [member, x_at], [*rows, *posts], 8,
    )


def added(values):
    total = values[0].astype(F32)
    for value in values[1:]:
        total = total + value.astype(F32)
    return total


PIECES = [((16, NB * HALF), F32)] + [((16, NB * HALF), BF16)] * 3


def turn_kernel(part, member_ref, x_ref, *refs):
    along_y = (member_ref[0] & 1) == part
    for n, out in enumerate(refs[4:]):
        group = jnp.where(along_y, (n & 1) * 2 + ((x_ref[0] >> 1) ^ (n >> 1)), n)
        mine = pl.ds(pl.multiple_of(group * 16, 16), 16)
        out[...] = added([ref[mine, :] for ref in refs[:4]]).astype(out.dtype)


def make_turn(part, member, x_at, values):
    return local(
        lambda *refs: turn_kernel(part, *refs), "turned_sums", PIECES, [member, x_at], values, 4
    )


def joined_kernel(block_ref, *refs):
    for n, out in enumerate(refs[8:]):
        spot = pl.ds(pl.multiple_of((block_ref[0] ^ n) * HALF, HALF), HALF)
        out[:, :HALF] = added([ref[:, spot] for ref in refs[:4]]).astype(out.dtype)
        out[:, HALF:] = added([ref[:, spot] for ref in refs[4:8]]).astype(out.dtype)


def after(value, *others):
    return lax.optimization_barrier((value, *others))[0]


def per_device(refs, particles, shift_ids, wedge, defocus, inv_sigma):
    dom = lax.axis_index("dom")
    x_at = (dom // 16) * 2 + lax.axis_index("blk") % 2
    place = [value.astype(jnp.int32).reshape(1) for value in (dom % G, (dom % 16) // G, x_at)]
    member, block, x_at = place
    geo = jnp.asarray(geometry())

    chunks = split_particles(place, particles, shift_ids, wedge, defocus, inv_sigma)
    got, gathered, rows, pens = {}, {}, {}, {}
    got[2] = send(chunks[2], partners(2))
    got[1] = send(chunks[1], partners(1))
    own = own_columns(member, refs, chunks[2])
    gathered[0, 0] = own
    gathered[1, 0] = send(own, flips(y=1))
    gathered[3, 0] = send(own, flips(y=3))
    gathered[0, 1] = send(own, flips(x=1))
    table, geo = make_table(member, geo)
    rows[0], pens[0] = make_rows(member, chunks[0], geo, table)
    wave = [got[1], gathered[1, 0], gathered[3, 0], gathered[0, 1], rows[0]]
    gathered[2, 1] = send(after(gathered[0, 1], *wave), flips(y=2))
    relayed = [gathered[1, 0], after(gathered[3, 0], *wave)]
    (relay,) = local(relay_kernel, "relay", [((16, WIDTH), BF16)], [member], relayed, 2)
    gathered[2, 0] = send(relay, second_hop())
    gathered[1, 1] = send(after(gathered[1, 0], relay), flips(x=1))
    gathered[3, 1] = send(after(gathered[3, 0], relay), flips(x=3))
    got[3] = send(after(chunks[3], got[2], *wave), partners(3))
    rows[2], pens[2] = make_rows(member, after(got[2], *wave), geo, table)
    rows[1], pens[1] = make_rows(member, after(got[1], rows[2]), geo, table)
    far = [gathered[2, 1], gathered[2, 0]]
    (gathered[2, 0],) = local(pair_kernel, "pair", [((32, WIDTH), BF16)], [], far, 2)
    blocks = [gathered[at] for at in ARRIVAL]

    second, power = make_scores([rows[2]], [after(pens[2], rows[1])], blocks)
    rows[3], pens[3] = make_rows(member, after(got[3], second), geo, table)
    (third,) = make_scores([rows[3]], [after(pens[3], second)], blocks, power)
    mine, other = make_scores([rows[0], rows[1]], [after(pens[0], third), pens[1]], blocks, power)
    near = [mine, send(second, partners(2)), send(third, partners(3))]
    (near,) = local(sum_kernel, "score_sums", [((ROWS, 128), F32)], [], near, 4)
    posterior = make_posterior([near, send(other, partners(1))])
    posts = {n: send(posterior, partners(n)) for n in (3, 2, 1)}
    posts = [posterior] + [posts[n] for n in range(1, G)]
    rows = [rows[n] for n in range(G)]

    first = make_accum(0, member, x_at, rows, posts)
    first = [first[0]] + [send(first[n], crossed(n, 0)) for n in (2, 1, 3)]
    second = make_accum(1, member, x_at, rows, posts)
    second = [second[0]] + [send(second[n], crossed(n, 1)) for n in (2, 1, 3)]
    first = make_turn(0, member, x_at, first)
    first = [first[0]] + [send(first[n], crossed(n, 1)) for n in (2, 1, 3)]
    second = make_turn(1, member, x_at, second)
    second = [second[0]] + [send(second[n], crossed(n, 0)) for n in (2, 1, 3)]
    outs = [((16, COLS), F32)] + [((16, COLS), BF16)] * (NB - 1)
    ends = local(joined_kernel, "joined_sums", outs, [block], [*first, *second], 4)
    return added([ends[0]] + [send(ends[n], flips(z=n * (G // 2))) for n in (2, 1, 3)])


def solution(mesh):
    return jax.shard_map(
        per_device,
        mesh=mesh,
        in_specs=(
            P("blk", None),
            P(("blk", "dom"), None),
            P(("blk", "dom"), None),
            P(("blk", "dom"), None),
            P(("blk", "dom"), None),
            P(("blk", "dom")),
        ),
        out_specs=P("blk", "dom"),
        check_vma=False,
    )
```

```python
import math

import jax
import jax.numpy as jnp
import numpy as np
from jax import lax
from jax.experimental import pallas as pl
from jax.experimental.pallas import tpu as pltpu
from jax.sharding import PartitionSpec as P

BOX = 32
TILTS = 32
SHIFTS = 8
P_DEV = 32
Y, X, Z = 4, 4, 8
COLS = 1024
HALF = 512
G = 4
NB = 16 // G
ROWS = P_DEV * SHIFTS
WIDTH = NB * 2 * COLS
EXTRA = 128
AXES = ("blk", "dom")
F32, BF16 = jnp.float32, jnp.bfloat16
NT = (((1,), (1,)), ((), ()))
MIB = 1 << 20


def linear(y, x, z, core):
    y, x, z = y % Y, x % X, z % Z
    return (y * 2 + x % 2) * 32 + (x // 2) * 16 + z * 2 + core


def flips(y=0, x=0, z=0):
    return [
        (linear(i, j, k, c), linear(i ^ y, j ^ x, k ^ z, c))
        for i in range(Y) for j in range(X) for k in range(Z) for c in range(2)
    ]


def crossed(n, core):
    return [
        (linear(i, j, k, c), linear(i ^ (n if c == core else 0), j ^ (0 if c == core else n), k, c))
        for i in range(Y) for j in range(X) for k in range(Z) for c in range(2)
    ]


def second_hop():
    return [
        (linear(i, j, k, c), linear(i ^ (1 if c else 3), j, k, c))
        for i in range(Y) for j in range(X) for k in range(Z) for c in range(2)
    ]


def partners(k):
    return [
        (linear(y, x, z, c), linear(y, x, z ^ (k >> 1), c ^ (k & 1)))
        for y in range(Y) for x in range(X) for z in range(Z) for c in range(2)
    ]


def send(value, pairs):
    return lax.ppermute(value, AXES, pairs)


def geometry():
    position = np.arange(TILTS * HALF)
    tilt, within = position // HALF, position % HALF
    radial = (within // BOX).astype(np.float64)
    lateral = (within % BOX - BOX // 2).astype(np.float64)
    angle = (tilt - 0.5 * (TILTS - 1)) * (2.0 / TILTS)
    shell = (radial * radial + lateral * lateral) / (0.25 * BOX * BOX)
    zero = np.zeros_like(shell)
    table = np.stack([radial * np.cos(angle), lateral, radial * np.sin(angle), shell] + [zero] * 4)
    return table.reshape(8, 16, COLS).transpose(1, 0, 2).astype(np.float32)


def fold(turns):
    turns = turns - jnp.floor(turns + 0.5)
    far = jnp.abs(turns) > 0.25
    near = jnp.where(far, jnp.where(turns > 0, 0.5, -0.5) - turns, turns)
    return near * (2.0 * math.pi), far


def series(square, terms):
    total = jnp.full_like(square, terms[-1])
    for term in terms[-2::-1]:
        total = total * square + term
    return total


SIN_TERMS = [(-1) ** n / math.factorial(2 * n + 1) for n in range(6)]
COS_TERMS = [(-1) ** n / math.factorial(2 * n) for n in range(7)]


def sine_turns(turns):
    angle, _ = fold(turns)
    return angle * series(angle * angle, SIN_TERMS)


def held(value):
    return pltpu.with_memory_space_constraint(value, pltpu.VMEM)


SCALARS = pl.BlockSpec(memory_space=pltpu.SMEM)
WHOLE = pl.BlockSpec(memory_space=pltpu.VMEM)
PLACED = pl.BlockSpec(memory_space=pl.ANY)


def local(kernel, name, outs, scalars, arrays, limit, placed=0, scratch=()):
    return pl.pallas_call(
        kernel,
        in_specs=[SCALARS] * len(scalars) + [PLACED] * placed + [WHOLE] * (len(arrays) - placed),
        out_specs=[WHOLE] * len(outs),
        out_shape=[pltpu.VMEM(shape, kind) for shape, kind in outs],
        scratch_shapes=list(scratch),
        cost_estimate=pl.CostEstimate(flops=0, bytes_accessed=0, transcendentals=0),
        compiler_params=pltpu.CompilerParams(vmem_limit_bytes=limit * MIB),
        name=name,
    )(
        *scalars,
        *[pltpu.with_memory_space_constraint(value, pltpu.HBM) for value in arrays[:placed]],
        *[held(value) for value in arrays[placed:]],
    )


def table_kernel(member_ref, geo_ref, out_ref, picked_ref, sems):
    copies = [
        pltpu.make_async_copy(geo_ref.at[block * G + member_ref[0]], picked_ref.at[block], sems.at[block])
        for block in range(NB)
    ]
    for copy in copies:
        copy.start()
    ids = lax.broadcasted_iota(jnp.int32, (64, 1), 0).astype(F32)
    high = jnp.floor((ids + 0.5) * (1 / 25))
    middle = jnp.floor((ids - 25 * high + 0.5) * (1 / 5))
    low = ids - 25 * high - 5 * middle
    move_x, move_y, move_z = ((digit - 2.0) * (0.5 / BOX) for digit in (high, middle, low))
    for copy in copies:
        copy.wait()

    @pl.loop(0, NB, unroll=True)
    def _(block):
        geo = picked_ref[block]
        for tilt in range(2):
            part = geo[:, tilt * HALF : (tilt + 1) * HALF]
            turns = move_x * part[0:1] + move_y * part[1:2] + move_z * part[2:3]
            angle, far = fold(turns)
            square = angle * angle
            sine = angle * series(square, SIN_TERMS)
            cosine = series(square, COS_TERMS)
            cosine = jnp.where(far, -cosine, cosine)
            for at, values in enumerate((cosine, sine)):
                high = values.astype(BF16)
                low = (values - high.astype(F32)).astype(BF16)
                spot = pl.ds(pl.multiple_of(block * 2 * COLS + tilt * COLS + at * HALF, HALF), HALF)
                out_ref[0:64, spot] = high
                out_ref[64:128, spot] = -high if at else high
                out_ref[128:192, spot] = low
                out_ref[192:256, spot] = -low if at else low


def make_table(member, geo):
    return local(
        table_kernel, "phase_table", [((256, WIDTH), BF16), ((NB, 8, COLS), F32)], [member], [geo], 8,
        placed=1, scratch=[pltpu.SemaphoreType.DMA((NB,))],
    )


def column(part, block, who):
    return pl.ds(pl.multiple_of((part * 16 + block * G + who) * COLS, COLS), COLS)


def pieces_of(source, out, who, sems, base):
    return [
        pltpu.make_async_copy(
            source.at[:, column(part, block, who)],
            out.at[:, pl.ds((block * 2 + part) * COLS, COLS)],
            sems.at[base + block * 2 + part],
        )
        for block in range(NB) for part in range(2)
    ]


def own_kernel(member_ref, source, after, out, sems):
    copies = pieces_of(source, out, member_ref[0], sems, 0)
    for copy in copies:
        copy.start()
    for copy in copies:
        copy.wait()


def own_columns(member, refs, after):
    (own,) = local(
        own_kernel, "own_references", [((16, WIDTH), BF16)], [member], [refs, after], 4,
        placed=1, scratch=[pltpu.SemaphoreType.DMA((2 * NB,))],
    )
    return own


def relay_kernel(member_ref, one, other, out):
    @pl.when(member_ref[0] & 1 == 0)
    def _():
        out[...] = one[...]

    @pl.when(member_ref[0] & 1 == 1)
    def _():
        out[...] = other[...]


def pair_kernel(one, other, out):
    out[16:32] = one[...]
    out[0:16] = other[...]


def parts_of(values):
    high = values.astype(BF16)
    rest = values - high.astype(F32)
    middle = rest.astype(BF16)
    return high, middle, (rest - middle.astype(F32)).astype(BF16)


def turned_over(values):
    rows, columns = values.shape
    same = lax.broadcasted_iota(jnp.int32, (columns, columns), 0) == lax.broadcasted_iota(
        jnp.int32, (columns, columns), 1
    )
    return sum(
        lax.dot_general(same.astype(BF16), part, NT, preferred_element_type=F32)
        for part in parts_of(values)
    )


def split_kernel(member_ref, block_ref, x_ref, source, ids, wedge, focus, sigma, *refs):
    outs, (ids_in, wedge_in, focus_in, sigma_in, sems, more) = refs[:G], refs[G:]
    copies = []
    for n in (2, 1, 3, 0):
        copies += pieces_of(source, outs[n], member_ref[0] ^ n, sems, n * 2 * NB)
    settings = [
        pltpu.make_async_copy(at, to, more.at[n])
        for n, (at, to) in enumerate(
            ((ids, ids_in), (wedge, wedge_in), (focus, focus_in), (sigma, sigma_in))
        )
    ]
    for copy in copies + settings:
        copy.start()
    for copy in settings:
        copy.wait()
    first = jnp.concatenate(
        [ids_in[...].astype(F32), jnp.broadcast_to(sigma_in[...], (8, P_DEV))], axis=0
    )
    turned = turned_over(first)
    pieces = [turned[:, :SHIFTS], *parts_of(turned[:, SHIFTS : SHIFTS + 1]), jnp.zeros((P_DEV, 5), F32)]
    pieces += [*parts_of(wedge_in[...].astype(F32) * focus_in[...]), jnp.zeros((P_DEV, 16), F32)]
    info = jnp.concatenate([piece.astype(F32) for piece in pieces], axis=1).astype(BF16)
    for out in outs:
        out[:, WIDTH:] = info
    for copy in copies:
        copy.wait()


def split_particles(place, particles, shift_ids, wedge, defocus, inv_sigma):
    return local(
        split_kernel, "split_particles", [((P_DEV, WIDTH + EXTRA), BF16)] * G, place,
        [particles, shift_ids.T, wedge, defocus, inv_sigma[None]], 4, placed=5,
        scratch=[
            pltpu.VMEM((SHIFTS, P_DEV), jnp.int32),
            pltpu.VMEM((P_DEV, TILTS), jnp.int32),
            pltpu.VMEM((P_DEV, TILTS), F32),
            pltpu.VMEM((1, P_DEV), F32),
            pltpu.SemaphoreType.DMA((G * 2 * NB,)),
            pltpu.SemaphoreType.DMA((4,)),
        ],
    )


def rows_kernel(member_ref, x_ref, geo_ref, table_ref, rows_ref, pen_ref):
    info = x_ref[:, WIDTH:].astype(F32)
    lane = lax.broadcasted_iota(jnp.int32, (ROWS, 256), 1) & 127
    ids = jnp.concatenate([info[:, s : s + 1] for s in range(SHIFTS)], axis=0)
    ids = jnp.where(ids > 62.5, 188.0 - ids, ids)
    pick = (ids == lane.astype(F32)).astype(BF16)
    sigma = sum(info[:, SHIFTS + n : SHIFTS + n + 1] for n in range(3))
    small = lax.broadcasted_iota(jnp.int32, (P_DEV, 128), 1)

    @pl.loop(0, NB, unroll=True)
    def _(block):
        first = 2 * (block * G + member_ref[0]) + 16
        start = pl.multiple_of(block * 2 * COLS, 2 * COLS)
        for tilt in range(2):
            at = first + tilt
            mine = (small == at) | (small == at + TILTS) | (small == at + 2 * TILTS)
            focus = jnp.sum(jnp.where(mine, info, 0.0), axis=1, keepdims=True)
            kept = jnp.where(focus > 0.5, 1.0, 0.0)
            shell = geo_ref[block, 3:4, tilt * HALF : (tilt + 1) * HALF]
            transfer = -sine_turns((4.0 * focus * shell + 0.1) * (0.5 / math.pi))
            weight = kept * transfer * sigma
            spot = pl.multiple_of(block * COLS + tilt * HALF, HALF)
            pen_ref[:, pl.ds(spot, HALF)] = (0.5 * weight * transfer).astype(BF16)
            lower, upper = pl.ds(start + tilt * HALF, HALF), pl.ds(start + COLS + tilt * HALF, HALF)
            real = (weight * x_ref[:, lower].astype(F32))[None]
            imag = (weight * x_ref[:, upper].astype(F32))[None]
            real, imag = real[0], imag[0]
            for part in range(0, HALF, 256):
                lanes = slice(part, part + 256)
                at = start + tilt * COLS + part
                cosine = jnp.dot(pick, table_ref[:, pl.ds(at, 256)], preferred_element_type=F32)
                sine = jnp.dot(pick, table_ref[:, pl.ds(at + HALF, 256)], preferred_element_type=F32)
                cosine, sine = cosine.reshape(SHIFTS, P_DEV, 256), sine.reshape(SHIFTS, P_DEV, 256)
                one, two = real[None, :, lanes], imag[None, :, lanes]
                low = pl.ds(start + tilt * HALF + part, 256)
                high = pl.ds(start + COLS + tilt * HALF + part, 256)
                rows_ref[:, low] = (one * cosine + two * sine).reshape(ROWS, 256).astype(BF16)
                rows_ref[:, high] = (two * cosine - one * sine).reshape(ROWS, 256).astype(BF16)


def make_rows(member, x, geo, table):
    return local(
        rows_kernel, "shifted_rows", [((ROWS, WIDTH), BF16), ((P_DEV, NB * COLS), BF16)], [member],
        [x, geo, table], 12,
    )


ARRIVAL = [(2, 0), (1, 1), (3, 1), (0, 1), (1, 0), (3, 0), (0, 0)]


def scores_kernel(count, fresh, *refs):
    blocks = refs[2 * count : 2 * count + 7]
    outs = refs[2 * count + 7 :]
    stacked = dict(zip(ARRIVAL, blocks))
    stacked = jnp.concatenate([stacked[at][...] for at in sorted(ARRIVAL)], axis=0)
    if fresh:
        for block in range(NB):
            start = block * 2 * COLS
            real = stacked[:, start : start + COLS].astype(F32)
            imag = stacked[:, start + COLS : start + 2 * COLS].astype(F32)
            outs[-1][:, block * COLS : (block + 1) * COLS] = (real * real + imag * imag).astype(BF16)
        power, outs = outs[-1][...], outs[:-1]
    else:
        power, outs = outs[0][...], outs[1:]
    pens = jnp.concatenate([pen[...] for pen in refs[count : 2 * count]], axis=0)
    rows = jnp.concatenate([row[...] for row in refs[:count]], axis=0)
    energy = lax.dot_general(pens, power, NT, preferred_element_type=F32)
    total = lax.dot_general(rows, stacked, NT, preferred_element_type=F32)
    for n, out in enumerate(outs):
        mine = total[n * ROWS : (n + 1) * ROWS].reshape(SHIFTS, P_DEV, 128)
        out[...] = (mine - energy[None, n * P_DEV : (n + 1) * P_DEV]).reshape(ROWS, 128)


def make_scores(rows, pens, blocks, power=None):
    count, fresh = len(rows), power is None
    outs = [((ROWS, 128), F32)] * count + [((128, NB * COLS), BF16)] * fresh
    return local(
        lambda *refs: scores_kernel(count, fresh, *refs), "partial_scores", outs, [],
        [*rows, *pens, *blocks] + ([] if fresh else [power]), 12,
    )


def sum_kernel(*refs):
    refs[-1][...] = refs[0][...] + refs[1][...] + refs[2][...]


def posterior_kernel(*refs):
    out = refs[-1]
    total = refs[0][...]
    for other in refs[1:-1]:
        total = total + other[...]
    total = total.reshape(SHIFTS, P_DEV, 128)
    peak = jnp.max(jnp.max(total, axis=0), axis=1, keepdims=True)
    expo = jnp.exp(total - peak[None])
    norm = jnp.sum(jnp.sum(expo, axis=0), axis=1, keepdims=True)
    share = (expo / norm[None]).reshape(ROWS, 128)
    out[...] = share.T.astype(BF16)


def make_posterior(parts):
    (out,) = local(posterior_kernel, "posterior", [((128, ROWS), BF16)], [], parts, 4)
    return out


def accum_kernel(part, member_ref, x_ref, *refs):
    rows, posts, outs = refs[:G], refs[G : 2 * G], refs[2 * G :]
    along_y = (member_ref[0] & 1) == part
    high = x_ref[0] >> 1

    @pl.loop(0, NB, unroll=True)
    def _(block):
        sums = []
        for half in range(2):
            start = pl.multiple_of(block * 2 * COLS + half * COLS + part * HALF, HALF)
            total = jnp.dot(posts[0][...], rows[0][:, pl.ds(start, HALF)], preferred_element_type=F32)
            for n in range(1, G):
                total = total + jnp.dot(
                    posts[n][...], rows[n][:, pl.ds(start, HALF)], preferred_element_type=F32
                )
            sums.append(total)
        spot = pl.ds(pl.multiple_of(block * HALF, HALF), HALF)
        for n, out in enumerate(outs):
            upper = high ^ (n >> 1) == 1
            for group in range(4):
                at = n * 32 + (group >> 1) * 16
                for_y = sums[group & 1][at : at + 16]
                at = group * 32 + (n & 1) * 16
                for_x = jnp.where(upper, sums[1][at : at + 16], sums[0][at : at + 16])
                out[group * 16 : (group + 1) * 16, spot] = jnp.where(along_y, for_y, for_x).astype(BF16)


def make_accum(part, member, x_at, rows, posts):
    return local(
        lambda *refs: accum_kernel(part, *refs), "weighted_sums", [((64, NB * HALF), BF16)] * 4,
        [member, x_at], [*rows, *posts], 8,
    )


def added(values):
    total = values[0].astype(F32)
    for value in values[1:]:
        total = total + value.astype(F32)
    return total


PIECES = [((16, NB * HALF), F32)] + [((16, NB * HALF), BF16)] * 3


def turn_kernel(part, member_ref, x_ref, *refs):
    along_y = (member_ref[0] & 1) == part
    for n, out in enumerate(refs[4:]):
        group = jnp.where(along_y, (n & 1) * 2 + ((x_ref[0] >> 1) ^ (n >> 1)), n)
        mine = pl.ds(pl.multiple_of(group * 16, 16), 16)
        out[...] = added([ref[mine, :] for ref in refs[:4]]).astype(out.dtype)


def make_turn(part, member, x_at, values):
    return local(
        lambda *refs: turn_kernel(part, *refs), "turned_sums", PIECES, [member, x_at], values, 4
    )


def joined_kernel(block_ref, *refs):
    for n, out in enumerate(refs[8:]):
        spot = pl.ds(pl.multiple_of((block_ref[0] ^ n) * HALF, HALF), HALF)
        out[:, :HALF] = added([ref[:, spot] for ref in refs[:4]]).astype(out.dtype)
        out[:, HALF:] = added([ref[:, spot] for ref in refs[4:8]]).astype(out.dtype)


def after(value, *others):
    return lax.optimization_barrier((value, *others))[0]


def per_device(refs, particles, shift_ids, wedge, defocus, inv_sigma):
    dom = lax.axis_index("dom")
    x_at = (dom // 16) * 2 + lax.axis_index("blk") % 2
    place = [value.astype(jnp.int32).reshape(1) for value in (dom % G, (dom % 16) // G, x_at)]
    member, block, x_at = place
    geo = jnp.asarray(geometry())

    chunks = split_particles(place, particles, shift_ids, wedge, defocus, inv_sigma)
    got, gathered, rows, pens = {}, {}, {}, {}
    got[2] = send(chunks[2], partners(2))
    got[1] = send(chunks[1], partners(1))
    own = own_columns(member, refs, chunks[2])
    gathered[0, 0] = own
    gathered[1, 0] = send(own, flips(y=1))
    gathered[3, 0] = send(own, flips(y=3))
    gathered[0, 1] = send(own, flips(x=1))
    table, geo = make_table(member, geo)
    rows[0], pens[0] = make_rows(member, chunks[0], geo, table)
    rows[1], pens[1] = make_rows(member, after(got[1], rows[0]), geo, table)
    wave = [gathered[1, 0], gathered[3, 0], gathered[0, 1], rows[1]]
    gathered[2, 1] = send(after(gathered[0, 1], *wave), flips(y=2))
    relayed = [gathered[1, 0], after(gathered[3, 0], *wave)]
    (relay,) = local(relay_kernel, "relay", [((16, WIDTH), BF16)], [member], relayed, 2)
    gathered[2, 0] = send(relay, second_hop())
    gathered[1, 1] = send(after(gathered[1, 0], relay), flips(x=1))
    gathered[3, 1] = send(after(gathered[3, 0], relay), flips(x=3))
    got[3] = send(after(chunks[3], got[2], *wave), partners(3))
    rows[2], pens[2] = make_rows(member, after(got[2], *wave), geo, table)
    far = [gathered[2, 1], gathered[2, 0]]
    (gathered[2, 0],) = local(pair_kernel, "pair", [((32, WIDTH), BF16)], [], far, 2)
    blocks = [gathered[at] for at in ARRIVAL]

    second, power = make_scores([rows[2]], [pens[2]], blocks)
    rows[3], pens[3] = make_rows(member, after(got[3], second), geo, table)
    (third,) = make_scores([rows[3]], [after(pens[3], second)], blocks, power)
    mine, other = make_scores([rows[0], rows[1]], [after(pens[0], third), pens[1]], blocks, power)
    near = [mine, send(second, partners(2)), send(third, partners(3))]
    (near,) = local(sum_kernel, "score_sums", [((ROWS, 128), F32)], [], near, 4)
    posterior = make_posterior([near, send(other, partners(1))])
    posts = {n: send(posterior, partners(n)) for n in (3, 2, 1)}
    posts = [posterior] + [posts[n] for n in range(1, G)]
    rows = [rows[n] for n in range(G)]

    first = make_accum(0, member, x_at, rows, posts)
    first = [first[0]] + [send(first[n], crossed(n, 0)) for n in (2, 1, 3)]
    second = make_accum(1, member, x_at, rows, posts)
    second = [second[0]] + [send(second[n], crossed(n, 1)) for n in (2, 1, 3)]
    first = make_turn(0, member, x_at, first)
    first = [first[0]] + [send(first[n], crossed(n, 1)) for n in (2, 1, 3)]
    second = make_turn(1, member, x_at, second)
    second = [second[0]] + [send(second[n], crossed(n, 0)) for n in (2, 1, 3)]
    outs = [((16, COLS), F32)] + [((16, COLS), BF16)] * (NB - 1)
    ends = local(joined_kernel, "joined_sums", outs, [block], [*first, *second], 4)
    return added([ends[0]] + [send(ends[n], flips(z=n * (G // 2))) for n in (2, 1, 3)])


def solution(mesh):
    return jax.shard_map(
        per_device,
        mesh=mesh,
        in_specs=(
            P("blk", None),
            P(("blk", "dom"), None),
            P(("blk", "dom"), None),
            P(("blk", "dom"), None),
            P(("blk", "dom"), None),
            P(("blk", "dom")),
        ),
        out_specs=P("blk", "dom"),
        check_vma=False,
    )
```

```python
import math

import jax
import jax.numpy as jnp
import numpy as np
from jax import lax
from jax.experimental import pallas as pl
from jax.experimental.pallas import tpu as pltpu
from jax.sharding import PartitionSpec as P

BOX = 32
TILTS = 32
SHIFTS = 8
P_DEV = 32
Y, X, Z = 4, 4, 8
COLS = 1024
HALF = 512
G = 4
NB = 16 // G
ROWS = P_DEV * SHIFTS
WIDTH = NB * 2 * COLS
EXTRA = 128
AXES = ("blk", "dom")
F32, BF16 = jnp.float32, jnp.bfloat16
NT = (((1,), (1,)), ((), ()))
MIB = 1 << 20


def linear(y, x, z, core):
    y, x, z = y % Y, x % X, z % Z
    return (y * 2 + x % 2) * 32 + (x // 2) * 16 + z * 2 + core


def flips(y=0, x=0, z=0):
    return [
        (linear(i, j, k, c), linear(i ^ y, j ^ x, k ^ z, c))
        for i in range(Y) for j in range(X) for k in range(Z) for c in range(2)
    ]


def crossed(n, core):
    return [
        (linear(i, j, k, c), linear(i ^ (n if c == core else 0), j ^ (0 if c == core else n), k, c))
        for i in range(Y) for j in range(X) for k in range(Z) for c in range(2)
    ]


def second_hop():
    return [
        (linear(i, j, k, c), linear(i ^ (1 if c else 3), j, k, c))
        for i in range(Y) for j in range(X) for k in range(Z) for c in range(2)
    ]


def partners(k):
    return [
        (linear(y, x, z, c), linear(y, x, z ^ (k >> 1), c ^ (k & 1)))
        for y in range(Y) for x in range(X) for z in range(Z) for c in range(2)
    ]


def send(value, pairs):
    return lax.ppermute(value, AXES, pairs)


def geometry():
    position = np.arange(TILTS * HALF)
    tilt, within = position // HALF, position % HALF
    radial = (within // BOX).astype(np.float64)
    lateral = (within % BOX - BOX // 2).astype(np.float64)
    angle = (tilt - 0.5 * (TILTS - 1)) * (2.0 / TILTS)
    shell = (radial * radial + lateral * lateral) / (0.25 * BOX * BOX)
    zero = np.zeros_like(shell)
    table = np.stack([radial * np.cos(angle), lateral, radial * np.sin(angle), shell] + [zero] * 4)
    return table.reshape(8, 16, COLS).transpose(1, 0, 2).astype(np.float32)


def fold(turns):
    turns = turns - jnp.floor(turns + 0.5)
    far = jnp.abs(turns) > 0.25
    near = jnp.where(far, jnp.where(turns > 0, 0.5, -0.5) - turns, turns)
    return near * (2.0 * math.pi), far


def series(square, terms):
    total = jnp.full_like(square, terms[-1])
    for term in terms[-2::-1]:
        total = total * square + term
    return total


SIN_TERMS = [(-1) ** n / math.factorial(2 * n + 1) for n in range(6)]
COS_TERMS = [(-1) ** n / math.factorial(2 * n) for n in range(7)]


def sine_turns(turns):
    angle, _ = fold(turns)
    return angle * series(angle * angle, SIN_TERMS)


def held(value):
    return pltpu.with_memory_space_constraint(value, pltpu.VMEM)


SCALARS = pl.BlockSpec(memory_space=pltpu.SMEM)
WHOLE = pl.BlockSpec(memory_space=pltpu.VMEM)
PLACED = pl.BlockSpec(memory_space=pl.ANY)


def local(kernel, name, outs, scalars, arrays, limit, placed=0, scratch=()):
    return pl.pallas_call(
        kernel,
        in_specs=[SCALARS] * len(scalars) + [PLACED] * placed + [WHOLE] * (len(arrays) - placed),
        out_specs=[WHOLE] * len(outs),
        out_shape=[pltpu.VMEM(shape, kind) for shape, kind in outs],
        scratch_shapes=list(scratch),
        cost_estimate=pl.CostEstimate(flops=0, bytes_accessed=0, transcendentals=0),
        compiler_params=pltpu.CompilerParams(vmem_limit_bytes=limit * MIB),
        name=name,
    )(
        *scalars,
        *[pltpu.with_memory_space_constraint(value, pltpu.HBM) for value in arrays[:placed]],
        *[held(value) for value in arrays[placed:]],
    )


def table_kernel(member_ref, geo_ref, out_ref, picked_ref, sems):
    copies = [
        pltpu.make_async_copy(geo_ref.at[block * G + member_ref[0]], picked_ref.at[block], sems.at[block])
        for block in range(NB)
    ]
    for copy in copies:
        copy.start()
    ids = lax.broadcasted_iota(jnp.int32, (64, 1), 0).astype(F32)
    high = jnp.floor((ids + 0.5) * (1 / 25))
    middle = jnp.floor((ids - 25 * high + 0.5) * (1 / 5))
    low = ids - 25 * high - 5 * middle
    move_x, move_y, move_z = ((digit - 2.0) * (0.5 / BOX) for digit in (high, middle, low))
    for copy in copies:
        copy.wait()

    @pl.loop(0, NB, unroll=True)
    def _(block):
        geo = picked_ref[block]
        for tilt in range(2):
            part = geo[:, tilt * HALF : (tilt + 1) * HALF]
            turns = move_x * part[0:1] + move_y * part[1:2] + move_z * part[2:3]
            angle, far = fold(turns)
            square = angle * angle
            sine = angle * series(square, SIN_TERMS)
            cosine = series(square, COS_TERMS)
            cosine = jnp.where(far, -cosine, cosine)
            for at, values in enumerate((cosine, sine)):
                high = values.astype(BF16)
                low = (values - high.astype(F32)).astype(BF16)
                spot = pl.ds(pl.multiple_of(block * 2 * COLS + tilt * COLS + at * HALF, HALF), HALF)
                out_ref[0:64, spot] = high
                out_ref[64:128, spot] = -high if at else high
                out_ref[128:192, spot] = low
                out_ref[192:256, spot] = -low if at else low


def make_table(member, geo):
    return local(
        table_kernel, "phase_table", [((256, WIDTH), BF16), ((NB, 8, COLS), F32)], [member], [geo], 8,
        placed=1, scratch=[pltpu.SemaphoreType.DMA((NB,))],
    )


def column(part, block, who):
    return pl.ds(pl.multiple_of((part * 16 + block * G + who) * COLS, COLS), COLS)


def pieces_of(source, out, who, sems, base):
    return [
        pltpu.make_async_copy(
            source.at[:, column(part, block, who)],
            out.at[:, pl.ds((block * 2 + part) * COLS, COLS)],
            sems.at[base + block * 2 + part],
        )
        for block in range(NB) for part in range(2)
    ]


def own_kernel(member_ref, source, after, out, sems):
    copies = pieces_of(source, out, member_ref[0], sems, 0)
    for copy in copies:
        copy.start()
    for copy in copies:
        copy.wait()


def own_columns(member, refs, after):
    (own,) = local(
        own_kernel, "own_references", [((16, WIDTH), BF16)], [member], [refs, after], 4,
        placed=1, scratch=[pltpu.SemaphoreType.DMA((2 * NB,))],
    )
    return own


def relay_kernel(member_ref, one, other, out):
    @pl.when(member_ref[0] & 1 == 0)
    def _():
        out[...] = one[...]

    @pl.when(member_ref[0] & 1 == 1)
    def _():
        out[...] = other[...]


def pair_kernel(one, other, out):
    out[16:32] = one[...]
    out[0:16] = other[...]


def parts_of(values):
    high = values.astype(BF16)
    rest = values - high.astype(F32)
    middle = rest.astype(BF16)
    return high, middle, (rest - middle.astype(F32)).astype(BF16)


def turned_over(values):
    rows, columns = values.shape
    same = lax.broadcasted_iota(jnp.int32, (columns, columns), 0) == lax.broadcasted_iota(
        jnp.int32, (columns, columns), 1
    )
    return sum(
        lax.dot_general(same.astype(BF16), part, NT, preferred_element_type=F32)
        for part in parts_of(values)
    )


def split_kernel(member_ref, block_ref, x_ref, source, ids, wedge, focus, sigma, *refs):
    outs, (ids_in, wedge_in, focus_in, sigma_in, sems, more) = refs[:G], refs[G:]
    copies = []
    for n in (2, 1, 3, 0):
        copies += pieces_of(source, outs[n], member_ref[0] ^ n, sems, n * 2 * NB)
    settings = [
        pltpu.make_async_copy(at, to, more.at[n])
        for n, (at, to) in enumerate(
            ((ids, ids_in), (wedge, wedge_in), (focus, focus_in), (sigma, sigma_in))
        )
    ]
    for copy in copies + settings:
        copy.start()
    for copy in settings:
        copy.wait()
    first = jnp.concatenate(
        [ids_in[...].astype(F32), jnp.broadcast_to(sigma_in[...], (8, P_DEV))], axis=0
    )
    turned = turned_over(first)
    pieces = [turned[:, :SHIFTS], *parts_of(turned[:, SHIFTS : SHIFTS + 1]), jnp.zeros((P_DEV, 5), F32)]
    pieces += [*parts_of(wedge_in[...].astype(F32) * focus_in[...]), jnp.zeros((P_DEV, 16), F32)]
    info = jnp.concatenate([piece.astype(F32) for piece in pieces], axis=1).astype(BF16)
    for out in outs:
        out[:, WIDTH:] = info
    for copy in copies:
        copy.wait()


def split_particles(place, particles, shift_ids, wedge, defocus, inv_sigma):
    return local(
        split_kernel, "split_particles", [((P_DEV, WIDTH + EXTRA), BF16)] * G, place,
        [particles, shift_ids.T, wedge, defocus, inv_sigma[None]], 4, placed=5,
        scratch=[
            pltpu.VMEM((SHIFTS, P_DEV), jnp.int32),
            pltpu.VMEM((P_DEV, TILTS), jnp.int32),
            pltpu.VMEM((P_DEV, TILTS), F32),
            pltpu.VMEM((1, P_DEV), F32),
            pltpu.SemaphoreType.DMA((G * 2 * NB,)),
            pltpu.SemaphoreType.DMA((4,)),
        ],
    )


def rows_kernel(member_ref, x_ref, geo_ref, table_ref, rows_ref, pen_ref):
    info = x_ref[:, WIDTH:].astype(F32)
    lane = lax.broadcasted_iota(jnp.int32, (ROWS, 256), 1) & 127
    ids = jnp.concatenate([info[:, s : s + 1] for s in range(SHIFTS)], axis=0)
    ids = jnp.where(ids > 62.5, 188.0 - ids, ids)
    pick = (ids == lane.astype(F32)).astype(BF16)
    sigma = sum(info[:, SHIFTS + n : SHIFTS + n + 1] for n in range(3))
    small = lax.broadcasted_iota(jnp.int32, (P_DEV, 128), 1)

    @pl.loop(0, NB, unroll=True)
    def _(block):
        first = 2 * (block * G + member_ref[0]) + 16
        start = pl.multiple_of(block * 2 * COLS, 2 * COLS)
        for tilt in range(2):
            at = first + tilt
            mine = (small == at) | (small == at + TILTS) | (small == at + 2 * TILTS)
            focus = jnp.sum(jnp.where(mine, info, 0.0), axis=1, keepdims=True)
            kept = jnp.where(focus > 0.5, 1.0, 0.0)
            shell = geo_ref[block, 3:4, tilt * HALF : (tilt + 1) * HALF]
            transfer = -sine_turns((4.0 * focus * shell + 0.1) * (0.5 / math.pi))
            weight = kept * transfer * sigma
            spot = pl.multiple_of(block * COLS + tilt * HALF, HALF)
            pen_ref[:, pl.ds(spot, HALF)] = (0.5 * weight * transfer).astype(BF16)
            lower, upper = pl.ds(start + tilt * HALF, HALF), pl.ds(start + COLS + tilt * HALF, HALF)
            real = (weight * x_ref[:, lower].astype(F32))[None]
            imag = (weight * x_ref[:, upper].astype(F32))[None]
            real, imag = real[0], imag[0]
            for part in range(0, HALF, 256):
                lanes = slice(part, part + 256)
                at = start + tilt * COLS + part
                cosine = jnp.dot(pick, table_ref[:, pl.ds(at, 256)], preferred_element_type=F32)
                sine = jnp.dot(pick, table_ref[:, pl.ds(at + HALF, 256)], preferred_element_type=F32)
                cosine, sine = cosine.reshape(SHIFTS, P_DEV, 256), sine.reshape(SHIFTS, P_DEV, 256)
                one, two = real[None, :, lanes], imag[None, :, lanes]
                low = pl.ds(start + tilt * HALF + part, 256)
                high = pl.ds(start + COLS + tilt * HALF + part, 256)
                rows_ref[:, low] = (one * cosine + two * sine).reshape(ROWS, 256).astype(BF16)
                rows_ref[:, high] = (two * cosine - one * sine).reshape(ROWS, 256).astype(BF16)


def make_rows(member, x, geo, table):
    return local(
        rows_kernel, "shifted_rows", [((ROWS, WIDTH), BF16), ((P_DEV, NB * COLS), BF16)], [member],
        [x, geo, table], 12,
    )


ARRIVAL = [(2, 0), (1, 1), (3, 1), (0, 1), (1, 0), (3, 0), (0, 0)]


def scores_kernel(count, fresh, *refs):
    blocks = refs[2 * count : 2 * count + 7]
    outs = refs[2 * count + 7 :]
    stacked = dict(zip(ARRIVAL, blocks))
    stacked = jnp.concatenate([stacked[at][...] for at in sorted(ARRIVAL)], axis=0)
    if fresh:
        for block in range(NB):
            start = block * 2 * COLS
            real = stacked[:, start : start + COLS].astype(F32)
            imag = stacked[:, start + COLS : start + 2 * COLS].astype(F32)
            outs[-1][:, block * COLS : (block + 1) * COLS] = (real * real + imag * imag).astype(BF16)
        power, outs = outs[-1][...], outs[:-1]
    else:
        power, outs = outs[0][...], outs[1:]
    pens = jnp.concatenate([pen[...] for pen in refs[count : 2 * count]], axis=0)
    rows = jnp.concatenate([row[...] for row in refs[:count]], axis=0)
    energy = lax.dot_general(pens, power, NT, preferred_element_type=F32)
    total = lax.dot_general(rows, stacked, NT, preferred_element_type=F32)
    for n, out in enumerate(outs):
        mine = total[n * ROWS : (n + 1) * ROWS].reshape(SHIFTS, P_DEV, 128)
        out[...] = (mine - energy[None, n * P_DEV : (n + 1) * P_DEV]).reshape(ROWS, 128)


def make_scores(rows, pens, blocks, power=None):
    count, fresh = len(rows), power is None
    outs = [((ROWS, 128), F32)] * count + [((128, NB * COLS), BF16)] * fresh
    return local(
        lambda *refs: scores_kernel(count, fresh, *refs), "partial_scores", outs, [],
        [*rows, *pens, *blocks] + ([] if fresh else [power]), 12,
    )


def sum_kernel(*refs):
    refs[-1][...] = refs[0][...] + refs[1][...] + refs[2][...]


def posterior_kernel(*refs):
    out = refs[-1]
    total = refs[0][...]
    for other in refs[1:-1]:
        total = total + other[...]
    total = total.reshape(SHIFTS, P_DEV, 128)
    peak = jnp.max(jnp.max(total, axis=0), axis=1, keepdims=True)
    expo = jnp.exp(total - peak[None])
    norm = jnp.sum(jnp.sum(expo, axis=0), axis=1, keepdims=True)
    share = (expo / norm[None]).reshape(ROWS, 128)
    out[...] = share.T.astype(BF16)


def make_posterior(parts):
    (out,) = local(posterior_kernel, "posterior", [((128, ROWS), BF16)], [], parts, 4)
    return out


def accum_kernel(part, member_ref, x_ref, *refs):
    rows, posts, outs = refs[:G], refs[G : 2 * G], refs[2 * G :]
    along_y = (member_ref[0] & 1) == part
    high = x_ref[0] >> 1

    @pl.loop(0, NB, unroll=True)
    def _(block):
        sums = []
        for half in range(2):
            start = pl.multiple_of(block * 2 * COLS + half * COLS + part * HALF, HALF)
            total = jnp.dot(posts[0][...], rows[0][:, pl.ds(start, HALF)], preferred_element_type=F32)
            for n in range(1, G):
                total = total + jnp.dot(
                    posts[n][...], rows[n][:, pl.ds(start, HALF)], preferred_element_type=F32
                )
            sums.append(total)
        spot = pl.ds(pl.multiple_of(block * HALF, HALF), HALF)
        for n, out in enumerate(outs):
            upper = high ^ (n >> 1) == 1
            for group in range(4):
                at = n * 32 + (group >> 1) * 16
                for_y = sums[group & 1][at : at + 16]
                at = group * 32 + (n & 1) * 16
                for_x = jnp.where(upper, sums[1][at : at + 16], sums[0][at : at + 16])
                out[group * 16 : (group + 1) * 16, spot] = jnp.where(along_y, for_y, for_x).astype(BF16)


def make_accum(part, member, x_at, rows, posts):
    return local(
        lambda *refs: accum_kernel(part, *refs), "weighted_sums", [((64, NB * HALF), BF16)] * 4,
        [member, x_at], [*rows, *posts], 8,
    )


def added(values):
    total = values[0].astype(F32)
    for value in values[1:]:
        total = total + value.astype(F32)
    return total


PIECES = [((16, NB * HALF), F32)] + [((16, NB * HALF), BF16)] * 3


def turn_kernel(part, member_ref, x_ref, *refs):
    along_y = (member_ref[0] & 1) == part
    for n, out in enumerate(refs[4:]):
        group = jnp.where(along_y, (n & 1) * 2 + ((x_ref[0] >> 1) ^ (n >> 1)), n)
        mine = pl.ds(pl.multiple_of(group * 16, 16), 16)
        out[...] = added([ref[mine, :] for ref in refs[:4]]).astype(out.dtype)


def make_turn(part, member, x_at, values):
    return local(
        lambda *refs: turn_kernel(part, *refs), "turned_sums", PIECES, [member, x_at], values, 4
    )


def joined_kernel(block_ref, *refs):
    for n, out in enumerate(refs[8:]):
        spot = pl.ds(pl.multiple_of((block_ref[0] ^ n) * HALF, HALF), HALF)
        out[:, :HALF] = added([ref[:, spot] for ref in refs[:4]]).astype(out.dtype)
        out[:, HALF:] = added([ref[:, spot] for ref in refs[4:8]]).astype(out.dtype)


def after(value, *others):
    return lax.optimization_barrier((value, *others))[0]


def per_device(refs, particles, shift_ids, wedge, defocus, inv_sigma):
    dom = lax.axis_index("dom")
    x_at = (dom // 16) * 2 + lax.axis_index("blk") % 2
    place = [value.astype(jnp.int32).reshape(1) for value in (dom % G, (dom % 16) // G, x_at)]
    member, block, x_at = place
    geo = jnp.asarray(geometry())

    chunks = split_particles(place, particles, shift_ids, wedge, defocus, inv_sigma)
    got, gathered, rows, pens = {}, {}, {}, {}
    got[2] = send(chunks[2], partners(2))
    got[1] = send(chunks[1], partners(1))
    own = own_columns(member, refs, chunks[2])
    gathered[0, 0] = own
    gathered[1, 0] = send(own, flips(y=1))
    gathered[3, 0] = send(own, flips(y=3))
    gathered[0, 1] = send(own, flips(x=1))
    table, geo = make_table(member, geo)
    rows[0], pens[0] = make_rows(member, chunks[0], geo, table)
    rows[1], pens[1] = make_rows(member, after(got[1], rows[0]), geo, table)
    wave = [gathered[1, 0], gathered[3, 0], gathered[0, 1], rows[1]]
    gathered[2, 1] = send(gathered[0, 1], flips(y=2))
    relayed = [gathered[1, 0], after(gathered[3, 0], *wave)]
    (relay,) = local(relay_kernel, "relay", [((16, WIDTH), BF16)], [member], relayed, 2)
    gathered[2, 0] = send(relay, second_hop())
    gathered[1, 1] = send(after(gathered[1, 0], relay), flips(x=1))
    gathered[3, 1] = send(after(gathered[3, 0], relay), flips(x=3))
    got[3] = send(after(chunks[3], got[2], *wave), partners(3))
    rows[2], pens[2] = make_rows(member, after(got[2], *wave), geo, table)
    far = [gathered[2, 1], gathered[2, 0]]
    (gathered[2, 0],) = local(pair_kernel, "pair", [((32, WIDTH), BF16)], [], far, 2)
    blocks = [gathered[at] for at in ARRIVAL]

    second, power = make_scores([rows[2]], [pens[2]], blocks)
    rows[3], pens[3] = make_rows(member, after(got[3], second), geo, table)
    (third,) = make_scores([rows[3]], [after(pens[3], second)], blocks, power)
    mine, other = make_scores([rows[0], rows[1]], [after(pens[0], third), pens[1]], blocks, power)
    near = [mine, send(second, partners(2)), send(third, partners(3))]
    (near,) = local(sum_kernel, "score_sums", [((ROWS, 128), F32)], [], near, 4)
    posterior = make_posterior([near, send(other, partners(1))])
    posts = {n: send(posterior, partners(n)) for n in (3, 2, 1)}
    posts = [posterior] + [posts[n] for n in range(1, G)]
    rows = [rows[n] for n in range(G)]

    first = make_accum(0, member, x_at, rows, posts)
    first = [first[0]] + [send(first[n], crossed(n, 0)) for n in (2, 1, 3)]
    second = make_accum(1, member, x_at, rows, posts)
    second = [second[0]] + [send(second[n], crossed(n, 1)) for n in (2, 1, 3)]
    first = make_turn(0, member, x_at, first)
    first = [first[0]] + [send(first[n], crossed(n, 1)) for n in (2, 1, 3)]
    second = make_turn(1, member, x_at, second)
    second = [second[0]] + [send(second[n], crossed(n, 0)) for n in (2, 1, 3)]
    outs = [((16, COLS), F32)] + [((16, COLS), BF16)] * (NB - 1)
    ends = local(joined_kernel, "joined_sums", outs, [block], [*first, *second], 4)
    return added([ends[0]] + [send(ends[n], flips(z=n * (G // 2))) for n in (2, 1, 3)])


def solution(mesh):
    return jax.shard_map(
        per_device,
        mesh=mesh,
        in_specs=(
            P("blk", None),
            P(("blk", "dom"), None),
            P(("blk", "dom"), None),
            P(("blk", "dom"), None),
            P(("blk", "dom"), None),
            P(("blk", "dom")),
        ),
        out_specs=P("blk", "dom"),
        check_vma=False,
    )
```

```python
import math

import jax
import jax.numpy as jnp
import numpy as np
from jax import lax
from jax.experimental import pallas as pl
from jax.experimental.pallas import tpu as pltpu
from jax.sharding import PartitionSpec as P

BOX = 32
TILTS = 32
SHIFTS = 8
P_DEV = 32
Y, X, Z = 4, 4, 8
COLS = 1024
HALF = 512
G = 4
NB = 16 // G
ROWS = P_DEV * SHIFTS
WIDTH = NB * 2 * COLS
EXTRA = 128
AXES = ("blk", "dom")
F32, BF16 = jnp.float32, jnp.bfloat16
NT = (((1,), (1,)), ((), ()))
MIB = 1 << 20


def linear(y, x, z, core):
    y, x, z = y % Y, x % X, z % Z
    return (y * 2 + x % 2) * 32 + (x // 2) * 16 + z * 2 + core


def flips(y=0, x=0, z=0):
    return [
        (linear(i, j, k, c), linear(i ^ y, j ^ x, k ^ z, c))
        for i in range(Y) for j in range(X) for k in range(Z) for c in range(2)
    ]


def second_hop():
    return [
        (linear(i, j, k, c), linear(i ^ (1 if c else 3), j, k, c))
        for i in range(Y) for j in range(X) for k in range(Z) for c in range(2)
    ]


def partners(k):
    return [
        (linear(y, x, z, c), linear(y, x, z ^ (k >> 1), c ^ (k & 1)))
        for y in range(Y) for x in range(X) for z in range(Z) for c in range(2)
    ]


def send(value, pairs):
    return lax.ppermute(value, AXES, pairs)


def geometry():
    position = np.arange(TILTS * HALF)
    tilt, within = position // HALF, position % HALF
    radial = (within // BOX).astype(np.float64)
    lateral = (within % BOX - BOX // 2).astype(np.float64)
    angle = (tilt - 0.5 * (TILTS - 1)) * (2.0 / TILTS)
    shell = (radial * radial + lateral * lateral) / (0.25 * BOX * BOX)
    zero = np.zeros_like(shell)
    table = np.stack([radial * np.cos(angle), lateral, radial * np.sin(angle), shell] + [zero] * 4)
    return table.reshape(8, 16, COLS).transpose(1, 0, 2).astype(np.float32)


def fold(turns):
    turns = turns - jnp.floor(turns + 0.5)
    far = jnp.abs(turns) > 0.25
    near = jnp.where(far, jnp.where(turns > 0, 0.5, -0.5) - turns, turns)
    return near * (2.0 * math.pi), far


def series(square, terms):
    total = jnp.full_like(square, terms[-1])
    for term in terms[-2::-1]:
        total = total * square + term
    return total


SIN_TERMS = [(-1) ** n / math.factorial(2 * n + 1) for n in range(6)]
COS_TERMS = [(-1) ** n / math.factorial(2 * n) for n in range(7)]


def sine_turns(turns):
    angle, _ = fold(turns)
    return angle * series(angle * angle, SIN_TERMS)


def held(value):
    return pltpu.with_memory_space_constraint(value, pltpu.VMEM)


SCALARS = pl.BlockSpec(memory_space=pltpu.SMEM)
WHOLE = pl.BlockSpec(memory_space=pltpu.VMEM)
PLACED = pl.BlockSpec(memory_space=pl.ANY)


def local(kernel, name, outs, scalars, arrays, limit, placed=0, scratch=()):
    return pl.pallas_call(
        kernel,
        in_specs=[SCALARS] * len(scalars) + [PLACED] * placed + [WHOLE] * (len(arrays) - placed),
        out_specs=[WHOLE] * len(outs),
        out_shape=[pltpu.VMEM(shape, kind) for shape, kind in outs],
        scratch_shapes=list(scratch),
        cost_estimate=pl.CostEstimate(flops=0, bytes_accessed=0, transcendentals=0),
        compiler_params=pltpu.CompilerParams(vmem_limit_bytes=limit * MIB),
        name=name,
    )(
        *scalars,
        *[pltpu.with_memory_space_constraint(value, pltpu.HBM) for value in arrays[:placed]],
        *[held(value) for value in arrays[placed:]],
    )


def table_kernel(member_ref, geo_ref, out_ref, picked_ref, sems):
    copies = [
        pltpu.make_async_copy(geo_ref.at[block * G + member_ref[0]], picked_ref.at[block], sems.at[block])
        for block in range(NB)
    ]
    for copy in copies:
        copy.start()
    ids = lax.broadcasted_iota(jnp.int32, (64, 1), 0).astype(F32)
    high = jnp.floor((ids + 0.5) * (1 / 25))
    middle = jnp.floor((ids - 25 * high + 0.5) * (1 / 5))
    low = ids - 25 * high - 5 * middle
    move_x, move_y, move_z = ((digit - 2.0) * (0.5 / BOX) for digit in (high, middle, low))
    for copy in copies:
        copy.wait()

    @pl.loop(0, NB, unroll=True)
    def _(block):
        geo = picked_ref[block]
        for tilt in range(2):
            part = geo[:, tilt * HALF : (tilt + 1) * HALF]
            turns = move_x * part[0:1] + move_y * part[1:2] + move_z * part[2:3]
            angle, far = fold(turns)
            square = angle * angle
            sine = angle * series(square, SIN_TERMS)
            cosine = series(square, COS_TERMS)
            cosine = jnp.where(far, -cosine, cosine)
            for at, values in enumerate((cosine, sine)):
                high = values.astype(BF16)
                low = (values - high.astype(F32)).astype(BF16)
                spot = pl.ds(pl.multiple_of(block * 2 * COLS + tilt * COLS + at * HALF, HALF), HALF)
                out_ref[0:64, spot] = high
                out_ref[64:128, spot] = -high if at else high
                out_ref[128:192, spot] = low
                out_ref[192:256, spot] = -low if at else low


def make_table(member, geo):
    return local(
        table_kernel, "phase_table", [((256, WIDTH), BF16), ((NB, 8, COLS), F32)], [member], [geo], 8,
        placed=1, scratch=[pltpu.SemaphoreType.DMA((NB,))],
    )


def column(part, block, who):
    return pl.ds(pl.multiple_of((part * 16 + block * G + who) * COLS, COLS), COLS)


def pieces_of(source, out, who, sems, base):
    return [
        pltpu.make_async_copy(
            source.at[:, column(part, block, who)],
            out.at[:, pl.ds((block * 2 + part) * COLS, COLS)],
            sems.at[base + block * 2 + part],
        )
        for block in range(NB) for part in range(2)
    ]


def own_kernel(member_ref, source, after, out, sems):
    copies = pieces_of(source, out, member_ref[0], sems, 0)
    for copy in copies:
        copy.start()
    for copy in copies:
        copy.wait()


def own_columns(member, refs, after):
    (own,) = local(
        own_kernel, "own_references", [((16, WIDTH), BF16)], [member], [refs, after], 4,
        placed=1, scratch=[pltpu.SemaphoreType.DMA((2 * NB,))],
    )
    return own


def relay_kernel(member_ref, one, other, out):
    @pl.when(member_ref[0] & 1 == 0)
    def _():
        out[...] = one[...]

    @pl.when(member_ref[0] & 1 == 1)
    def _():
        out[...] = other[...]


def pair_kernel(one, other, out):
    out[16:32] = one[...]
    out[0:16] = other[...]


def parts_of(values):
    high = values.astype(BF16)
    rest = values - high.astype(F32)
    middle = rest.astype(BF16)
    return high, middle, (rest - middle.astype(F32)).astype(BF16)


def turned_over(values):
    rows, columns = values.shape
    same = lax.broadcasted_iota(jnp.int32, (columns, columns), 0) == lax.broadcasted_iota(
        jnp.int32, (columns, columns), 1
    )
    return sum(
        lax.dot_general(same.astype(BF16), part, NT, preferred_element_type=F32)
        for part in parts_of(values)
    )


def split_kernel(member_ref, block_ref, x_ref, source, ids, wedge, focus, sigma, *refs):
    outs, (ids_in, wedge_in, focus_in, sigma_in, sems, more) = refs[:G], refs[G:]
    copies = []
    for n in (2, 1, 3, 0):
        copies += pieces_of(source, outs[n], member_ref[0] ^ n, sems, n * 2 * NB)
    settings = [
        pltpu.make_async_copy(at, to, more.at[n])
        for n, (at, to) in enumerate(
            ((ids, ids_in), (wedge, wedge_in), (focus, focus_in), (sigma, sigma_in))
        )
    ]
    for copy in copies + settings:
        copy.start()
    for copy in settings:
        copy.wait()
    first = jnp.concatenate(
        [ids_in[...].astype(F32), jnp.broadcast_to(sigma_in[...], (8, P_DEV))], axis=0
    )
    turned = turned_over(first)
    pieces = [turned[:, :SHIFTS], *parts_of(turned[:, SHIFTS : SHIFTS + 1]), jnp.zeros((P_DEV, 5), F32)]
    pieces += [*parts_of(wedge_in[...].astype(F32) * focus_in[...]), jnp.zeros((P_DEV, 16), F32)]
    info = jnp.concatenate([piece.astype(F32) for piece in pieces], axis=1).astype(BF16)
    for out in outs:
        out[:, WIDTH:] = info
    for copy in copies:
        copy.wait()


def split_particles(place, particles, shift_ids, wedge, defocus, inv_sigma):
    return local(
        split_kernel, "split_particles", [((P_DEV, WIDTH + EXTRA), BF16)] * G, place,
        [particles, shift_ids.T, wedge, defocus, inv_sigma[None]], 4, placed=5,
        scratch=[
            pltpu.VMEM((SHIFTS, P_DEV), jnp.int32),
            pltpu.VMEM((P_DEV, TILTS), jnp.int32),
            pltpu.VMEM((P_DEV, TILTS), F32),
            pltpu.VMEM((1, P_DEV), F32),
            pltpu.SemaphoreType.DMA((G * 2 * NB,)),
            pltpu.SemaphoreType.DMA((4,)),
        ],
    )


def rows_kernel(member_ref, x_ref, geo_ref, table_ref, rows_ref, pen_ref):
    info = x_ref[:, WIDTH:].astype(F32)
    lane = lax.broadcasted_iota(jnp.int32, (ROWS, 256), 1) & 127
    ids = jnp.concatenate([info[:, s : s + 1] for s in range(SHIFTS)], axis=0)
    ids = jnp.where(ids > 62.5, 188.0 - ids, ids)
    pick = (ids == lane.astype(F32)).astype(BF16)
    sigma = sum(info[:, SHIFTS + n : SHIFTS + n + 1] for n in range(3))
    small = lax.broadcasted_iota(jnp.int32, (P_DEV, 128), 1)

    @pl.loop(0, NB, unroll=True)
    def _(block):
        first = 2 * (block * G + member_ref[0]) + 16
        start = pl.multiple_of(block * 2 * COLS, 2 * COLS)
        for tilt in range(2):
            at = first + tilt
            mine = (small == at) | (small == at + TILTS) | (small == at + 2 * TILTS)
            focus = jnp.sum(jnp.where(mine, info, 0.0), axis=1, keepdims=True)
            kept = jnp.where(focus > 0.5, 1.0, 0.0)
            shell = geo_ref[block, 3:4, tilt * HALF : (tilt + 1) * HALF]
            transfer = -sine_turns((4.0 * focus * shell + 0.1) * (0.5 / math.pi))
            weight = kept * transfer * sigma
            spot = pl.multiple_of(block * COLS + tilt * HALF, HALF)
            pen_ref[:, pl.ds(spot, HALF)] = (0.5 * weight * transfer).astype(BF16)
            lower, upper = pl.ds(start + tilt * HALF, HALF), pl.ds(start + COLS + tilt * HALF, HALF)
            real = (weight * x_ref[:, lower].astype(F32))[None]
            imag = (weight * x_ref[:, upper].astype(F32))[None]
            real, imag = real[0], imag[0]
            for part in range(0, HALF, 256):
                lanes = slice(part, part + 256)
                at = start + tilt * COLS + part
                cosine = jnp.dot(pick, table_ref[:, pl.ds(at, 256)], preferred_element_type=F32)
                sine = jnp.dot(pick, table_ref[:, pl.ds(at + HALF, 256)], preferred_element_type=F32)
                cosine, sine = cosine.reshape(SHIFTS, P_DEV, 256), sine.reshape(SHIFTS, P_DEV, 256)
                one, two = real[None, :, lanes], imag[None, :, lanes]
                low = pl.ds(start + tilt * HALF + part, 256)
                high = pl.ds(start + COLS + tilt * HALF + part, 256)
                rows_ref[:, low] = (one * cosine + two * sine).reshape(ROWS, 256).astype(BF16)
                rows_ref[:, high] = (two * cosine - one * sine).reshape(ROWS, 256).astype(BF16)


def make_rows(member, x, geo, table):
    return local(
        rows_kernel, "shifted_rows", [((ROWS, WIDTH), BF16), ((P_DEV, NB * COLS), BF16)], [member],
        [x, geo, table], 12,
    )


ARRIVAL = [(2, 0), (1, 1), (3, 1), (0, 1), (1, 0), (3, 0), (0, 0)]


def scores_kernel(count, fresh, *refs):
    blocks = refs[2 * count : 2 * count + 7]
    outs = refs[2 * count + 7 :]
    stacked = dict(zip(ARRIVAL, blocks))
    stacked = jnp.concatenate([stacked[at][...] for at in sorted(ARRIVAL)], axis=0)
    if fresh:
        for block in range(NB):
            start = block * 2 * COLS
            real = stacked[:, start : start + COLS].astype(F32)
            imag = stacked[:, start + COLS : start + 2 * COLS].astype(F32)
            outs[-1][:, block * COLS : (block + 1) * COLS] = (real * real + imag * imag).astype(BF16)
        power, outs = outs[-1][...], outs[:-1]
    else:
        power, outs = outs[0][...], outs[1:]
    pens = jnp.concatenate([pen[...] for pen in refs[count : 2 * count]], axis=0)
    rows = jnp.concatenate([row[...] for row in refs[:count]], axis=0)
    energy = lax.dot_general(pens, power, NT, preferred_element_type=F32)
    total = lax.dot_general(rows, stacked, NT, preferred_element_type=F32)
    for n, out in enumerate(outs):
        mine = total[n * ROWS : (n + 1) * ROWS].reshape(SHIFTS, P_DEV, 128)
        out[...] = (mine - energy[None, n * P_DEV : (n + 1) * P_DEV]).reshape(ROWS, 128)


def make_scores(rows, pens, blocks, power=None):
    count, fresh = len(rows), power is None
    outs = [((ROWS, 128), F32)] * count + [((128, NB * COLS), BF16)] * fresh
    return local(
        lambda *refs: scores_kernel(count, fresh, *refs), "partial_scores", outs, [],
        [*rows, *pens, *blocks] + ([] if fresh else [power]), 12,
    )


def sum_kernel(*refs):
    refs[-1][...] = refs[0][...] + refs[1][...] + refs[2][...]


def posterior_kernel(*refs):
    out = refs[-1]
    total = refs[0][...]
    for other in refs[1:-1]:
        total = total + other[...]
    total = total.reshape(SHIFTS, P_DEV, 128)
    peak = jnp.max(jnp.max(total, axis=0), axis=1, keepdims=True)
    expo = jnp.exp(total - peak[None])
    norm = jnp.sum(jnp.sum(expo, axis=0), axis=1, keepdims=True)
    share = (expo / norm[None]).reshape(ROWS, 128)
    out[...] = share.T.astype(BF16)


def make_posterior(parts):
    (out,) = local(posterior_kernel, "posterior", [((128, ROWS), BF16)], [], parts, 4)
    return out


def accum_kernel(part, member_ref, x_ref, *refs):
    rows, posts, outs = refs[:G], refs[G : 2 * G], refs[2 * G :]
    along_y = part == 0
    high = x_ref[0] >> 1

    @pl.loop(0, NB, unroll=True)
    def _(block):
        sums = []
        for half in range(2):
            start = pl.multiple_of(block * 2 * COLS + half * COLS + part * HALF, HALF)
            total = jnp.dot(posts[0][...], rows[0][:, pl.ds(start, HALF)], preferred_element_type=F32)
            for n in range(1, G):
                total = total + jnp.dot(
                    posts[n][...], rows[n][:, pl.ds(start, HALF)], preferred_element_type=F32
                )
            sums.append(total)
        spot = pl.ds(pl.multiple_of(block * HALF, HALF), HALF)
        for n, out in enumerate(outs):
            upper = high ^ (n >> 1) == 1
            for group in range(4):
                at = n * 32 + (group >> 1) * 16
                for_y = sums[group & 1][at : at + 16]
                at = group * 32 + (n & 1) * 16
                for_x = jnp.where(upper, sums[1][at : at + 16], sums[0][at : at + 16])
                out[group * 16 : (group + 1) * 16, spot] = (for_y if along_y else for_x).astype(BF16)


def make_accum(part, member, x_at, rows, posts):
    return local(
        lambda *refs: accum_kernel(part, *refs), "weighted_sums", [((64, NB * HALF), BF16)] * 4,
        [member, x_at], [*rows, *posts], 8,
    )


def added(values):
    total = values[0].astype(F32)
    for value in values[1:]:
        total = total + value.astype(F32)
    return total


PIECES = [((16, NB * HALF), F32)] + [((16, NB * HALF), BF16)] * 3


def turn_kernel(part, member_ref, x_ref, *refs):
    along_y = part == 0
    for n, out in enumerate(refs[4:]):
        group = (n & 1) * 2 + ((x_ref[0] >> 1) ^ (n >> 1)) if along_y else n
        mine = pl.ds(pl.multiple_of(group * 16, 16), 16)
        out[...] = added([ref[mine, :] for ref in refs[:4]]).astype(out.dtype)


def make_turn(part, member, x_at, values):
    return local(
        lambda *refs: turn_kernel(part, *refs), "turned_sums", PIECES, [member, x_at], values, 4
    )


def joined_kernel(block_ref, *refs):
    for n, out in enumerate(refs[8:]):
        spot = pl.ds(pl.multiple_of((block_ref[0] ^ n) * HALF, HALF), HALF)
        out[:, :HALF] = added([ref[:, spot] for ref in refs[:4]]).astype(out.dtype)
        out[:, HALF:] = added([ref[:, spot] for ref in refs[4:8]]).astype(out.dtype)


def after(value, *others):
    return lax.optimization_barrier((value, *others))[0]


def per_device(refs, particles, shift_ids, wedge, defocus, inv_sigma):
    dom = lax.axis_index("dom")
    x_at = (dom // 16) * 2 + lax.axis_index("blk") % 2
    place = [value.astype(jnp.int32).reshape(1) for value in (dom % G, (dom % 16) // G, x_at)]
    member, block, x_at = place
    geo = jnp.asarray(geometry())

    chunks = split_particles(place, particles, shift_ids, wedge, defocus, inv_sigma)
    got, gathered, rows, pens = {}, {}, {}, {}
    got[2] = send(chunks[2], partners(2))
    got[1] = send(chunks[1], partners(1))
    own = own_columns(member, refs, chunks[2])
    gathered[0, 0] = own
    gathered[1, 0] = send(own, flips(y=1))
    gathered[3, 0] = send(own, flips(y=3))
    gathered[0, 1] = send(own, flips(x=1))
    table, geo = make_table(member, geo)
    rows[0], pens[0] = make_rows(member, chunks[0], geo, table)
    rows[1], pens[1] = make_rows(member, after(got[1], rows[0]), geo, table)
    wave = [gathered[1, 0], gathered[3, 0], gathered[0, 1], rows[1]]
    gathered[2, 1] = send(gathered[0, 1], flips(y=2))
    relayed = [gathered[1, 0], after(gathered[3, 0], *wave)]
    (relay,) = local(relay_kernel, "relay", [((16, WIDTH), BF16)], [member], relayed, 2)
    gathered[2, 0] = send(relay, second_hop())
    gathered[1, 1] = send(after(gathered[1, 0], relay), flips(x=1))
    gathered[3, 1] = send(after(gathered[3, 0], relay), flips(x=3))
    got[3] = send(after(chunks[3], got[2], *wave), partners(3))
    rows[2], pens[2] = make_rows(member, after(got[2], *wave), geo, table)
    far = [gathered[2, 1], gathered[2, 0]]
    (gathered[2, 0],) = local(pair_kernel, "pair", [((32, WIDTH), BF16)], [], far, 2)
    blocks = [gathered[at] for at in ARRIVAL]

    second, power = make_scores([rows[2]], [pens[2]], blocks)
    rows[3], pens[3] = make_rows(member, after(got[3], second), geo, table)
    (third,) = make_scores([rows[3]], [after(pens[3], second)], blocks, power)
    mine, other = make_scores([rows[0], rows[1]], [after(pens[0], third), pens[1]], blocks, power)
    near = [mine, send(second, partners(2)), send(third, partners(3))]
    (near,) = local(sum_kernel, "score_sums", [((ROWS, 128), F32)], [], near, 4)
    posterior = make_posterior([near, send(other, partners(1))])
    posts = {n: send(posterior, partners(n)) for n in (3, 2, 1)}
    posts = [posterior] + [posts[n] for n in range(1, G)]
    rows = [rows[n] for n in range(G)]

    first = make_accum(0, member, x_at, rows, posts)
    first = [first[0]] + [send(first[n], flips(y=n)) for n in (2, 1, 3)]
    second = make_accum(1, member, x_at, rows, posts)
    second = [second[0]] + [send(second[n], flips(x=n)) for n in (2, 1, 3)]
    first = make_turn(0, member, x_at, first)
    first = [first[0]] + [send(first[n], flips(x=n)) for n in (2, 1, 3)]
    second = make_turn(1, member, x_at, second)
    second = [second[0]] + [send(second[n], flips(y=n)) for n in (2, 1, 3)]
    outs = [((16, COLS), F32)] + [((16, COLS), BF16)] * (NB - 1)
    ends = local(joined_kernel, "joined_sums", outs, [block], [*first, *second], 4)
    return added([ends[0]] + [send(ends[n], flips(z=n * (G // 2))) for n in (2, 1, 3)])


def solution(mesh):
    return jax.shard_map(
        per_device,
        mesh=mesh,
        in_specs=(
            P("blk", None),
            P(("blk", "dom"), None),
            P(("blk", "dom"), None),
            P(("blk", "dom"), None),
            P(("blk", "dom"), None),
            P(("blk", "dom")),
        ),
        out_specs=P("blk", "dom"),
        check_vma=False,
    )
```

```python
import math

import jax
import jax.numpy as jnp
import numpy as np
from jax import lax
from jax.experimental import pallas as pl
from jax.experimental.pallas import tpu as pltpu
from jax.sharding import PartitionSpec as P

BOX = 32
TILTS = 32
SHIFTS = 8
P_DEV = 32
Y, X, Z = 4, 4, 8
COLS = 1024
HALF = 512
G = 4
NB = 16 // G
ROWS = P_DEV * SHIFTS
WIDTH = NB * 2 * COLS
EXTRA = 128
AXES = ("blk", "dom")
F32, BF16 = jnp.float32, jnp.bfloat16
NT = (((1,), (1,)), ((), ()))
MIB = 1 << 20


def linear(y, x, z, core):
    y, x, z = y % Y, x % X, z % Z
    return (y * 2 + x % 2) * 32 + (x // 2) * 16 + z * 2 + core


def flips(y=0, x=0, z=0):
    return [
        (linear(i, j, k, c), linear(i ^ y, j ^ x, k ^ z, c))
        for i in range(Y) for j in range(X) for k in range(Z) for c in range(2)
    ]


def crossed(n, core):
    return [
        (linear(i, j, k, c), linear(i ^ (n if c == core else 0), j ^ (0 if c == core else n), k, c))
        for i in range(Y) for j in range(X) for k in range(Z) for c in range(2)
    ]


def second_hop():
    return [
        (linear(i, j, k, c), linear(i ^ (1 if c else 3), j, k, c))
        for i in range(Y) for j in range(X) for k in range(Z) for c in range(2)
    ]


def partners(k):
    return [
        (linear(y, x, z, c), linear(y, x, z ^ (k >> 1), c ^ (k & 1)))
        for y in range(Y) for x in range(X) for z in range(Z) for c in range(2)
    ]


def send(value, pairs):
    return lax.ppermute(value, AXES, pairs)


def geometry():
    position = np.arange(TILTS * HALF)
    tilt, within = position // HALF, position % HALF
    radial = (within // BOX).astype(np.float64)
    lateral = (within % BOX - BOX // 2).astype(np.float64)
    angle = (tilt - 0.5 * (TILTS - 1)) * (2.0 / TILTS)
    shell = (radial * radial + lateral * lateral) / (0.25 * BOX * BOX)
    zero = np.zeros_like(shell)
    table = np.stack([radial * np.cos(angle), lateral, radial * np.sin(angle), shell] + [zero] * 4)
    return table.reshape(8, 16, COLS).transpose(1, 0, 2).astype(np.float32)


def fold(turns):
    turns = turns - jnp.floor(turns + 0.5)
    far = jnp.abs(turns) > 0.25
    near = jnp.where(far, jnp.where(turns > 0, 0.5, -0.5) - turns, turns)
    return near * (2.0 * math.pi), far


def series(square, terms):
    total = jnp.full_like(square, terms[-1])
    for term in terms[-2::-1]:
        total = total * square + term
    return total


SIN_TERMS = [(-1) ** n / math.factorial(2 * n + 1) for n in range(6)]
COS_TERMS = [(-1) ** n / math.factorial(2 * n) for n in range(7)]


def sine_turns(turns):
    angle, _ = fold(turns)
    return angle * series(angle * angle, SIN_TERMS)


def held(value):
    return pltpu.with_memory_space_constraint(value, pltpu.VMEM)


SCALARS = pl.BlockSpec(memory_space=pltpu.SMEM)
WHOLE = pl.BlockSpec(memory_space=pltpu.VMEM)
PLACED = pl.BlockSpec(memory_space=pl.ANY)


def local(kernel, name, outs, scalars, arrays, limit, placed=0, scratch=()):
    return pl.pallas_call(
        kernel,
        in_specs=[SCALARS] * len(scalars) + [PLACED] * placed + [WHOLE] * (len(arrays) - placed),
        out_specs=[WHOLE] * len(outs),
        out_shape=[pltpu.VMEM(shape, kind) for shape, kind in outs],
        scratch_shapes=list(scratch),
        cost_estimate=pl.CostEstimate(flops=0, bytes_accessed=0, transcendentals=0),
        compiler_params=pltpu.CompilerParams(vmem_limit_bytes=limit * MIB),
        name=name,
    )(
        *scalars,
        *[pltpu.with_memory_space_constraint(value, pltpu.HBM) for value in arrays[:placed]],
        *[held(value) for value in arrays[placed:]],
    )


def table_kernel(member_ref, geo_ref, out_ref, picked_ref, sems):
    copies = [
        pltpu.make_async_copy(geo_ref.at[block * G + member_ref[0]], picked_ref.at[block], sems.at[block])
        for block in range(NB)
    ]
    for copy in copies:
        copy.start()
    ids = lax.broadcasted_iota(jnp.int32, (64, 1), 0).astype(F32)
    high = jnp.floor((ids + 0.5) * (1 / 25))
    middle = jnp.floor((ids - 25 * high + 0.5) * (1 / 5))
    low = ids - 25 * high - 5 * middle
    move_x, move_y, move_z = ((digit - 2.0) * (0.5 / BOX) for digit in (high, middle, low))
    for copy in copies:
        copy.wait()

    @pl.loop(0, NB, unroll=True)
    def _(block):
        geo = picked_ref[block]
        for tilt in range(2):
            part = geo[:, tilt * HALF : (tilt + 1) * HALF]
            turns = move_x * part[0:1] + move_y * part[1:2] + move_z * part[2:3]
            angle, far = fold(turns)
            square = angle * angle
            sine = angle * series(square, SIN_TERMS)
            cosine = series(square, COS_TERMS)
            cosine = jnp.where(far, -cosine, cosine)
            for at, values in enumerate((cosine, sine)):
                high = values.astype(BF16)
                low = (values - high.astype(F32)).astype(BF16)
                spot = pl.ds(pl.multiple_of(block * 2 * COLS + tilt * COLS + at * HALF, HALF), HALF)
                out_ref[0:64, spot] = high
                out_ref[64:128, spot] = -high if at else high
                out_ref[128:192, spot] = low
                out_ref[192:256, spot] = -low if at else low


def make_table(member, geo):
    return local(
        table_kernel, "phase_table", [((256, WIDTH), BF16), ((NB, 8, COLS), F32)], [member], [geo], 8,
        placed=1, scratch=[pltpu.SemaphoreType.DMA((NB,))],
    )


def column(part, block, who):
    return pl.ds(pl.multiple_of((part * 16 + block * G + who) * COLS, COLS), COLS)


def pieces_of(source, out, who, sems, base):
    return [
        pltpu.make_async_copy(
            source.at[:, column(part, block, who)],
            out.at[:, pl.ds((block * 2 + part) * COLS, COLS)],
            sems.at[base + block * 2 + part],
        )
        for block in range(NB) for part in range(2)
    ]


def own_kernel(member_ref, source, after, out, sems):
    copies = pieces_of(source, out, member_ref[0], sems, 0)
    for copy in copies:
        copy.start()
    for copy in copies:
        copy.wait()


def own_columns(member, refs, after):
    (own,) = local(
        own_kernel, "own_references", [((16, WIDTH), BF16)], [member], [refs, after], 4,
        placed=1, scratch=[pltpu.SemaphoreType.DMA((2 * NB,))],
    )
    return own


def relay_kernel(member_ref, one, other, out):
    @pl.when(member_ref[0] & 1 == 0)
    def _():
        out[...] = one[...]

    @pl.when(member_ref[0] & 1 == 1)
    def _():
        out[...] = other[...]


def pair_kernel(one, other, out):
    out[16:32] = one[...]
    out[0:16] = other[...]


def parts_of(values):
    high = values.astype(BF16)
    rest = values - high.astype(F32)
    middle = rest.astype(BF16)
    return high, middle, (rest - middle.astype(F32)).astype(BF16)


def turned_over(values):
    rows, columns = values.shape
    same = lax.broadcasted_iota(jnp.int32, (columns, columns), 0) == lax.broadcasted_iota(
        jnp.int32, (columns, columns), 1
    )
    return sum(
        lax.dot_general(same.astype(BF16), part, NT, preferred_element_type=F32)
        for part in parts_of(values)
    )


def split_kernel(member_ref, block_ref, x_ref, source, ids, wedge, focus, sigma, *refs):
    outs, (ids_in, wedge_in, focus_in, sigma_in, sems, more) = refs[:G], refs[G:]
    copies = []
    for n in (2, 1, 3, 0):
        copies += pieces_of(source, outs[n], member_ref[0] ^ n, sems, n * 2 * NB)
    settings = [
        pltpu.make_async_copy(at, to, more.at[n])
        for n, (at, to) in enumerate(
            ((ids, ids_in), (wedge, wedge_in), (focus, focus_in), (sigma, sigma_in))
        )
    ]
    for copy in copies + settings:
        copy.start()
    for copy in settings:
        copy.wait()
    first = jnp.concatenate(
        [ids_in[...].astype(F32), jnp.broadcast_to(sigma_in[...], (8, P_DEV))], axis=0
    )
    turned = turned_over(first)
    pieces = [turned[:, :SHIFTS], *parts_of(turned[:, SHIFTS : SHIFTS + 1]), jnp.zeros((P_DEV, 5), F32)]
    pieces += [*parts_of(wedge_in[...].astype(F32) * focus_in[...]), jnp.zeros((P_DEV, 16), F32)]
    info = jnp.concatenate([piece.astype(F32) for piece in pieces], axis=1).astype(BF16)
    for out in outs:
        out[:, WIDTH:] = info
    for copy in copies:
        copy.wait()


def split_particles(place, particles, shift_ids, wedge, defocus, inv_sigma):
    return local(
        split_kernel, "split_particles", [((P_DEV, WIDTH + EXTRA), BF16)] * G, place,
        [particles, shift_ids.T, wedge, defocus, inv_sigma[None]], 4, placed=5,
        scratch=[
            pltpu.VMEM((SHIFTS, P_DEV), jnp.int32),
            pltpu.VMEM((P_DEV, TILTS), jnp.int32),
            pltpu.VMEM((P_DEV, TILTS), F32),
            pltpu.VMEM((1, P_DEV), F32),
            pltpu.SemaphoreType.DMA((G * 2 * NB,)),
            pltpu.SemaphoreType.DMA((4,)),
        ],
    )


def rows_kernel(member_ref, x_ref, geo_ref, table_ref, rows_ref, pen_ref):
    info = x_ref[:, WIDTH:].astype(F32)
    lane = lax.broadcasted_iota(jnp.int32, (ROWS, 256), 1) & 127
    ids = jnp.concatenate([info[:, s : s + 1] for s in range(SHIFTS)], axis=0)
    ids = jnp.where(ids > 62.5, 188.0 - ids, ids)
    pick = (ids == lane.astype(F32)).astype(BF16)
    sigma = sum(info[:, SHIFTS + n : SHIFTS + n + 1] for n in range(3))
    small = lax.broadcasted_iota(jnp.int32, (P_DEV, 128), 1)

    @pl.loop(0, NB, unroll=True)
    def _(block):
        first = 2 * (block * G + member_ref[0]) + 16
        start = pl.multiple_of(block * 2 * COLS, 2 * COLS)
        for tilt in range(2):
            at = first + tilt
            mine = (small == at) | (small == at + TILTS) | (small == at + 2 * TILTS)
            focus = jnp.sum(jnp.where(mine, info, 0.0), axis=1, keepdims=True)
            kept = jnp.where(focus > 0.5, 1.0, 0.0)
            shell = geo_ref[block, 3:4, tilt * HALF : (tilt + 1) * HALF]
            transfer = -sine_turns((4.0 * focus * shell + 0.1) * (0.5 / math.pi))
            weight = kept * transfer * sigma
            spot = pl.multiple_of(block * COLS + tilt * HALF, HALF)
            pen_ref[:, pl.ds(spot, HALF)] = (0.5 * weight * transfer).astype(BF16)
            lower, upper = pl.ds(start + tilt * HALF, HALF), pl.ds(start + COLS + tilt * HALF, HALF)
            real = (weight * x_ref[:, lower].astype(F32))[None]
            imag = (weight * x_ref[:, upper].astype(F32))[None]
            real, imag = real[0], imag[0]
            for part in range(0, HALF, 256):
                lanes = slice(part, part + 256)
                at = start + tilt * COLS + part
                cosine = jnp.dot(pick, table_ref[:, pl.ds(at, 256)], preferred_element_type=F32)
                sine = jnp.dot(pick, table_ref[:, pl.ds(at + HALF, 256)], preferred_element_type=F32)
                cosine, sine = cosine.reshape(SHIFTS, P_DEV, 256), sine.reshape(SHIFTS, P_DEV, 256)
                one, two = real[None, :, lanes], imag[None, :, lanes]
                low = pl.ds(start + tilt * HALF + part, 256)
                high = pl.ds(start + COLS + tilt * HALF + part, 256)
                rows_ref[:, low] = (one * cosine + two * sine).reshape(ROWS, 256).astype(BF16)
                rows_ref[:, high] = (two * cosine - one * sine).reshape(ROWS, 256).astype(BF16)


def make_rows(member, x, geo, table):
    return local(
        rows_kernel, "shifted_rows", [((ROWS, WIDTH), BF16), ((P_DEV, NB * COLS), BF16)], [member],
        [x, geo, table], 12,
    )


ARRIVAL = [(2, 0), (1, 1), (3, 1), (0, 1), (1, 0), (3, 0), (0, 0)]


def scores_kernel(count, fresh, *refs):
    blocks = refs[2 * count : 2 * count + 7]
    outs = refs[2 * count + 7 :]
    stacked = dict(zip(ARRIVAL, blocks))
    stacked = jnp.concatenate([stacked[at][...] for at in sorted(ARRIVAL)], axis=0)
    if fresh:
        for block in range(NB):
            start = block * 2 * COLS
            real = stacked[:, start : start + COLS].astype(F32)
            imag = stacked[:, start + COLS : start + 2 * COLS].astype(F32)
            outs[-1][:, block * COLS : (block + 1) * COLS] = (real * real + imag * imag).astype(BF16)
        power, outs = outs[-1][...], outs[:-1]
    else:
        power, outs = outs[0][...], outs[1:]
    pens = jnp.concatenate([pen[...] for pen in refs[count : 2 * count]], axis=0)
    rows = jnp.concatenate([row[...] for row in refs[:count]], axis=0)
    energy = lax.dot_general(pens, power, NT, preferred_element_type=F32)
    total = lax.dot_general(rows, stacked, NT, preferred_element_type=F32)
    for n, out in enumerate(outs):
        mine = total[n * ROWS : (n + 1) * ROWS].reshape(SHIFTS, P_DEV, 128)
        out[...] = (mine - energy[None, n * P_DEV : (n + 1) * P_DEV]).reshape(ROWS, 128)


def make_scores(rows, pens, blocks, power=None):
    count, fresh = len(rows), power is None
    outs = [((ROWS, 128), F32)] * count + [((128, NB * COLS), BF16)] * fresh
    return local(
        lambda *refs: scores_kernel(count, fresh, *refs), "partial_scores", outs, [],
        [*rows, *pens, *blocks] + ([] if fresh else [power]), 12,
    )


def sum_kernel(*refs):
    refs[-1][...] = refs[0][...] + refs[1][...] + refs[2][...]


def posterior_kernel(*refs):
    out = refs[-1]
    total = refs[0][...]
    for other in refs[1:-1]:
        total = total + other[...]
    total = total.reshape(SHIFTS, P_DEV, 128)
    peak = jnp.max(jnp.max(total, axis=0), axis=1, keepdims=True)
    expo = jnp.exp(total - peak[None])
    norm = jnp.sum(jnp.sum(expo, axis=0), axis=1, keepdims=True)
    share = (expo / norm[None]).reshape(ROWS, 128)
    out[...] = share.T.astype(BF16)


def make_posterior(parts):
    (out,) = local(posterior_kernel, "posterior", [((128, ROWS), BF16)], [], parts, 4)
    return out


def accum_kernel(part, member_ref, x_ref, *refs):
    rows, posts, outs = refs[:G], refs[G : 2 * G], refs[2 * G :]
    along_y = (member_ref[0] & 1) == part
    high = x_ref[0] >> 1

    @pl.loop(0, NB, unroll=True)
    def _(block):
        sums = []
        for half in range(2):
            start = pl.multiple_of(block * 2 * COLS + half * COLS + part * HALF, HALF)
            total = jnp.dot(posts[0][...], rows[0][:, pl.ds(start, HALF)], preferred_element_type=F32)
            for n in range(1, G):
                total = total + jnp.dot(
                    posts[n][...], rows[n][:, pl.ds(start, HALF)], preferred_element_type=F32
                )
            sums.append(total)
        spot = pl.ds(pl.multiple_of(block * HALF, HALF), HALF)
        for n, out in enumerate(outs):
            upper = high ^ (n >> 1) == 1
            for group in range(4):
                at = n * 32 + (group >> 1) * 16
                for_y = sums[group & 1][at : at + 16]
                at = group * 32 + (n & 1) * 16
                for_x = jnp.where(upper, sums[1][at : at + 16], sums[0][at : at + 16])
                out[group * 16 : (group + 1) * 16, spot] = jnp.where(along_y, for_y, for_x).astype(BF16)


def make_accum(part, member, x_at, rows, posts):
    return local(
        lambda *refs: accum_kernel(part, *refs), "weighted_sums", [((64, NB * HALF), BF16)] * 4,
        [member, x_at], [*rows, *posts], 8,
    )


def added(values):
    total = values[0].astype(F32)
    for value in values[1:]:
        total = total + value.astype(F32)
    return total


PIECES = [((16, NB * HALF), F32)] + [((16, NB * HALF), BF16)] * 3


def turn_kernel(part, member_ref, x_ref, *refs):
    along_y = (member_ref[0] & 1) == part
    for n, out in enumerate(refs[4:]):
        group = jnp.where(along_y, (n & 1) * 2 + ((x_ref[0] >> 1) ^ (n >> 1)), n)
        mine = pl.ds(pl.multiple_of(group * 16, 16), 16)
        out[...] = added([ref[mine, :] for ref in refs[:4]]).astype(out.dtype)


def make_turn(part, member, x_at, values):
    return local(
        lambda *refs: turn_kernel(part, *refs), "turned_sums", PIECES, [member, x_at], values, 4
    )


def joined_kernel(picks, block_ref, *refs):
    for n, out in zip(picks, refs[8:]):
        spot = pl.ds(pl.multiple_of((block_ref[0] ^ n) * HALF, HALF), HALF)
        out[:, :HALF] = added([ref[:, spot] for ref in refs[:4]]).astype(out.dtype)
        out[:, HALF:] = added([ref[:, spot] for ref in refs[4:8]]).astype(out.dtype)


def make_joined(picks, block, values):
    outs = [((16, COLS), BF16 if n else F32) for n in picks]
    return local(lambda *refs: joined_kernel(picks, *refs), "joined_sums", outs, [block], values, 4)


def after(value, *others):
    return lax.optimization_barrier((value, *others))[0]


def per_device(refs, particles, shift_ids, wedge, defocus, inv_sigma):
    dom = lax.axis_index("dom")
    x_at = (dom // 16) * 2 + lax.axis_index("blk") % 2
    place = [value.astype(jnp.int32).reshape(1) for value in (dom % G, (dom % 16) // G, x_at)]
    member, block, x_at = place
    geo = jnp.asarray(geometry())

    chunks = split_particles(place, particles, shift_ids, wedge, defocus, inv_sigma)
    got, gathered, rows, pens = {}, {}, {}, {}
    got[2] = send(chunks[2], partners(2))
    got[1] = send(chunks[1], partners(1))
    own = own_columns(member, refs, chunks[2])
    gathered[0, 0] = own
    gathered[1, 0] = send(own, flips(y=1))
    gathered[3, 0] = send(own, flips(y=3))
    gathered[0, 1] = send(own, flips(x=1))
    table, geo = make_table(member, geo)
    rows[0], pens[0] = make_rows(member, chunks[0], geo, table)
    rows[1], pens[1] = make_rows(member, after(got[1], rows[0]), geo, table)
    wave = [gathered[1, 0], gathered[3, 0], gathered[0, 1], rows[1]]
    gathered[2, 1] = send(gathered[0, 1], flips(y=2))
    relayed = [gathered[1, 0], after(gathered[3, 0], *wave)]
    (relay,) = local(relay_kernel, "relay", [((16, WIDTH), BF16)], [member], relayed, 2)
    gathered[2, 0] = send(relay, second_hop())
    gathered[1, 1] = send(after(gathered[1, 0], relay), flips(x=1))
    gathered[3, 1] = send(after(gathered[3, 0], relay), flips(x=3))
    got[3] = send(after(chunks[3], got[2], *wave), partners(3))
    rows[2], pens[2] = make_rows(member, after(got[2], *wave), geo, table)
    far = [gathered[2, 1], gathered[2, 0]]
    (gathered[2, 0],) = local(pair_kernel, "pair", [((32, WIDTH), BF16)], [], far, 2)
    blocks = [gathered[at] for at in ARRIVAL]

    second, power = make_scores([rows[2]], [pens[2]], blocks)
    rows[3], pens[3] = make_rows(member, after(got[3], second), geo, table)
    (third,) = make_scores([rows[3]], [after(pens[3], second)], blocks, power)
    mine, other = make_scores([rows[0], rows[1]], [after(pens[0], third), pens[1]], blocks, power)
    near = [mine, send(second, partners(2)), send(third, partners(3))]
    (near,) = local(sum_kernel, "score_sums", [((ROWS, 128), F32)], [], near, 4)
    posterior = make_posterior([near, send(other, partners(1))])
    posts = {n: send(posterior, partners(n)) for n in (3, 2, 1)}
    posts = [posterior] + [posts[n] for n in range(1, G)]
    rows = [rows[n] for n in range(G)]

    first = make_accum(0, member, x_at, rows, posts)
    first = [first[0]] + [send(first[n], crossed(n, 0)) for n in (2, 1, 3)]
    second = make_accum(1, member, x_at, rows, posts)
    second = [second[0]] + [send(second[n], crossed(n, 1)) for n in (2, 1, 3)]
    first = make_turn(0, member, x_at, first)
    first = [first[0]] + [send(first[n], crossed(n, 1)) for n in (2, 1, 3)]
    second = make_turn(1, member, x_at, second)
    second = [second[0]] + [send(second[n], crossed(n, 0)) for n in (2, 1, 3)]
    values = [*first, *second]
    (far,) = make_joined([2], block, values)
    values[0] = after(values[0], far)
    far = send(far, flips(z=2 * (G // 2)))
    mine, one, three = make_joined([0, 1, 3], block, values)
    near = [send(one, flips(z=G // 2)), send(three, flips(z=3 * (G // 2)))]
    return added([mine, far, *near])


def solution(mesh):
    return jax.shard_map(
        per_device,
        mesh=mesh,
        in_specs=(
            P("blk", None),
            P(("blk", "dom"), None),
            P(("blk", "dom"), None),
            P(("blk", "dom"), None),
            P(("blk", "dom"), None),
            P(("blk", "dom")),
        ),
        out_specs=P("blk", "dom"),
        check_vma=False,
    )
```
